256 devices in a mesh: dp: 32 (over y_lo, z, core), ctx: 8 (over x, y_hi).
Axes of the slice: x: 4, y: 4 (y_hi: 2, y_lo: 2; y = y_hi * 2 + y_lo), z: 8, core: 2. Of those that a mesh axis runs over, the one named last changes fastest.
Arguments:
- history: bfloat16 [32, 1024, 1024], P('dp', 'ctx'), may hold values from -6 to 6
- cotangent: bfloat16 [32, 1024, 1024], P('dp', 'ctx'), may hold values from -6 to 6
- lengths: int32 [32, 3], P('dp'), may hold values from 1 to 819, as said below
- w_proj: bfloat16 [1024, 2048], replicated, may hold values from -0.1875 to 0.1875
- w_out: bfloat16 [512, 1024], replicated, may hold values from -0.25 to 0.25
Outputs:
- d_history: bfloat16 [32, 1024, 1024], P('dp', 'ctx')
- grad_proj: bfloat16 [1024, 2048], replicated
- grad_out: bfloat16 [512, 1024], replicated
The draws below stay inside these ranges and needn't reach their ends.
Inputs may be any that keep to these rules, and one draw needn't show every extreme that they name: Each batch's lengths sum to 1024; the first history of each batch is its longest, with exactly 819 events.
All inputs are finite; a program needn't handle non-finite values.
Results may differ from the reference program's by a relative error of at most 0.0092.
Values may be sent and summed in bfloat16 or wider, within the bound.
A program may use at most 128 MiB of HBM per device.

```python
import jax
import jax.numpy as jnp
from jax import lax

D = 1024
HEAD_DIM = 128
INNER = 512
SEQS = 3
GROUP = 1024
BATCHES = 32


def draw_lengths(key, part):
    key = jax.random.fold_in(key, 7)
    longest = GROUP * 4 // 5
    extra = GROUP - longest - (SEQS - 1)
    cuts = jnp.sort(jax.random.randint(key, (BATCHES, SEQS - 2), 0, extra + 1), axis=1)
    low = jnp.zeros((BATCHES, 1), jnp.int32)
    high = jnp.full((BATCHES, 1), extra, jnp.int32)
    bounds = jnp.concatenate([low, cuts.astype(jnp.int32), high], axis=1)
    others = bounds[:, 1:] - bounds[:, :-1] + 1
    first = jnp.full((BATCHES, 1), longest, jnp.int32)
    return jnp.concatenate([first, others], axis=1).astype(jnp.int32)


def block_levels(rng, shape, pieces, low, top_value):
    def one(position, parts):
        heights = jax.random.uniform(jax.random.fold_in(jax.random.fold_in(rng, 6), position), (parts,), jnp.float32, low / len(pieces), top_value / len(pieces))
        return jnp.repeat(jnp.exp(heights), shape[position] // parts).reshape((-1,) + (1,) * (len(shape) - position - 1))

    gain = one(*pieces[0])
    for cut in pieces[1:]:
        gain = gain * one(*cut)
    return gain


def bell_draw(stream_key, shape, deviation, most, cuts=(), kind=jnp.bfloat16):
    level = block_levels(stream_key, shape, cuts, -0.22, 0.18) if cuts else 1.0
    result = jax.random.normal(stream_key, shape, jnp.float32) * deviation * level
    return jnp.minimum(jnp.maximum(result, -most), most).astype(kind)


def setup_inputs(seed: int = 0) -> dict:
    key_of = jax.random.split(jax.random.key(seed), 6)
    history = bell_draw(key_of[0], (BATCHES, GROUP, D), 1.0, 6.0, ((0, 32), (1, 8)))
    cotangent = bell_draw(key_of[1], (BATCHES, GROUP, D), 1.0, 6.0, ((0, 32), (1, 8)))
    lengths = draw_lengths(jax.random.fold_in(key_of[5], 71), 0)
    w_proj = bell_draw(key_of[3], (D, 4 * INNER), D ** -0.5, 0.1875)
    w_out = bell_draw(key_of[4], (INNER, D), INNER ** -0.5, 0.25)
    return {"history": history, "cotangent": cotangent, "lengths": lengths, "w_proj": w_proj, "w_out": w_out}


EPSILON = 1e-05

def silu_grad(values):
    sigmoid = jax.nn.sigmoid(values)
    return sigmoid * (1.0 + values * (1.0 - sigmoid))

def normalize(values):
    average = lax.optimization_barrier(jnp.mean(values, axis=-1, keepdims=True))
    centred = values - average
    variance = lax.optimization_barrier(jnp.mean(centred * centred, axis=-1, keepdims=True))
    inv_scale = lax.rsqrt(variance + EPSILON)
    return (centred * inv_scale, inv_scale)

def norm_back(grad, normed, inv_scale):
    first = lax.optimization_barrier(jnp.mean(grad, axis=-1, keepdims=True))
    second = lax.optimization_barrier(jnp.mean(grad * normed, axis=-1, keepdims=True))
    return inv_scale * (grad - first - normed * second)

def segment_of(positions, history_ends):
    return lax.optimization_barrier(jnp.sum((positions[:, None] >= history_ends[None, :]).astype(jnp.int32), axis=1))

def reference(history, cotangent, lengths, w_proj, w_out):
    inner_width = w_out.shape[0]
    head_count = inner_width // HEAD_DIM
    score_scale = HEAD_DIM ** (-0.5)
    proj_f = w_proj.astype(jnp.float32)
    out_f = w_out.astype(jnp.float32)

    def one_group(grads, inputs):
        tokens_in, cot_rows, lens = inputs
        row_count = tokens_in.shape[0]
        positions = jnp.arange(row_count, dtype=jnp.int32)
        segment = segment_of(positions, jnp.cumsum(lens).astype(jnp.int32))
        allowed = (segment[:, None] == segment[None, :]) & (positions[None, :] >= positions[:, None])
        x_norm, x_scale = normalize(tokens_in.astype(jnp.float32))
        normed = x_norm.astype(jnp.bfloat16)
        pre = jnp.dot(normed, w_proj, preferred_element_type=jnp.float32)
        proj = jax.nn.silu(pre).astype(jnp.bfloat16)
        gate_u = proj[:, :inner_width].astype(jnp.float32)
        value = proj[:, inner_width:2 * inner_width].astype(jnp.float32).reshape(row_count, head_count, HEAD_DIM)
        query = proj[:, 2 * inner_width:3 * inner_width].astype(jnp.float32).reshape(row_count, head_count, HEAD_DIM)
        keys = proj[:, 3 * inner_width:].astype(jnp.float32).reshape(row_count, head_count, HEAD_DIM)
        logits = jnp.einsum('qhd,khd->hqk', query, keys) * score_scale
        weights = jnp.where(allowed[None], jax.nn.silu(logits), 0.0).astype(jnp.bfloat16)
        attn = jnp.einsum('hqk,khd->qhd', weights.astype(jnp.float32), value).reshape(row_count, inner_width)
        a_norm, a_scale = normalize(attn)
        gated = (a_norm * gate_u).astype(jnp.bfloat16)
        grad_o = jnp.dot(gated.T, cot_rows, preferred_element_type=jnp.float32)
        d_gated = jnp.dot(cot_rows.astype(jnp.float32), out_f.T)
        d_u = d_gated * a_norm
        d_attn = norm_back(d_gated * gate_u, a_norm, a_scale).astype(jnp.bfloat16)
        d_heads = d_attn.astype(jnp.float32).reshape(row_count, head_count, HEAD_DIM)
        d_weights = jnp.einsum('qhd,khd->hqk', d_heads, value)
        d_logits = jnp.where(allowed[None], d_weights * silu_grad(logits), 0.0).astype(jnp.bfloat16).astype(jnp.float32)
        d_query = jnp.einsum('hqk,khd->qhd', d_logits, keys) * score_scale
        d_keys = jnp.einsum('hqk,qhd->khd', d_logits, query) * score_scale
        d_value = jnp.einsum('hqk,qhd->khd', weights.astype(jnp.float32), d_heads)
        d_proj = jnp.concatenate([d_u, d_value.reshape(row_count, inner_width), d_query.reshape(row_count, inner_width), d_keys.reshape(row_count, inner_width)], axis=1)
        d_pre = (d_proj * silu_grad(pre)).astype(jnp.bfloat16)
        grad_p = jnp.dot(normed.T, d_pre, preferred_element_type=jnp.float32)
        d_normed = jnp.dot(d_pre.astype(jnp.float32), proj_f.T)
        d_rows = (cot_rows.astype(jnp.float32) + norm_back(d_normed, x_norm, x_scale)).astype(jnp.bfloat16)
        return ((grads[0] + grad_p, grads[1] + grad_o), d_rows)
    start = (jnp.zeros(w_proj.shape, jnp.float32), jnp.zeros(w_out.shape, jnp.float32))
    grads, d_history = lax.scan(one_group, start, (history, cotangent, lengths))
    return (d_history, grads[0].astype(jnp.bfloat16), grads[1].astype(jnp.bfloat16))
```

```python
import jax
import jax.numpy as jnp
from jax import lax
from jax.experimental import pallas as pl
from jax.experimental.pallas import tpu as pltpu
from jax.sharding import PartitionSpec as P

F32, BF16 = jnp.float32, jnp.bfloat16
MESH = pl.DeviceIdType.MESH
EPSILON = 1e-05
D = 1024
EVENTS = 1024
HD = 128
ROWS = 128
PAIR = 256
SCALE = HD ** (-0.5)
NT = (((1,), (1,)), ((), ()))


def dot(a, b):
    return jnp.dot(a, b, preferred_element_type=F32)


def dot_nt(a, b):
    return lax.dot_general(a, b, NT, preferred_element_type=F32)


def sigmoid(z):
    return 0.5 * jnp.tanh(0.5 * z) + 0.5


def device(x, yh, yl, z, c):
    return ((yl * 8 + z) * 2 + c, x * 2 + yh)


def remote(src, dst, send, recv, target):
    return pltpu.make_async_remote_copy(
        src_ref=src,
        dst_ref=dst,
        send_sem=send,
        recv_sem=recv,
        device_id=target,
        device_id_type=MESH,
    )


def kernel(
    hist, cot, lens, w_proj, w_out, d_hist, gs,
    xg, cg, xn, wp, wht, wo, lown, lsib, projt, spt, kr, vr, wm, sm, attnt, dgt, st, stx,
    gt, dat, dkt, dvt, dpt, dpr, pay, ybuf, zsend, zbuf, dn,
    wsem, osem, lsem, swsem, xsem, xrsem, fsem, frsem, csem, crsem, gsem, grsem, stsem, strsem,
    asem, arsem, asem0, ysem, yrsem, zsem, zrsem, g1s, g1r, g2s, g2r, g3s, g3r, g4s, g4r,
):
    dp, ctx = lax.axis_index("dp"), lax.axis_index("ctx")
    c, z, yl = lax.rem(dp, 2), lax.rem(dp // 2, 8), dp // 16
    x, yh = ctx // 2, lax.rem(ctx, 2)
    y = yh * 2 + yl
    sib = device(x, yh, yl, z, 1 - c)

    def x_mate(d):
        return device(lax.rem(x + d, 4), yh, yl, z, c)

    def y_mate(d):
        other = lax.rem(y + d, 4)
        return device(x, other // 2, lax.rem(other, 2), z, c)

    def z_mate(d):
        return device(x, yh, yl, lax.rem(z + d, 8), c)

    def x_from(d):
        return lax.rem(x + 4 - d, 4)

    def y_from(d):
        return lax.rem(y + 4 - d, 4)

    def z_from(d):
        return lax.rem(z + 8 - d, 8)

    get_w = pltpu.make_async_copy(w_proj, wp, wsem)
    get_w.start()
    get_o = pltpu.make_async_copy(w_out.at[pl.ds(pl.multiple_of(x * HD, HD), HD), :], wo, osem)
    get_o.start()

    barrier = pltpu.get_barrier_semaphore()
    group = [(i // 4, (i // 2) % 2, i % 2) for i in range(1, 16)]
    mates = [device(lax.rem(x + a, 4), lax.rem(yh + b, 2), yl, z, lax.rem(c + e, 2)) for a, b, e in group]
    mates += [z_mate(d) for d in range(1, 8)] + [y_mate(1), y_mate(3)]
    for mate in mates:
        pl.semaphore_signal(barrier, inc=1, device_id=mate, device_id_type=MESH)

    lane = lax.broadcasted_iota(jnp.int32, (8, 128), 1)
    first = jnp.broadcast_to(lens[0:1, 0:1], (8, 128))
    second = first + jnp.broadcast_to(lens[0:1, 1:2], (8, 128))
    lown[...] = jnp.where(lane == 0, first, jnp.where(lane == 1, second, 0))

    pl.semaphore_wait(barrier, len(mates))

    slot = pl.ds(pl.multiple_of((2 * x + c) * ROWS, ROWS), ROWS)
    over = pl.ds(pl.multiple_of((2 * x + 1 - c) * ROWS, ROWS), ROWS)
    here = c == yh
    swap = device(x, 1 - yh, yl, z, 1 - c)
    swap_x = remote(hist, xg.at[over, :], swsem.at[0], swsem.at[1], swap)
    swap_c = remote(cot, cg.at[over, :], swsem.at[2], swsem.at[3], swap)
    send_l = remote(lown, lsib, lsem.at[0], lsem.at[1], sib)
    send_l.start()

    @pl.when(here)
    def _():
        xg[slot, :] = hist[...]
        cg[slot, :] = cot[...]

    @pl.when(jnp.logical_not(here))
    def _():
        swap_x.start()
        swap_c.start()
        swap_x.wait_recv()

    def block_of(d, core):
        return pl.ds(pl.multiple_of((2 * x_from(d) + core) * ROWS, ROWS), ROWS)

    push_x = [remote(xg.at[slot, :], xg.at[slot, :], xsem.at[d], xrsem.at[d], x_mate(d)) for d in range(1, 4)]
    push_c = [remote(cg.at[slot, :], cg.at[slot, :], csem.at[d], crsem.at[d], x_mate(d)) for d in range(1, 4)]
    pass_x = [remote(xg.at[block_of(d, c), :], xg.at[block_of(d, c), :], fsem.at[d], frsem.at[d], sib) for d in range(4)]
    pass_c = [remote(cg.at[block_of(d, c), :], cg.at[block_of(d, c), :], gsem.at[d], grsem.at[d], sib) for d in range(4)]
    for copy in push_x:
        copy.start()
    pass_x[0].start()

    get_w.wait()
    for j in range(4):
        columns = pl.ds(pl.multiple_of(j * 512 + x * HD, HD), HD)
        wht[j * HD : (j + 1) * HD, :] = wp[:, columns].T

    def project(d):
        base = x_from(d) * PAIR

        @pl.loop(0, PAIR // 32)
        def _(i):
            rows = pl.ds(pl.multiple_of(base + i * 32, 32), 32)
            values = xg[rows, :].astype(F32)
            centred = values - jnp.mean(values, axis=-1, keepdims=True)
            variance = jnp.mean(centred * centred, axis=-1, keepdims=True)
            xn[rows, :] = (centred * lax.rsqrt(variance + EPSILON)).astype(BF16)

        rows = pl.ds(pl.multiple_of(base, PAIR), PAIR)
        normed = xn[rows, :]
        for j in range(4):
            pre = dot_nt(wht[j * HD : (j + 1) * HD, :], normed)
            s = sigmoid(pre)
            value = pre * s
            spt[j * HD : (j + 1) * HD, rows] = s + value * (1.0 - s)
            value = value.astype(BF16)
            projt[j * HD : (j + 1) * HD, rows] = value
            if j == 1:
                vr[rows, :] = value.T
            if j == 3:
                kr[rows, :] = value.T

    for d in (0, 1, 3, 2):
        if d:
            push_x[d - 1].wait_recv()
            pass_x[d].start()
        if d == 2:
            @pl.when(jnp.logical_not(here))
            def _():
                swap_c.wait_recv()

            for copy in push_c:
                copy.start()
            pass_c[0].start()
        pass_x[d].wait_recv()
        project(d)

    send_l.wait_recv()
    ends = jnp.where(here, lown[...], lsib[...])
    first, second = ends[0:1, 0:1], ends[0:1, 1:2]

    for pb in range(4):
        cols = slice(pb * PAIR, (pb + 1) * PAIR)
        q = projt[2 * HD : 3 * HD, cols]
        p_at = lax.broadcasted_iota(jnp.int32, (1, PAIR), 1) + pb * PAIR
        p_end = jnp.where(p_at < first, first, jnp.where(p_at < second, second, EVENTS))
        total = None
        for rb in range(pb, 4):
            rows = slice(rb * PAIR, (rb + 1) * PAIR)
            logits = dot(kr[rows, :], q) * SCALE
            s = sigmoid(logits)
            weight = logits * s
            slope = s + weight * (1.0 - s)
            r_at = lax.broadcasted_iota(jnp.int32, (PAIR, PAIR), 0) + rb * PAIR
            allowed = (r_at >= p_at) & (r_at < p_end)
            weight = jnp.where(allowed, weight, 0.0).astype(BF16)
            wm[rows, cols] = weight
            sm[rows, cols] = jnp.where(allowed, slope, 0.0)
            term = dot(projt[HD : 2 * HD, rows], weight)
            total = term if total is None else total + term
        attnt[:, cols] = total

    for d in (1, 3, 2):
        push_c[d - 1].wait_recv()
        pass_c[d].start()
    for d in range(4):
        pass_c[d].wait_recv()
    get_o.wait()

    st[4:8, :] = jnp.zeros((4, EVENTS), F32)
    for pb in range(4):
        cols = slice(pb * PAIR, (pb + 1) * PAIR)
        d_gated = dot_nt(wo[...], cg[cols, :])
        dgt[:, cols] = d_gated
        attn = attnt[:, cols]
        g = d_gated * projt[0:HD, cols].astype(F32)
        average = jnp.mean(attn, axis=0, keepdims=True)
        centred = attn - average
        st[0:1, cols] = average
        st[1:2, cols] = jnp.sum(centred * centred, axis=0, keepdims=True)
        st[2:3, cols] = jnp.sum(g, axis=0, keepdims=True)
        st[3:4, cols] = jnp.sum(g * centred, axis=0, keepdims=True)

    push_s = [remote(st, stx.at[d], stsem.at[d], strsem.at[d], x_mate(d)) for d in range(1, 4)]
    for copy in push_s:
        copy.start()
    for copy in push_s:
        copy.wait_recv()
    parts = [st[...]] + [stx[d] for d in range(1, 4)]
    average = (parts[0][0:1] + parts[1][0:1] + parts[2][0:1] + parts[3][0:1]) * 0.25
    spread = sum(p[1:2] + HD * (p[0:1] - average) ** 2 for p in parts) * (1.0 / 512)
    a_scale = lax.rsqrt(spread + EPSILON)
    g_mean = sum(p[2:3] for p in parts) * (1.0 / 512)
    ga_mean = a_scale * (sum(p[3:4] + (p[0:1] - average) * p[2:3] for p in parts) * (1.0 / 512))

    for pb in range(4):
        cols = slice(pb * PAIR, (pb + 1) * PAIR)
        u = projt[0:HD, cols].astype(F32)
        d_gated = dgt[:, cols]
        scale = a_scale[:, cols]
        a_norm = (attnt[:, cols] - average[:, cols]) * scale
        gt[:, cols] = (a_norm * u).astype(BF16)
        dpt[0, :, cols] = (d_gated * a_norm * spt[0:HD, cols]).astype(BF16)
        dat[:, cols] = (scale * (d_gated * u - g_mean[:, cols] - a_norm * ga_mean[:, cols])).astype(BF16)

    for pb in range(4):
        cols = slice(pb * PAIR, (pb + 1) * PAIR)
        q = projt[2 * HD : 3 * HD, cols]
        da = dat[:, cols]
        total = None
        for rb in range(pb, 4):
            rows = slice(rb * PAIR, (rb + 1) * PAIR)
            d_logits = (dot(vr[rows, :], da) * sm[rows, cols]).astype(BF16)
            term = dot(projt[3 * HD : 4 * HD, rows], d_logits)
            total = term if total is None else total + term
            d_key = dot_nt(q, d_logits)
            d_value = dot_nt(da, wm[rows, cols])
            if pb == 0:
                dkt[:, rows] = d_key
                dvt[:, rows] = d_value
            else:
                dkt[:, rows] += d_key
                dvt[:, rows] += d_value
        dpt[2, :, cols] = (total * SCALE * spt[2 * HD : 3 * HD, cols]).astype(BF16)
    dpt[1] = (dvt[...] * spt[HD : 2 * HD, :]).astype(BF16)
    dpt[3] = (dkt[...] * SCALE * spt[3 * HD : 4 * HD, :]).astype(BF16)

    mine = pl.ds(2 * c, 2)
    backs = []
    for dx in range(4):
        for dy in range(2):
            tx, ty = lax.rem(x + dx, 4), lax.rem(yh + dy, 2)
            lanes = pl.ds(pl.multiple_of((tx * 2 + ty) * ROWS, ROWS), ROWS)
            copy = remote(
                dpt.at[mine, :, lanes], dpr.at[mine, x], asem.at[dx * 2 + dy], arsem.at[dx * 2 + c], device(tx, ty, yl, z, yh)
            )
            if dx == 0 and dy == 0:
                @pl.when(jnp.logical_not(here))
                def _(copy=copy):
                    copy.start()

                @pl.when(here)
                def _(lanes=lanes):
                    pltpu.make_async_copy(dpt.at[mine, :, lanes], dpr.at[mine, x], asem0).start()
            else:
                copy.start()
            backs.append(copy)

    half = pl.ds(pl.multiple_of(c * 512, 512), 512)
    grad_o = dot(gt[...], cg[:, half]).astype(BF16)
    for j in range(4):
        pay[j, 512:640, :] = grad_o[:, j * HD : (j + 1) * HD]
    push_y = []
    for d in (1, 3, 2, 0):
        j = lax.rem(y + d, 4)
        pay[j, 0:512, :] = dot(dpt[j], xn[:, half]).T.astype(BF16)
        if d:
            copy = remote(pay.at[j], ybuf.at[d], ysem.at[d], yrsem.at[d], y_mate(d))
            copy.start()
            push_y.append(copy)
    for copy in push_y:
        copy.wait_recv()
    zsend[...] = (
        pay[y].astype(F32) + ybuf[1].astype(F32) + ybuf[2].astype(F32) + ybuf[3].astype(F32)
    ).astype(BF16)
    push_z = []
    for d in (1, 7, 2, 6, 3, 5, 4):
        rows = pl.ds(pl.multiple_of(lax.rem(z + d, 8) * 80, 16), 80)
        copy = remote(zsend.at[rows, :], zbuf.at[d], zsem.at[d], zrsem.at[d], z_mate(d))
        copy.start()
        push_z.append(copy)
    for copy in push_z:
        copy.wait_recv()
    total = zsend[pl.ds(pl.multiple_of(z * 80, 16), 80), :].astype(F32)
    for d in range(1, 8):
        total = total + zbuf[d].astype(F32)
    gs[c, x, y, z] = total.astype(BF16)

    stage1 = []
    for d in range(1, 8):
        ref = gs.at[c, x, y, z, 0:64]
        stage1.append(remote(ref, ref, g1s.at[d], g1r.at[d], z_mate(d)))
    for d in range(1, 4):
        ref = gs.at[c, x, y, z, 64:80]
        stage1.append(remote(ref, ref, g1s.at[7 + d], g1r.at[7 + d], y_mate(d)))
    for copy in stage1:
        copy.start()

    for dx in range(4):
        for core in range(2):
            arrived = remote(
                dpr.at[pl.ds(2 * core, 2), x_from(dx)], dpr.at[pl.ds(2 * core, 2), x_from(dx)], asem.at[0], arsem.at[dx * 2 + core], sib
            )
            if dx == 0:
                local = here & (c == core)

                @pl.when(jnp.logical_not(local))
                def _(arrived=arrived):
                    arrived.wait_recv()

                @pl.when(local)
                def _(core=core):
                    ref = dpr.at[pl.ds(2 * core, 2), x]
                    pltpu.make_async_copy(ref, ref, asem0).wait()
            else:
                arrived.wait_recv()

    for copy in stage1:
        copy.wait_recv()
    stage2 = []
    for d in range(1, 4):
        ref = gs.at[c, x, y, :, 0:32]
        stage2.append(remote(ref, ref, g2s.at[d], g2r.at[d], y_mate(d)))
    for d in range(1, 4):
        ref = gs.at[c, x, y, :, 32:64]
        stage2.append(remote(ref, ref, g2s.at[3 + d], g2r.at[3 + d], x_mate(d)))
    for d in range(1, 4):
        ref = gs.at[c, x, :, z, 64:80]
        stage2.append(remote(ref, ref, g2s.at[6 + d], g2r.at[6 + d], x_mate(d)))
    for copy in stage2:
        copy.start()

    columns = dpr[...].reshape(2048, ROWS)
    for i in range(4):
        part = dot(wp[i * 256 : (i + 1) * 256, :], columns)
        dn[:, i * 256 : (i + 1) * 256] = part.T

    for copy in stage2:
        copy.wait_recv()
    stage3, stage4 = [], []

    def to_sibling(i, ref):
        copy = remote(ref, ref, g4s.at[i], g4r.at[i], sib)
        copy.start()
        stage4.append(copy)

    for d in range(1, 4):
        ref = gs.at[c, x, :, :, 0:32]
        stage3.append((remote(ref, ref, g3s.at[d], g3r.at[d], x_mate(d)), gs.at[c, x_from(d), :, :, 0:32]))
        ref = gs.at[c, :, y, :, 32:64]
        stage3.append((remote(ref, ref, g3s.at[3 + d], g3r.at[3 + d], y_mate(d)), gs.at[c, :, y_from(d), :, 32:64]))
    for d in (1, 7, 2, 6, 3, 5, 4):
        ref = gs.at[c, :, :, z, 64:80]
        stage3.append((remote(ref, ref, g3s.at[6 + d], g3r.at[6 + d], z_mate(d)), gs.at[c, :, :, z_from(d), 64:80]))
    for copy, _ in stage3:
        copy.start()
    to_sibling(0, gs.at[c, x, :, :, 0:32])
    to_sibling(1, gs.at[c, :, y, :, 32:64])
    to_sibling(2, gs.at[c, :, :, z, 64:80])

    @pl.loop(0, ROWS // 32)
    def _(i):
        rows = pl.ds(pl.multiple_of(i * 32, 32), 32)
        values = hist[rows, :].astype(F32)
        centred = values - jnp.mean(values, axis=-1, keepdims=True)
        variance = jnp.mean(centred * centred, axis=-1, keepdims=True)
        scale = lax.rsqrt(variance + EPSILON)
        normed = centred * scale
        grad = dn[rows, :]
        one = jnp.mean(grad, axis=-1, keepdims=True)
        two = jnp.mean(grad * normed, axis=-1, keepdims=True)
        d_hist[rows, :] = (cot[rows, :].astype(F32) + scale * (grad - one - normed * two)).astype(BF16)

    for i, (copy, ref) in enumerate(stage3):
        copy.wait_recv()
        to_sibling(3 + i, ref)
    for copy in stage4:
        copy.wait_recv()

    send_l.wait_send()

    @pl.when(jnp.logical_not(here))
    def _():
        swap_x.wait_send()
        swap_c.wait_send()
        backs[0].wait_send()

    sent = push_x + push_c + pass_x + pass_c + push_s + backs[1:] + push_y + push_z + stage1 + stage2
    for copy in sent + [copy for copy, _ in stage3] + stage4:
        copy.wait_send()


def on_device(history, cotangent, lengths, w_proj, w_out):
    vmem, dma = pltpu.VMEM, pltpu.SemaphoreType.DMA
    whole = pl.BlockSpec(memory_space=vmem)
    anywhere = pl.BlockSpec(memory_space=pl.ANY)
    scratch = [
        vmem((EVENTS, D), BF16),
        vmem((EVENTS, D), BF16),
        vmem((EVENTS, D), BF16),
        vmem((D, 2048), BF16),
        vmem((512, D), BF16),
        vmem((HD, D), BF16),
        vmem((8, 128), jnp.int32),
        vmem((8, 128), jnp.int32),
        vmem((512, EVENTS), BF16),
        vmem((512, EVENTS), F32),
        vmem((EVENTS, HD), BF16),
        vmem((EVENTS, HD), BF16),
        vmem((EVENTS, EVENTS), BF16),
        vmem((EVENTS, EVENTS), F32),
        vmem((HD, EVENTS), F32),
        vmem((HD, EVENTS), F32),
        vmem((8, EVENTS), F32),
        vmem((4, 8, EVENTS), F32),
        vmem((HD, EVENTS), BF16),
        vmem((HD, EVENTS), BF16),
        vmem((HD, EVENTS), F32),
        vmem((HD, EVENTS), F32),
        vmem((4, HD, EVENTS), BF16),
        vmem((4, 4, HD, ROWS), BF16),
        vmem((4, 640, HD), BF16),
        vmem((4, 640, HD), BF16),
        vmem((640, HD), BF16),
        vmem((8, 80, HD), BF16),
        vmem((ROWS, D), F32),
        dma, dma, dma((2,)), dma((4,)),
        dma((4,)), dma((4,)), dma((4,)), dma((4,)), dma((4,)), dma((4,)), dma((4,)), dma((4,)), dma((4,)), dma((4,)),
        dma((8,)), dma((8,)), dma, dma((4,)), dma((4,)), dma((8,)), dma((8,)),
        dma((11,)), dma((11,)), dma((10,)), dma((10,)), dma((14,)), dma((14,)), dma((16,)), dma((16,)),
    ]
    d_rows, sheets = pl.pallas_call(
        kernel,
        out_shape=(
            jax.ShapeDtypeStruct((ROWS, D), BF16),
            jax.ShapeDtypeStruct((2, 4, 4, 8, 80, HD), BF16),
        ),
        in_specs=[whole, whole, whole, anywhere, anywhere],
        out_specs=(whole, whole),
        scratch_shapes=scratch,
        compiler_params=pltpu.CompilerParams(
            collective_id=0, has_side_effects=True, vmem_limit_bytes=56 * 2**20
        ),
        name="layer",
    )(history[0], cotangent[0], lengths, w_proj, w_out)
    sheets = sheets.reshape(2, 4, 4, 640, HD)
    grad_p = sheets[:, :, :, :512].transpose(0, 3, 2, 1, 4).reshape(1024, 2048)
    grad_o = sheets[:, :, :, 512:].transpose(1, 3, 0, 2, 4).reshape(512, 1024)
    return d_rows[None], grad_p, grad_o


def solution(mesh):
    in_specs = (P("dp", "ctx", None), P("dp", "ctx", None), P("dp", None), P(), P())
    out_specs = (P("dp", "ctx", None), P(), P())
    return jax.shard_map(
        on_device, mesh=mesh, in_specs=in_specs, out_specs=out_specs, check_vma=False
    )
```

```python
import jax
import jax.numpy as jnp
from jax import lax
from jax.experimental import pallas as pl
from jax.experimental.pallas import tpu as pltpu
from jax.sharding import PartitionSpec as P

F32, BF16 = jnp.float32, jnp.bfloat16
MESH = pl.DeviceIdType.MESH
EPSILON = 1e-05
D = 1024
EVENTS = 1024
HD = 128
ROWS = 128
PAIR = 256
SCALE = HD ** (-0.5)
NT = (((1,), (1,)), ((), ()))


def dot(a, b):
    return jnp.dot(a, b, preferred_element_type=F32)


def dot_nt(a, b):
    return lax.dot_general(a, b, NT, preferred_element_type=F32)


def sigmoid(z):
    return 0.5 * jnp.tanh(0.5 * z) + 0.5


def device(x, yh, yl, z, c):
    return ((yl * 8 + z) * 2 + c, x * 2 + yh)


def remote(src, dst, send, recv, target):
    return pltpu.make_async_remote_copy(
        src_ref=src,
        dst_ref=dst,
        send_sem=send,
        recv_sem=recv,
        device_id=target,
        device_id_type=MESH,
    )


class Flight:
    def __init__(self):
        self.unsent, self.unreceived = [], []

    @staticmethod
    def do(action, when):
        if when is None:
            action()
        else:
            pl.when(when)(action)

    def start(self, copy, when=None, mirrored=True):
        self.do(copy.start, when)
        self.unsent.append((copy.wait_send, when))
        if mirrored:
            self.expect(copy, copy.wait_recv, when)

    def start_local(self, copy, when=None):
        self.do(copy.start, when)
        self.expect(copy, copy.wait, when)

    def expect(self, copy, wait, when=None):
        self.unreceived.append((copy, wait, when))

    def receive(self, copy):
        (entry,) = [e for e in self.unreceived if e[0] is copy]
        self.unreceived = [e for e in self.unreceived if e[0] is not copy]
        self.do(entry[1], entry[2])

    def land(self):
        for entry in list(self.unreceived):
            self.receive(entry[0])
        for wait, when in self.unsent:
            self.do(wait, when)


def kernel(
    hist_in, cot_in, lens, w_proj, w_out, d_hist, gp, go,
    hist, cot, xg, cg, xn, wp, wht, wo, lown, lsib, projt, spt, kr, vr, wm, sm, attnt, dgt, st, stx,
    gt, dat, dkt, dvt, dpt, dpr, pay, ybuf, zsend, zbuf, piece_p, piece_o, dn,
    known, insem, wsem, osem, lsem, swsem, xsem, xrsem, fsem, frsem, csem, crsem, gsem, grsem, stsem, strsem,
    asem, arsem, asem0, ysem, yrsem, zsem, zrsem, g0, g1s, g1r, g2s, g2r, g3s, g3r, g4s, g4r,
):
    dp, ctx = lax.axis_index("dp"), lax.axis_index("ctx")
    c, z, yl = lax.rem(dp, 2), lax.rem(dp // 2, 8), dp // 16
    x, yh = ctx // 2, lax.rem(ctx, 2)
    y = yh * 2 + yl
    sib = device(x, yh, yl, z, 1 - c)

    def x_mate(d):
        return device(lax.rem(x + d, 4), yh, yl, z, c)

    def y_mate(d):
        other = lax.rem(y + d, 4)
        return device(x, other // 2, lax.rem(other, 2), z, c)

    def z_mate(d):
        return device(x, yh, yl, lax.rem(z + d, 8), c)

    def x_from(d):
        return lax.rem(x + 4 - d, 4)

    def y_from(d):
        return lax.rem(y + 4 - d, 4)

    def z_from(d):
        return lax.rem(z + 8 - d, 8)

    here = c == yh
    away = jnp.logical_not(here)
    flight = Flight()

    get_w = pltpu.make_async_copy(w_proj, wp, wsem)
    get_o = pltpu.make_async_copy(w_out.at[pl.ds(pl.multiple_of(x * HD, HD), HD), :], wo, osem)
    get_x = pltpu.make_async_copy(hist_in, hist, insem.at[0])
    get_c = pltpu.make_async_copy(cot_in, cot, insem.at[1])
    flight.start_local(get_x)
    flight.start_local(get_c)
    flight.start_local(get_w)
    flight.start_local(get_o)

    barrier = pltpu.get_barrier_semaphore()
    swap = device(x, 1 - yh, yl, z, 1 - c)
    near = [sib, swap] + [x_mate(d) for d in range(1, 4)] + [y_mate(d) for d in range(1, 4)] + [z_mate(1), z_mate(7)]
    for mate in near:
        pl.semaphore_signal(barrier, inc=1, device_id=mate, device_id_type=MESH)

    def tell(level):
        for mate in (sib, y_mate(2), z_mate(1), z_mate(7)):
            pl.semaphore_signal(known.at[level], inc=1, device_id=mate, device_id_type=MESH)

    def hear(level):
        pl.semaphore_wait(known.at[level], 4)

    lane = lax.broadcasted_iota(jnp.int32, (8, 128), 1)
    first = jnp.broadcast_to(lens[0:1, 0:1], (8, 128))
    second = first + jnp.broadcast_to(lens[0:1, 1:2], (8, 128))
    lown[...] = jnp.where(lane == 0, first, jnp.where(lane == 1, second, 0))

    pl.semaphore_wait(barrier, len(near))
    tell(0)

    slot = pl.ds(pl.multiple_of((2 * x + c) * ROWS, ROWS), ROWS)
    over = pl.ds(pl.multiple_of((2 * x + 1 - c) * ROWS, ROWS), ROWS)
    swap_x = remote(hist, xg.at[over, :], swsem.at[0], swsem.at[1], swap)
    swap_c = remote(cot, cg.at[over, :], swsem.at[2], swsem.at[3], swap)
    flight.receive(get_x)
    flight.start(swap_x, away)
    send_l = remote(lown, lsib, lsem.at[0], lsem.at[1], sib)
    flight.start(send_l)

    @pl.when(here)
    def _():
        xg[slot, :] = hist[...]

    flight.receive(swap_x)
    flight.receive(get_c)
    flight.start(swap_c, away)

    def block_of(d, core):
        return pl.ds(pl.multiple_of((2 * x_from(d) + core) * ROWS, ROWS), ROWS)

    push_x = [remote(xg.at[slot, :], xg.at[slot, :], xsem.at[d], xrsem.at[d], x_mate(d)) for d in range(1, 4)]
    push_c = [remote(cg.at[slot, :], cg.at[slot, :], csem.at[d], crsem.at[d], x_mate(d)) for d in range(1, 4)]
    pass_x = [remote(xg.at[block_of(d, c), :], xg.at[block_of(d, c), :], fsem.at[d], frsem.at[d], sib) for d in range(4)]
    pass_c = [remote(cg.at[block_of(d, c), :], cg.at[block_of(d, c), :], gsem.at[d], grsem.at[d], sib) for d in range(4)]
    for copy in push_x:
        flight.start(copy)
    flight.start(pass_x[0])

    flight.receive(get_w)
    for j in range(4):
        columns = pl.ds(pl.multiple_of(j * 512 + x * HD, HD), HD)
        wht[j * HD : (j + 1) * HD, :] = wp[:, columns].T

    def project(d):
        base = x_from(d) * PAIR

        @pl.loop(0, PAIR // 16, unroll=4)
        def _(i):
            rows = pl.ds(pl.multiple_of(base + i * 16, 16), 16)
            values = xg[rows, :].astype(F32)
            centred = values - jnp.mean(values, axis=-1, keepdims=True)
            variance = jnp.mean(centred * centred, axis=-1, keepdims=True)
            xn[rows, :] = (centred * lax.rsqrt(variance + EPSILON)).astype(BF16)

        rows = pl.ds(pl.multiple_of(base, PAIR), PAIR)
        normed = xn[rows, :]
        pres = dot_nt(wht[...], normed)
        for j in range(4):
            pre = pres[j * HD : (j + 1) * HD]
            s = sigmoid(pre)
            value = pre * s
            spt[j * HD : (j + 1) * HD, rows] = s + value * (1.0 - s)
            value = value.astype(BF16)
            projt[j * HD : (j + 1) * HD, rows] = value
            if j == 1:
                vr[rows, :] = value.T
            if j == 3:
                kr[rows, :] = value.T

    flight.receive(pass_x[0])
    project(0)
    hear(0)
    tell(1)
    for d in (1, 3):
        flight.receive(push_x[d - 1])
        flight.start(pass_x[d])
    flight.receive(swap_c)

    @pl.when(here)
    def _():
        cg[slot, :] = cot[...]

    for copy in push_c:
        flight.start(copy)
    flight.start(pass_c[0])
    for d in (1, 3):
        flight.receive(pass_x[d])
        project(d)
    hear(1)
    tell(2)
    flight.receive(push_x[1])
    flight.start(pass_x[2])
    flight.receive(pass_x[2])
    project(2)

    hear(2)
    flight.receive(send_l)
    ends = jnp.where(here, lown[...], lsib[...])
    first, second = ends[0:1, 0:1], ends[0:1, 1:2]

    for pb in range(4):
        cols = slice(pb * PAIR, (pb + 1) * PAIR)
        q = projt[2 * HD : 3 * HD, cols]
        p_at = lax.broadcasted_iota(jnp.int32, (1, PAIR), 1) + pb * PAIR
        p_end = jnp.where(p_at < first, first, jnp.where(p_at < second, second, EVENTS))
        total = None
        for rb in range(pb, 4):
            rows = slice(rb * PAIR, (rb + 1) * PAIR)
            logits = dot(kr[rows, :], q) * SCALE
            s = sigmoid(logits)
            weight = logits * s
            slope = s + weight * (1.0 - s)
            r_at = lax.broadcasted_iota(jnp.int32, (PAIR, PAIR), 0) + rb * PAIR
            allowed = (r_at >= p_at) & (r_at < p_end)
            weight = jnp.where(allowed, weight, 0.0).astype(BF16)
            wm[rows, cols] = weight
            sm[rows, cols] = jnp.where(allowed, slope, 0.0)
            term = dot(projt[HD : 2 * HD, rows], weight)
            total = term if total is None else total + term
        attnt[:, cols] = total

    for d in (1, 3, 2):
        flight.receive(push_c[d - 1])
        flight.start(pass_c[d])
    for d in range(4):
        flight.receive(pass_c[d])
    flight.receive(get_o)

    st[4:8, :] = jnp.zeros((4, EVENTS), F32)
    for pb in range(4):
        cols = slice(pb * PAIR, (pb + 1) * PAIR)
        d_gated = dot_nt(wo[...], cg[cols, :])
        dgt[:, cols] = d_gated
        attn = attnt[:, cols]
        g = d_gated * projt[0:HD, cols].astype(F32)
        average = jnp.mean(attn, axis=0, keepdims=True)
        centred = attn - average
        st[0:1, cols] = average
        st[1:2, cols] = jnp.sum(centred * centred, axis=0, keepdims=True)
        st[2:3, cols] = jnp.sum(g, axis=0, keepdims=True)
        st[3:4, cols] = jnp.sum(g * centred, axis=0, keepdims=True)

    push_s = [remote(st, stx.at[d], stsem.at[d], strsem.at[d], x_mate(d)) for d in range(1, 4)]
    for copy in push_s:
        flight.start(copy)
    for copy in push_s:
        flight.receive(copy)
    parts = [st[...]] + [stx[d] for d in range(1, 4)]
    average = (parts[0][0:1] + parts[1][0:1] + parts[2][0:1] + parts[3][0:1]) * 0.25
    spread = sum(p[1:2] + HD * (p[0:1] - average) ** 2 for p in parts) * (1.0 / 512)
    a_scale = lax.rsqrt(spread + EPSILON)
    g_mean = sum(p[2:3] for p in parts) * (1.0 / 512)
    ga_mean = a_scale * (sum(p[3:4] + (p[0:1] - average) * p[2:3] for p in parts) * (1.0 / 512))

    for pb in range(4):
        cols = slice(pb * PAIR, (pb + 1) * PAIR)
        u = projt[0:HD, cols].astype(F32)
        d_gated = dgt[:, cols]
        scale = a_scale[:, cols]
        a_norm = (attnt[:, cols] - average[:, cols]) * scale
        gt[:, cols] = (a_norm * u).astype(BF16)
        dpt[0, :, cols] = (d_gated * a_norm * spt[0:HD, cols]).astype(BF16)
        dat[:, cols] = (scale * (d_gated * u - g_mean[:, cols] - a_norm * ga_mean[:, cols])).astype(BF16)

    for pb in range(4):
        cols = slice(pb * PAIR, (pb + 1) * PAIR)
        q = projt[2 * HD : 3 * HD, cols]
        da = dat[:, cols]
        total = None
        for rb in range(pb, 4):
            rows = slice(rb * PAIR, (rb + 1) * PAIR)
            d_logits = (dot(vr[rows, :], da) * sm[rows, cols]).astype(BF16)
            term = dot(projt[3 * HD : 4 * HD, rows], d_logits)
            total = term if total is None else total + term
            d_key = dot_nt(q, d_logits)
            d_value = dot_nt(da, wm[rows, cols])
            if pb == 0:
                dkt[:, rows] = d_key
                dvt[:, rows] = d_value
            else:
                dkt[:, rows] += d_key
                dvt[:, rows] += d_value
        dpt[2, :, cols] = (total * SCALE * spt[2 * HD : 3 * HD, cols]).astype(BF16)
    dpt[1] = (dvt[...] * spt[HD : 2 * HD, :]).astype(BF16)
    dpt[3] = (dkt[...] * SCALE * spt[3 * HD : 4 * HD, :]).astype(BF16)

    half = pl.ds(pl.multiple_of(c * 512, 512), 512)
    grad_o = dot(gt[...], cg[:, half]).astype(BF16)
    for j in range(4):
        pay[j, :, 64:80, :] = grad_o[:, j * HD : (j + 1) * HD].reshape(8, 16, HD)
    push_y = []
    for d in (1, 3, 2, 0):
        j = lax.rem(y + d, 4)
        pay[j, :, 0:64, :] = dot(dpt[j], xn[:, half]).T.astype(BF16).reshape(8, 64, HD)
        if d:
            copy = remote(pay.at[j], ybuf.at[d], ysem.at[d], yrsem.at[d], y_mate(d))
            flight.start(copy)
            push_y.append(copy)
    for copy in push_y:
        flight.receive(copy)
    zsend[...] = (
        pay[y].astype(F32) + ybuf[1].astype(F32) + ybuf[2].astype(F32) + ybuf[3].astype(F32)
    ).astype(BF16)
    push_z = []
    for d in (1, 7, 2, 6, 3, 5, 4):
        copy = remote(zsend.at[lax.rem(z + d, 8)], zbuf.at[d], zsem.at[d], zrsem.at[d], z_mate(d))
        flight.start(copy)
        push_z.append(copy)
    mine = pl.ds(2 * c, 2)
    for dx in range(4):
        for dy in range(2):
            tx, ty = lax.rem(x + dx, 4), lax.rem(yh + dy, 2)
            lanes = pl.ds(pl.multiple_of((tx * 2 + ty) * ROWS, ROWS), ROWS)
            source, place = dpt.at[mine, :, lanes], dpr.at[mine, x]
            copy = remote(source, place, asem.at[dx * 2 + dy], arsem.at[dx * 2 + c], device(tx, ty, yl, z, yh))
            if dx or dy:
                flight.start(copy, mirrored=False)
            else:
                flight.start(copy, away, mirrored=False)
                keep = pltpu.make_async_copy(source, place, asem0)
                flight.start_local(keep, here)
    arrivals = [keep]
    for dx in range(4):
        for core in range(2):
            place = dpr.at[pl.ds(2 * core, 2), x_from(dx)]
            copy = remote(place, place, asem.at[0], arsem.at[dx * 2 + core], sib)
            flight.expect(copy, copy.wait_recv, None if dx else jnp.logical_not(here & (c == core)))
            arrivals.append(copy)

    for copy in push_z:
        flight.receive(copy)
    total = zsend[z].astype(F32)
    for d in range(1, 8):
        total = total + zbuf[d].astype(F32)
    total = total.astype(BF16)
    piece_p[...] = total[0:64].reshape(2, 32, HD)
    piece_o[...] = total[64:80]

    def kind_at(j, head):
        return pl.ds(pl.multiple_of(j * 512 + head * HD, HD), HD)

    own_p = gp.at[c, z, :, :, kind_at(y, x)]
    own_o = go.at[x, z, :, pl.ds(pl.multiple_of(c * 512 + y * HD, HD), HD)]
    keep_p = pltpu.make_async_copy(piece_p, own_p, g0.at[0])
    keep_o = pltpu.make_async_copy(piece_o, own_o, g0.at[1])
    stage1 = [keep_p, keep_o]
    for d in (1, 7, 2, 6, 3, 5, 4):
        stage1.append(remote(piece_p, own_p, g1s.at[d], g1r.at[d], z_mate(d)))
    for d in range(1, 4):
        stage1.append(remote(piece_o, own_o, g1s.at[7 + d], g1r.at[7 + d], y_mate(d)))
    flight.start_local(keep_p)
    flight.start_local(keep_o)
    for copy in stage1[2:]:
        flight.start(copy)

    stage4 = []

    def to_sibling(ref):
        i = len(stage4)
        copy = remote(ref, ref, g4s.at[i], g4r.at[i], sib)
        flight.start(copy)
        stage4.append(copy)

    def part_a(kind, head):
        return gp.at[c, :, 0, :, kind_at(kind, head)]

    def part_b(kind, head):
        return gp.at[c, :, 1, :, kind_at(kind, head)]

    def out_row(copies):
        for copy in copies:
            flight.start(copy)
        return copies

    flight.receive(keep_o)
    for copy in stage1[9:]:
        flight.receive(copy)
    ref = go.at[x, z, :, half]
    second_c = out_row([remote(ref, ref, g2s.at[6 + d], g2r.at[6 + d], x_mate(d)) for d in range(1, 4)])

    def third_a(dj):
        ref = part_a(y_from(dj), x)
        to_sibling(ref)
        return out_row([remote(ref, ref, g3s.at[dj * 4 + d], g3r.at[dj * 4 + d], x_mate(d)) for d in (1, 3, 2)])

    def third_b(dx):
        ref = part_b(y, x_from(dx))
        to_sibling(ref)
        return out_row([remote(ref, ref, g3s.at[16 + dx * 4 + d], g3r.at[16 + dx * 4 + d], y_mate(d)) for d in (1, 3, 2)])

    flight.receive(keep_p)
    for copy in stage1[2:9]:
        flight.receive(copy)
    ref = part_a(y, x)
    second_a = out_row([remote(ref, ref, g2s.at[d], g2r.at[d], y_mate(d)) for d in range(1, 4)])
    ref = part_b(y, x)
    second_b = out_row([remote(ref, ref, g2s.at[3 + d], g2r.at[3 + d], x_mate(d)) for d in range(1, 4)])
    last_a, last_b = {0: third_a(0)}, {0: third_b(0)}
    for copy in second_c:
        flight.receive(copy)
    ref = go.at[:, z, :, half]
    last_c = out_row([remote(ref, ref, g3s.at[32 + d], g3r.at[32 + d], z_mate(d)) for d in (1, 7, 2, 6, 3, 5, 4)])
    to_sibling(ref)
    for d in (1, 3, 2):
        flight.receive(second_a[d - 1])
        last_a[d] = third_a(d)
        flight.receive(second_b[d - 1])
        last_b[d] = third_b(d)

    for copy in arrivals:
        flight.receive(copy)
    columns = dpr[...].reshape(2048, ROWS)
    for i in range(4):
        part = dot(wp[i * 256 : (i + 1) * 256, :], columns)
        dn[:, i * 256 : (i + 1) * 256] = part.T

    @pl.loop(0, ROWS // 16, unroll=2)
    def _(i):
        rows = pl.ds(pl.multiple_of(i * 16, 16), 16)
        values = hist[rows, :].astype(F32)
        centred = values - jnp.mean(values, axis=-1, keepdims=True)
        variance = jnp.mean(centred * centred, axis=-1, keepdims=True)
        scale = lax.rsqrt(variance + EPSILON)
        normed = centred * scale
        grad = dn[rows, :]
        one = jnp.mean(grad, axis=-1, keepdims=True)
        two = jnp.mean(grad * normed, axis=-1, keepdims=True)
        d_hist[rows, :] = (cot[rows, :].astype(F32) + scale * (grad - one - normed * two)).astype(BF16)

    for dj in (0, 1, 3, 2):
        for i, d in enumerate((1, 3, 2)):
            flight.receive(last_a[dj][i])
            to_sibling(part_a(y_from(dj), x_from(d)))
            flight.receive(last_b[dj][i])
            to_sibling(part_b(y_from(d), x_from(dj)))
    for copy, d in zip(last_c, (1, 7, 2, 6, 3, 5, 4)):
        flight.receive(copy)
        to_sibling(go.at[:, z_from(d), :, half])
    for copy in stage4:
        flight.receive(copy)
    flight.land()


def hand_over(rows_in, gp_in, go_in, rows, gp, go, rows_held, gp_held, go_held, get, put):
    steps = []
    for s in range(2):
        for i in range(4):
            at = (s, pl.ds(2 * i, 2))
            steps.append((gp_in.at[at], gp_held.at[at], gp.at[at]))
    for i in range(2):
        at = pl.ds(2 * i, 2)
        steps.append((go_in.at[at], go_held.at[at], go.at[at]))
    steps.append((rows_in, rows_held, rows))
    gets = [pltpu.make_async_copy(a, b, get.at[i]) for i, (a, b, _) in enumerate(steps)]
    puts = [pltpu.make_async_copy(b, c, put.at[i]) for i, (_, b, c) in enumerate(steps)]
    for copy in gets:
        copy.start()
    for first, second in zip(gets, puts):
        first.wait()
        second.start()
    for copy in puts:
        copy.wait()


def on_device(history, cotangent, lengths, w_proj, w_out):
    vmem, dma = pltpu.VMEM, pltpu.SemaphoreType.DMA
    whole = pl.BlockSpec(memory_space=vmem)
    anywhere = pl.BlockSpec(memory_space=pl.ANY)
    scratch = [
        vmem((ROWS, D), BF16),
        vmem((ROWS, D), BF16),
        vmem((EVENTS, D), BF16),
        vmem((EVENTS, D), BF16),
        vmem((EVENTS, D), BF16),
        vmem((D, 2048), BF16),
        vmem((512, D), BF16),
        vmem((HD, D), BF16),
        vmem((8, 128), jnp.int32),
        vmem((8, 128), jnp.int32),
        vmem((512, EVENTS), BF16),
        vmem((512, EVENTS), F32),
        vmem((EVENTS, HD), BF16),
        vmem((EVENTS, HD), BF16),
        vmem((EVENTS, EVENTS), BF16),
        vmem((EVENTS, EVENTS), F32),
        vmem((HD, EVENTS), F32),
        vmem((HD, EVENTS), F32),
        vmem((8, EVENTS), F32),
        vmem((4, 8, EVENTS), F32),
        vmem((HD, EVENTS), BF16),
        vmem((HD, EVENTS), BF16),
        vmem((HD, EVENTS), F32),
        vmem((HD, EVENTS), F32),
        vmem((4, HD, EVENTS), BF16),
        vmem((4, 4, HD, ROWS), BF16),
        vmem((4, 8, 80, HD), BF16),
        vmem((4, 8, 80, HD), BF16),
        vmem((8, 80, HD), BF16),
        vmem((8, 80, HD), BF16),
        vmem((2, 32, HD), BF16),
        vmem((16, HD), BF16),
        vmem((ROWS, D), F32),
        pltpu.SemaphoreType.REGULAR((3,)), dma((2,)), dma, dma, dma((2,)), dma((4,)),
        dma((4,)), dma((4,)), dma((4,)), dma((4,)), dma((4,)), dma((4,)), dma((4,)), dma((4,)), dma((4,)), dma((4,)),
        dma((8,)), dma((8,)), dma, dma((4,)), dma((4,)), dma((8,)), dma((8,)),
        dma((2,)), dma((11,)), dma((11,)), dma((10,)), dma((10,)), dma((40,)), dma((40,)), dma((40,)), dma((40,)),
    ]
    shapes = (
        jax.ShapeDtypeStruct((ROWS, D), BF16),
        jax.ShapeDtypeStruct((2, 8, 2, 32, 2048), BF16),
        jax.ShapeDtypeStruct((4, 8, 16, 1024), BF16),
    )
    results = pl.pallas_call(
        kernel,
        out_shape=shapes,
        in_specs=[anywhere, anywhere, whole, anywhere, anywhere],
        out_specs=(whole, anywhere, anywhere),
        scratch_shapes=scratch,
        compiler_params=pltpu.CompilerParams(
            collective_id=0, has_side_effects=True, vmem_limit_bytes=58 * 2**20
        ),
        name="layer",
    )(history[0], cotangent[0], lengths, w_proj, w_out)
    d_rows, grad_p, grad_o = pl.pallas_call(
        hand_over,
        out_shape=shapes,
        in_specs=[anywhere] * 3,
        out_specs=(anywhere,) * 3,
        scratch_shapes=[vmem(s.shape, s.dtype) for s in shapes] + [dma((11,)), dma((11,))],
        compiler_params=pltpu.CompilerParams(vmem_limit_bytes=58 * 2**20),
        name="hand_over",
    )(*results)
    return d_rows[None], grad_p.reshape(1024, 2048), grad_o.reshape(512, 1024)


def solution(mesh):
    in_specs = (P("dp", "ctx", None), P("dp", "ctx", None), P("dp", None), P(), P())
    out_specs = (P("dp", "ctx", None), P(), P())
    return jax.shard_map(
        on_device, mesh=mesh, in_specs=in_specs, out_specs=out_specs, check_vma=False
    )
```

```python
import jax
import jax.numpy as jnp
from jax import lax
from jax.experimental import pallas as pl
from jax.experimental.pallas import tpu as pltpu
from jax.sharding import PartitionSpec as P

F32, BF16 = jnp.float32, jnp.bfloat16
MESH = pl.DeviceIdType.MESH
EPSILON = 1e-05
D = 1024
EVENTS = 1024
HD = 128
ROWS = 128
PAIR = 256
SCALE = HD ** (-0.5)
NT = (((1,), (1,)), ((), ()))


def dot(a, b):
    return jnp.dot(a, b, preferred_element_type=F32)


def dot_nt(a, b):
    return lax.dot_general(a, b, NT, preferred_element_type=F32)


def sigmoid(z):
    return 0.5 * jnp.tanh(0.5 * z) + 0.5


def device(x, yh, yl, z, c):
    return ((yl * 8 + z) * 2 + c, x * 2 + yh)


def remote(src, dst, send, recv, target):
    return pltpu.make_async_remote_copy(
        src_ref=src,
        dst_ref=dst,
        send_sem=send,
        recv_sem=recv,
        device_id=target,
        device_id_type=MESH,
    )


class Flight:
    def __init__(self):
        self.unsent, self.unreceived = [], []

    @staticmethod
    def do(action, when):
        if when is None:
            action()
        else:
            pl.when(when)(action)

    def start(self, copy, when=None, mirrored=True):
        self.do(copy.start, when)
        self.unsent.append((copy.wait_send, when))
        if mirrored:
            self.expect(copy, copy.wait_recv, when)

    def start_local(self, copy, when=None):
        self.do(copy.start, when)
        self.expect(copy, copy.wait, when)

    def expect(self, copy, wait, when=None):
        self.unreceived.append((copy, wait, when))

    def receive(self, copy):
        (entry,) = [e for e in self.unreceived if e[0] is copy]
        self.unreceived = [e for e in self.unreceived if e[0] is not copy]
        self.do(entry[1], entry[2])

    def land(self):
        for entry in list(self.unreceived):
            self.receive(entry[0])
        for wait, when in self.unsent:
            self.do(wait, when)


def kernel(
    hist_in, cot_in, lens, w_proj, w_out, d_hist, gp, go,
    hist, cot, xg, cg, xn, wp, wht, wo, dgs, lown, lsib, projt, spt, kr, vr, wm, sm, attnt, dgt, st, stx,
    gt, dat, dkt, dvt, dpt, dpr, pay, payo, ybuf, yobuf, zsend, zbuf, piece_p, piece_o, dn,
    known, dgsem, dgrsem, dgfsem, insem, wsem, osem, lsem, swsem, xsem, xrsem, fsem, frsem, csem, crsem, gsem, grsem, stsem, strsem,
    asem, arsem, asem0, ysem, yrsem, zsem, zrsem, g0, g1s, g1r, g2s, g2r, g3s, g3r, g4s, g4r,
):
    dp, ctx = lax.axis_index("dp"), lax.axis_index("ctx")
    c, z, yl = lax.rem(dp, 2), lax.rem(dp // 2, 8), dp // 16
    x, yh = ctx // 2, lax.rem(ctx, 2)
    y = yh * 2 + yl
    sib = device(x, yh, yl, z, 1 - c)

    def x_mate(d):
        return device(lax.rem(x + d, 4), yh, yl, z, c)

    def y_mate(d):
        other = lax.rem(y + d, 4)
        return device(x, other // 2, lax.rem(other, 2), z, c)

    def z_mate(d):
        return device(x, yh, yl, lax.rem(z + d, 8), c)

    def x_from(d):
        return lax.rem(x + 4 - d, 4)

    def y_from(d):
        return lax.rem(y + 4 - d, 4)

    def z_from(d):
        return lax.rem(z + 8 - d, 8)

    here = c == yh
    away = jnp.logical_not(here)
    flight = Flight()

    get_w = pltpu.make_async_copy(w_proj, wp, wsem)
    get_o = pltpu.make_async_copy(w_out, wo, osem)
    get_x = pltpu.make_async_copy(hist_in, hist, insem.at[0])
    get_c = pltpu.make_async_copy(cot_in, cot, insem.at[1])
    flight.start_local(get_x)
    flight.start_local(get_c)
    flight.start_local(get_o)
    flight.start_local(get_w)

    barrier = pltpu.get_barrier_semaphore()
    swap = device(x, 1 - yh, yl, z, 1 - c)
    near = [sib, swap] + [x_mate(d) for d in range(1, 4)] + [y_mate(d) for d in range(1, 4)] + [z_mate(1), z_mate(7)]
    for mate in near:
        pl.semaphore_signal(barrier, inc=1, device_id=mate, device_id_type=MESH)

    def tell(level):
        for mate in (sib, y_mate(2), z_mate(1), z_mate(7)):
            pl.semaphore_signal(known.at[level], inc=1, device_id=mate, device_id_type=MESH)

    def hear(level):
        pl.semaphore_wait(known.at[level], 4)

    lane = lax.broadcasted_iota(jnp.int32, (8, 128), 1)
    first = jnp.broadcast_to(lens[0:1, 0:1], (8, 128))
    second = first + jnp.broadcast_to(lens[0:1, 1:2], (8, 128))
    lown[...] = jnp.where(lane == 0, first, jnp.where(lane == 1, second, 0))

    pl.semaphore_wait(barrier, len(near))
    tell(0)

    slot = pl.ds(pl.multiple_of((2 * x + c) * ROWS, ROWS), ROWS)
    over = pl.ds(pl.multiple_of((2 * x + 1 - c) * ROWS, ROWS), ROWS)
    swap_x = remote(hist, xg.at[over, :], swsem.at[0], swsem.at[1], swap)
    swap_c = remote(cot, cg.at[over, :], swsem.at[2], swsem.at[3], swap)
    flight.receive(get_x)
    flight.start(swap_x, away)
    send_l = remote(lown, lsib, lsem.at[0], lsem.at[1], sib)
    flight.start(send_l)

    @pl.when(here)
    def _():
        xg[slot, :] = hist[...]

    flight.receive(swap_x)
    flight.receive(get_c)
    flight.start(swap_c, away)

    def block_of(d, core):
        return pl.ds(pl.multiple_of((2 * x_from(d) + core) * ROWS, ROWS), ROWS)

    def half_of(d, part):
        return pl.ds(pl.multiple_of((2 * x_from(d) + c) * ROWS + part * (ROWS // 2), ROWS // 2), ROWS // 2)

    push_x = {d: remote(xg.at[slot, :], xg.at[slot, :], xsem.at[d], xrsem.at[d], x_mate(d)) for d in (1, 3)}
    push_c = {d: remote(cg.at[slot, :], cg.at[slot, :], csem.at[d], crsem.at[d], x_mate(d)) for d in (1, 3)}

    def relay(ref, sends, receives, d):
        part = half_of(d, d // 2)
        return remote(ref.at[part, :], ref.at[part, :], sends.at[d - 1], receives.at[d - 1], x_mate(d))

    relay_x = {d: relay(xg, xsem, xrsem, d) for d in (1, 3)}
    relay_c = {d: relay(cg, csem, crsem, d) for d in (1, 3)}
    pass_x = [remote(xg.at[block_of(d, c), :], xg.at[block_of(d, c), :], fsem.at[d], frsem.at[d], sib) for d in range(4)]
    half = pl.ds(pl.multiple_of(c * 512, 512), 512)
    rest = pl.ds(pl.multiple_of(512 - c * 512, 512), 512)
    pass_c = [remote(cg.at[block_of(d, c), rest], cg.at[block_of(d, c), rest], gsem.at[d], grsem.at[d], sib) for d in range(4)]
    for d in (1, 3):
        flight.start(push_x[d])
    flight.start(pass_x[0])

    flight.receive(get_w)
    for j in range(4):
        columns = pl.ds(pl.multiple_of(j * 512 + x * HD, HD), HD)
        wht[j * HD : (j + 1) * HD, :] = wp[:, columns].T

    flight.receive(get_o)
    for i in range(2):
        dgs[i * PAIR : (i + 1) * PAIR, :] = dot_nt(wo[i * PAIR : (i + 1) * PAIR, :], cot[...]).astype(BF16)
    hear(0)
    tell(1)
    at_block = pl.ds(pl.multiple_of((2 * x + yh) * ROWS, ROWS), ROWS)
    for d in range(4):
        head = lax.rem(x + d, 4)
        source = dgs.at[pl.ds(pl.multiple_of(head * HD, HD), HD), :]
        copy = remote(source, dgt.at[:, at_block], dgsem.at[d], dgrsem.at[d * 2 + yh], device(head, c, yl, z, c))
        flight.start(copy, None if d else away, mirrored=False)

    @pl.when(here)
    def _():
        dgt[:, at_block] = dgs[pl.ds(pl.multiple_of(x * HD, HD), HD), :]

    graded = []
    for d in range(4):
        for row in range(2):
            place = dgt.at[:, pl.ds(pl.multiple_of((2 * x_from(d) + row) * ROWS, ROWS), ROWS)]
            copy = remote(place, place, dgsem.at[0], dgrsem.at[d * 2 + row], sib)
            flight.expect(copy, copy.wait_recv, here if d else here & (yh != row))
            graded.append(copy)
    pass_g = remote(dgt, dgt, dgfsem.at[0], dgfsem.at[1], sib)

    def project(d):
        base = x_from(d) * PAIR

        @pl.loop(0, PAIR // 16, unroll=8)
        def _(i):
            rows = pl.ds(pl.multiple_of(base + i * 16, 16), 16)
            values = xg[rows, :].astype(F32)
            centred = values - jnp.mean(values, axis=-1, keepdims=True)
            variance = jnp.mean(centred * centred, axis=-1, keepdims=True)
            xn[rows, :] = (centred * lax.rsqrt(variance + EPSILON)).astype(BF16)

        rows = pl.ds(pl.multiple_of(base, PAIR), PAIR)
        normed = xn[rows, :]
        pres = dot_nt(wht[...], normed)
        for j in range(4):
            pre = pres[j * HD : (j + 1) * HD]
            s = sigmoid(pre)
            value = pre * s
            spt[j * HD : (j + 1) * HD, rows] = s + value * (1.0 - s)
            value = value.astype(BF16)
            projt[j * HD : (j + 1) * HD, rows] = value
            if j == 1:
                vr[rows, :] = value.T
            if j == 3:
                kr[rows, :] = value.T

    flight.receive(pass_x[0])
    project(0)
    for d in (1, 3):
        flight.receive(push_x[d])
        flight.start(relay_x[d])
        flight.start(pass_x[d])
    flight.receive(swap_c)

    @pl.when(here)
    def _():
        cg[slot, :] = cot[...]

    for d in (1, 3):
        flight.start(push_c[d])
    flight.start(pass_c[0])
    for d in (1, 3):
        flight.receive(pass_x[d])
        project(d)
    hear(1)
    tell(2)
    for d in (1, 3):
        flight.receive(relay_x[d])
    flight.start(pass_x[2])
    flight.receive(pass_x[2])
    project(2)

    hear(2)
    flight.receive(send_l)
    ends = jnp.where(here, lown[...], lsib[...])
    first, second = ends[0:1, 0:1], ends[0:1, 1:2]

    for pb in range(4):
        cols = slice(pb * PAIR, (pb + 1) * PAIR)
        q = projt[2 * HD : 3 * HD, cols]
        p_at = lax.broadcasted_iota(jnp.int32, (1, PAIR), 1) + pb * PAIR
        p_end = jnp.where(p_at < first, first, jnp.where(p_at < second, second, EVENTS))
        total = None
        for rb in range(pb, 4):
            rows = slice(rb * PAIR, (rb + 1) * PAIR)
            logits = dot(kr[rows, :], q) * SCALE
            s = sigmoid(logits)
            weight = logits * s
            slope = s + weight * (1.0 - s)
            r_at = lax.broadcasted_iota(jnp.int32, (PAIR, PAIR), 0) + rb * PAIR
            allowed = (r_at >= p_at) & (r_at < p_end)
            weight = jnp.where(allowed, weight, 0.0).astype(BF16)
            wm[rows, cols] = weight
            sm[rows, cols] = jnp.where(allowed, slope, 0.0)
            term = dot(projt[HD : 2 * HD, rows], weight)
            total = term if total is None else total + term
        attnt[:, cols] = total

    for copy in graded:
        flight.receive(copy)
    flight.start(pass_g, here, mirrored=False)
    flight.expect(pass_g, pass_g.wait_recv, away)
    flight.receive(pass_g)
    st[4:8, :] = jnp.zeros((4, EVENTS), F32)
    for pb in range(4):
        cols = slice(pb * PAIR, (pb + 1) * PAIR)
        d_gated = dgt[:, cols].astype(F32)
        attn = attnt[:, cols]
        g = d_gated * projt[0:HD, cols].astype(F32)
        average = jnp.mean(attn, axis=0, keepdims=True)
        centred = attn - average
        st[0:1, cols] = average
        st[1:2, cols] = jnp.sum(centred * centred, axis=0, keepdims=True)
        st[2:3, cols] = jnp.sum(g, axis=0, keepdims=True)
        st[3:4, cols] = jnp.sum(g * centred, axis=0, keepdims=True)

    push_s = [remote(st, stx.at[d], stsem.at[d], strsem.at[d], x_mate(d)) for d in range(1, 4)]
    for copy in push_s:
        flight.start(copy)
    for d in (1, 3):
        flight.receive(push_c[d])
        flight.start(relay_c[d])
        flight.start(pass_c[d])
    for copy in push_s:
        flight.receive(copy)
    parts = [st[...]] + [stx[d] for d in range(1, 4)]
    average = (parts[0][0:1] + parts[1][0:1] + parts[2][0:1] + parts[3][0:1]) * 0.25
    spread = sum(p[1:2] + HD * (p[0:1] - average) ** 2 for p in parts) * (1.0 / 512)
    a_scale = lax.rsqrt(spread + EPSILON)
    g_mean = sum(p[2:3] for p in parts) * (1.0 / 512)
    ga_mean = a_scale * (sum(p[3:4] + (p[0:1] - average) * p[2:3] for p in parts) * (1.0 / 512))

    for pb in range(4):
        cols = slice(pb * PAIR, (pb + 1) * PAIR)
        u = projt[0:HD, cols].astype(F32)
        d_gated = dgt[:, cols].astype(F32)
        scale = a_scale[:, cols]
        a_norm = (attnt[:, cols] - average[:, cols]) * scale
        gt[:, cols] = (a_norm * u).astype(BF16)
        dpt[0, :, cols] = (d_gated * a_norm * spt[0:HD, cols]).astype(BF16)
        dat[:, cols] = (scale * (d_gated * u - g_mean[:, cols] - a_norm * ga_mean[:, cols])).astype(BF16)

    for pb in range(4):
        cols = slice(pb * PAIR, (pb + 1) * PAIR)
        q = projt[2 * HD : 3 * HD, cols]
        da = dat[:, cols]
        total = None
        for rb in range(pb, 4):
            rows = slice(rb * PAIR, (rb + 1) * PAIR)
            d_logits = (dot(vr[rows, :], da) * sm[rows, cols]).astype(BF16)
            term = dot(projt[3 * HD : 4 * HD, rows], d_logits)
            total = term if total is None else total + term
            d_key = dot_nt(q, d_logits)
            d_value = dot_nt(da, wm[rows, cols])
            if pb == 0:
                dkt[:, rows] = d_key
                dvt[:, rows] = d_value
            else:
                dkt[:, rows] += d_key
                dvt[:, rows] += d_value
        dpt[2, :, cols] = (total * SCALE * spt[2 * HD : 3 * HD, cols]).astype(BF16)
    dpt[1] = (dvt[...] * spt[HD : 2 * HD, :]).astype(BF16)
    dpt[3] = (dkt[...] * SCALE * spt[3 * HD : 4 * HD, :]).astype(BF16)

    push_y = []
    for d in (1, 3, 2, 0):
        j = lax.rem(y + d, 4)
        pay[j] = dot(dpt[j], xn[:, half]).T.astype(BF16).reshape(8, 64, HD)
        if d:
            push_y.append(remote(pay.at[j], ybuf.at[d], ysem.at[d], yrsem.at[d], y_mate(d)))
            flight.start(push_y[-1])
    for d in (1, 3):
        flight.receive(relay_c[d])
    flight.start(pass_c[2])
    for d in range(4):
        flight.receive(pass_c[d])
    grad_o = dot(gt[...], cg[:, half]).astype(BF16)
    for j in range(4):
        payo[j] = grad_o[:, j * HD : (j + 1) * HD].reshape(8, 16, HD)
    push_o = []
    for d in (1, 3, 2):
        push_o.append(remote(payo.at[lax.rem(y + d, 4)], yobuf.at[d], ysem.at[3 + d], yrsem.at[3 + d], y_mate(d)))
        flight.start(push_o[-1])
    for copy in push_y + push_o:
        flight.receive(copy)
    zsend[:, 0:64, :] = (
        pay[y].astype(F32) + ybuf[1].astype(F32) + ybuf[2].astype(F32) + ybuf[3].astype(F32)
    ).astype(BF16)
    zsend[:, 64:80, :] = (
        payo[y].astype(F32) + yobuf[1].astype(F32) + yobuf[2].astype(F32) + yobuf[3].astype(F32)
    ).astype(BF16)
    push_z = []
    for d in (1, 7, 2, 6, 3, 5, 4):
        copy = remote(zsend.at[lax.rem(z + d, 8)], zbuf.at[d], zsem.at[d], zrsem.at[d], z_mate(d))
        flight.start(copy)
        push_z.append(copy)
    mine = pl.ds(2 * c, 2)
    for dx in range(4):
        for dy in range(2):
            tx, ty = lax.rem(x + dx, 4), lax.rem(yh + dy, 2)
            lanes = pl.ds(pl.multiple_of((tx * 2 + ty) * ROWS, ROWS), ROWS)
            source, place = dpt.at[mine, :, lanes], dpr.at[mine, x]
            copy = remote(source, place, asem.at[dx * 2 + dy], arsem.at[dx * 2 + c], device(tx, ty, yl, z, yh))
            if dx or dy:
                flight.start(copy, mirrored=False)
            else:
                flight.start(copy, away, mirrored=False)
                keep = pltpu.make_async_copy(source, place, asem0)
                flight.start_local(keep, here)
    arrivals = [keep]
    for dx in range(4):
        for core in range(2):
            place = dpr.at[pl.ds(2 * core, 2), x_from(dx)]
            copy = remote(place, place, asem.at[0], arsem.at[dx * 2 + core], sib)
            flight.expect(copy, copy.wait_recv, None if dx else jnp.logical_not(here & (c == core)))
            arrivals.append(copy)

    for copy in push_z:
        flight.receive(copy)
    total = zsend[z].astype(F32)
    for d in range(1, 8):
        total = total + zbuf[d].astype(F32)
    total = total.astype(BF16)
    piece_p[...] = total[0:64].reshape(2, 32, HD)
    piece_o[...] = total[64:80]

    def kind_at(j, head):
        return pl.ds(pl.multiple_of(j * 512 + head * HD, HD), HD)

    own_p = gp.at[c, z, :, :, kind_at(y, x)]
    own_o = go.at[x, z, :, pl.ds(pl.multiple_of(c * 512 + y * HD, HD), HD)]
    keep_p = pltpu.make_async_copy(piece_p, own_p, g0.at[0])
    keep_o = pltpu.make_async_copy(piece_o, own_o, g0.at[1])
    stage1 = [keep_p, keep_o]
    for d in (1, 7, 2, 6, 3, 5, 4):
        stage1.append(remote(piece_p, own_p, g1s.at[d], g1r.at[d], z_mate(d)))
    for d in range(1, 4):
        stage1.append(remote(piece_o, own_o, g1s.at[7 + d], g1r.at[7 + d], y_mate(d)))
    flight.start_local(keep_p)
    flight.start_local(keep_o)
    for copy in stage1[2:]:
        flight.start(copy)

    stage4 = []

    def to_sibling(ref):
        i = len(stage4)
        copy = remote(ref, ref, g4s.at[i], g4r.at[i], sib)
        flight.start(copy)
        stage4.append(copy)

    def part_a(kind, head):
        return gp.at[c, :, 0, :, kind_at(kind, head)]

    def part_b(kind, head):
        return gp.at[c, :, 1, :, kind_at(kind, head)]

    def out_row(copies):
        for copy in copies:
            flight.start(copy)
        return copies

    flight.receive(keep_o)
    for copy in stage1[9:]:
        flight.receive(copy)
    ref = go.at[x, z, :, half]
    second_c = out_row([remote(ref, ref, g2s.at[6 + d], g2r.at[6 + d], x_mate(d)) for d in range(1, 4)])

    def third_a(dj):
        ref = part_a(y_from(dj), x)
        to_sibling(ref)
        return out_row([remote(ref, ref, g3s.at[dj * 4 + d], g3r.at[dj * 4 + d], x_mate(d)) for d in (1, 3, 2)])

    def third_b(dx):
        ref = part_b(y, x_from(dx))
        to_sibling(ref)
        return out_row([remote(ref, ref, g3s.at[16 + dx * 4 + d], g3r.at[16 + dx * 4 + d], y_mate(d)) for d in (1, 3, 2)])

    flight.receive(keep_p)
    for copy in stage1[2:9]:
        flight.receive(copy)
    ref = part_a(y, x)
    second_a = out_row([remote(ref, ref, g2s.at[d], g2r.at[d], y_mate(d)) for d in range(1, 4)])
    ref = part_b(y, x)
    second_b = out_row([remote(ref, ref, g2s.at[3 + d], g2r.at[3 + d], x_mate(d)) for d in range(1, 4)])
    last_a, last_b = {0: third_a(0)}, {0: third_b(0)}
    for copy in second_c:
        flight.receive(copy)
    ref = go.at[:, z, :, half]
    last_c = out_row([remote(ref, ref, g3s.at[32 + d], g3r.at[32 + d], z_mate(d)) for d in (1, 7, 2, 6, 3, 5, 4)])
    to_sibling(ref)
    for d in (1, 3, 2):
        flight.receive(second_a[d - 1])
        last_a[d] = third_a(d)
        flight.receive(second_b[d - 1])
        last_b[d] = third_b(d)

    for copy in arrivals:
        flight.receive(copy)
    columns = dpr[...].reshape(2048, ROWS)
    for i in range(4):
        part = dot(wp[i * 256 : (i + 1) * 256, :], columns)
        dn[:, i * 256 : (i + 1) * 256] = part.T

    @pl.loop(0, ROWS // 16, unroll=2)
    def _(i):
        rows = pl.ds(pl.multiple_of(i * 16, 16), 16)
        values = hist[rows, :].astype(F32)
        centred = values - jnp.mean(values, axis=-1, keepdims=True)
        variance = jnp.mean(centred * centred, axis=-1, keepdims=True)
        scale = lax.rsqrt(variance + EPSILON)
        normed = centred * scale
        grad = dn[rows, :]
        one = jnp.mean(grad, axis=-1, keepdims=True)
        two = jnp.mean(grad * normed, axis=-1, keepdims=True)
        d_hist[rows, :] = (cot[rows, :].astype(F32) + scale * (grad - one - normed * two)).astype(BF16)

    for dj in (0, 1, 3, 2):
        for i, d in enumerate((1, 3, 2)):
            flight.receive(last_a[dj][i])
            to_sibling(part_a(y_from(dj), x_from(d)))
            flight.receive(last_b[dj][i])
            to_sibling(part_b(y_from(d), x_from(dj)))
    for copy, d in zip(last_c, (1, 7, 2, 6, 3, 5, 4)):
        flight.receive(copy)
        to_sibling(go.at[:, z_from(d), :, half])
    for copy in stage4:
        flight.receive(copy)
    flight.land()


def hand_over(rows_in, gp_in, go_in, rows, gp, go, rows_held, gp_held, go_held, get, put):
    steps = []
    for s in range(2):
        for i in range(4):
            at = (s, pl.ds(2 * i, 2))
            steps.append((gp_in.at[at], gp_held.at[at], gp.at[at]))
    for i in range(2):
        at = pl.ds(2 * i, 2)
        steps.append((go_in.at[at], go_held.at[at], go.at[at]))
    steps.append((rows_in, rows_held, rows))
    gets = [pltpu.make_async_copy(a, b, get.at[i]) for i, (a, b, _) in enumerate(steps)]
    puts = [pltpu.make_async_copy(b, c, put.at[i]) for i, (_, b, c) in enumerate(steps)]
    for copy in gets:
        copy.start()
    for first, second in zip(gets, puts):
        first.wait()
        second.start()
    for copy in puts:
        copy.wait()


def on_device(history, cotangent, lengths, w_proj, w_out):
    vmem, dma = pltpu.VMEM, pltpu.SemaphoreType.DMA
    whole = pl.BlockSpec(memory_space=vmem)
    anywhere = pl.BlockSpec(memory_space=pl.ANY)
    scratch = [
        vmem((ROWS, D), BF16),
        vmem((ROWS, D), BF16),
        vmem((EVENTS, D), BF16),
        vmem((EVENTS, D), BF16),
        vmem((EVENTS, D), BF16),
        vmem((D, 2048), BF16),
        vmem((512, D), BF16),
        vmem((512, D), BF16),
        vmem((512, ROWS), BF16),
        vmem((8, 128), jnp.int32),
        vmem((8, 128), jnp.int32),
        vmem((512, EVENTS), BF16),
        vmem((512, EVENTS), F32),
        vmem((EVENTS, HD), BF16),
        vmem((EVENTS, HD), BF16),
        vmem((EVENTS, EVENTS), BF16),
        vmem((EVENTS, EVENTS), F32),
        vmem((HD, EVENTS), F32),
        vmem((HD, EVENTS), BF16),
        vmem((8, EVENTS), F32),
        vmem((4, 8, EVENTS), F32),
        vmem((HD, EVENTS), BF16),
        vmem((HD, EVENTS), BF16),
        vmem((HD, EVENTS), F32),
        vmem((HD, EVENTS), F32),
        vmem((4, HD, EVENTS), BF16),
        vmem((4, 4, HD, ROWS), BF16),
        vmem((4, 8, 64, HD), BF16),
        vmem((4, 8, 16, HD), BF16),
        vmem((4, 8, 64, HD), BF16),
        vmem((4, 8, 16, HD), BF16),
        vmem((8, 80, HD), BF16),
        vmem((8, 80, HD), BF16),
        vmem((2, 32, HD), BF16),
        vmem((16, HD), BF16),
        vmem((ROWS, D), F32),
        pltpu.SemaphoreType.REGULAR((3,)), dma((4,)), dma((8,)), dma((2,)), dma((2,)), dma, dma, dma((2,)), dma((4,)),
        dma((4,)), dma((4,)), dma((4,)), dma((4,)), dma((4,)), dma((4,)), dma((4,)), dma((4,)), dma((4,)), dma((4,)),
        dma((8,)), dma((8,)), dma, dma((8,)), dma((8,)), dma((8,)), dma((8,)),
        dma((2,)), dma((11,)), dma((11,)), dma((10,)), dma((10,)), dma((40,)), dma((40,)), dma((40,)), dma((40,)),
    ]
    shapes = (
        jax.ShapeDtypeStruct((ROWS, D), BF16),
        jax.ShapeDtypeStruct((2, 8, 2, 32, 2048), BF16),
        jax.ShapeDtypeStruct((4, 8, 16, 1024), BF16),
    )
    results = pl.pallas_call(
        kernel,
        out_shape=shapes,
        in_specs=[anywhere, anywhere, whole, anywhere, anywhere],
        out_specs=(whole, anywhere, anywhere),
        scratch_shapes=scratch,
        compiler_params=pltpu.CompilerParams(
            collective_id=0, has_side_effects=True, vmem_limit_bytes=58 * 2**20
        ),
        name="layer",
    )(history[0], cotangent[0], lengths, w_proj, w_out)
    d_rows, grad_p, grad_o = pl.pallas_call(
        hand_over,
        out_shape=shapes,
        in_specs=[anywhere] * 3,
        out_specs=(anywhere,) * 3,
        scratch_shapes=[vmem(s.shape, s.dtype) for s in shapes] + [dma((11,)), dma((11,))],
        compiler_params=pltpu.CompilerParams(vmem_limit_bytes=58 * 2**20),
        name="hand_over",
    )(*results)
    return d_rows[None], grad_p.reshape(1024, 2048), grad_o.reshape(512, 1024)


def solution(mesh):
    in_specs = (P("dp", "ctx", None), P("dp", "ctx", None), P("dp", None), P(), P())
    out_specs = (P("dp", "ctx", None), P(), P())
    return jax.shard_map(
        on_device, mesh=mesh, in_specs=in_specs, out_specs=out_specs, check_vma=False
    )
```

```python
import jax
import jax.numpy as jnp
from jax import lax
from jax.experimental import pallas as pl
from jax.experimental.pallas import tpu as pltpu
from jax.sharding import PartitionSpec as P

F32, BF16 = jnp.float32, jnp.bfloat16
MESH = pl.DeviceIdType.MESH
EPSILON = 1e-05
D = 1024
EVENTS = 1024
HD = 128
ROWS = 128
PAIR = 256
SCALE = HD ** (-0.5)
NT = (((1,), (1,)), ((), ()))


def dot(a, b):
    return jnp.dot(a, b, preferred_element_type=F32)


def dot_nt(a, b):
    return lax.dot_general(a, b, NT, preferred_element_type=F32)


def sigmoid(z):
    return 0.5 * jnp.tanh(0.5 * z) + 0.5


def device(x, yh, yl, z, c):
    return ((yl * 8 + z) * 2 + c, x * 2 + yh)


def remote(src, dst, send, recv, target):
    return pltpu.make_async_remote_copy(
        src_ref=src,
        dst_ref=dst,
        send_sem=send,
        recv_sem=recv,
        device_id=target,
        device_id_type=MESH,
    )


class Flight:
    def __init__(self):
        self.unsent, self.unreceived = [], []

    @staticmethod
    def do(action, when):
        if when is None:
            action()
        else:
            pl.when(when)(action)

    def start(self, copy, when=None, mirrored=True):
        self.do(copy.start, when)
        self.unsent.append((copy.wait_send, when))
        if mirrored:
            self.expect(copy, copy.wait_recv, when)

    def start_local(self, copy, when=None):
        self.do(copy.start, when)
        self.expect(copy, copy.wait, when)

    def expect(self, copy, wait, when=None):
        self.unreceived.append((copy, wait, when))

    def receive(self, copy):
        (entry,) = [e for e in self.unreceived if e[0] is copy]
        self.unreceived = [e for e in self.unreceived if e[0] is not copy]
        self.do(entry[1], entry[2])

    def land(self):
        for entry in list(self.unreceived):
            self.receive(entry[0])
        for wait, when in self.unsent:
            self.do(wait, when)


def kernel(
    hist_in, cot_in, lens, w_proj, w_out, d_hist, gp, go,
    hist, cot, xg, cg, xn, wp, wht, wo, dgs, lown, lsib, projt, spt, kr, vr, wm, sm, attnt, dgt, st, stx,
    gt, dat, dkt, dvt, dpt, dpr, pay, payo, ybuf, yobuf, zsend, zbuf, piece_p, piece_o, dn,
    known, dgsem, dgrsem, dgfsem, insem, wsem, osem, lsem, swsem, xsem, xrsem, fsem, frsem, csem, crsem, gsem, grsem, stsem, strsem,
    asem, arsem, asem0, ysem, yrsem, zsem, zrsem, g0, g1s, g1r, g2s, g2r, g3s, g3r, g4s, g4r,
):
    dp, ctx = lax.axis_index("dp"), lax.axis_index("ctx")
    c, z, yl = lax.rem(dp, 2), lax.rem(dp // 2, 8), dp // 16
    x, yh = ctx // 2, lax.rem(ctx, 2)
    y = yh * 2 + yl
    sib = device(x, yh, yl, z, 1 - c)

    def x_mate(d):
        return device(lax.rem(x + d, 4), yh, yl, z, c)

    def y_mate(d):
        other = lax.rem(y + d, 4)
        return device(x, other // 2, lax.rem(other, 2), z, c)

    def z_mate(d):
        return device(x, yh, yl, lax.rem(z + d, 8), c)

    def x_from(d):
        return lax.rem(x + 4 - d, 4)

    def y_from(d):
        return lax.rem(y + 4 - d, 4)

    def z_from(d):
        return lax.rem(z + 8 - d, 8)

    here = c == yh
    away = jnp.logical_not(here)
    flight = Flight()

    get_w = pltpu.make_async_copy(w_proj, wp, wsem)
    get_o = pltpu.make_async_copy(w_out, wo, osem)
    get_x = pltpu.make_async_copy(hist_in, hist, insem.at[0])
    get_c = pltpu.make_async_copy(cot_in, cot, insem.at[1])
    flight.start_local(get_x)
    flight.start_local(get_c)
    flight.start_local(get_o)
    flight.start_local(get_w)

    barrier = pltpu.get_barrier_semaphore()
    swap = device(x, 1 - yh, yl, z, 1 - c)
    near = [sib, swap] + [x_mate(d) for d in range(1, 4)] + [y_mate(d) for d in range(1, 4)] + [z_mate(1), z_mate(7)]
    for mate in near:
        pl.semaphore_signal(barrier, inc=1, device_id=mate, device_id_type=MESH)

    def tell(level):
        for mate in (sib, swap, y_mate(2), z_mate(1), z_mate(7)):
            pl.semaphore_signal(known.at[level], inc=1, device_id=mate, device_id_type=MESH)

    def hear(level):
        pl.semaphore_wait(known.at[level], 5)

    lane = lax.broadcasted_iota(jnp.int32, (8, 128), 1)
    first = jnp.broadcast_to(lens[0:1, 0:1], (8, 128))
    second = first + jnp.broadcast_to(lens[0:1, 1:2], (8, 128))
    lown[...] = jnp.where(lane == 0, first, jnp.where(lane == 1, second, 0))

    pl.semaphore_wait(barrier, len(near))
    tell(0)

    slot = pl.ds(pl.multiple_of((2 * x + c) * ROWS, ROWS), ROWS)
    over = pl.ds(pl.multiple_of((2 * x + 1 - c) * ROWS, ROWS), ROWS)
    swap_x = remote(hist, xg.at[over, :], swsem.at[0], swsem.at[1], swap)
    swap_c = remote(cot, cg.at[over, :], swsem.at[2], swsem.at[3], swap)
    flight.receive(get_x)
    flight.start(swap_x, away)
    send_l = remote(lown, lsib, lsem.at[0], lsem.at[1], sib)
    flight.start(send_l)

    @pl.when(here)
    def _():
        xg[slot, :] = hist[...]

    def block_of(d, core):
        return pl.ds(pl.multiple_of((2 * x_from(d) + core) * ROWS, ROWS), ROWS)

    def half_of(d, part):
        return pl.ds(pl.multiple_of((2 * x_from(d) + c) * ROWS + part * (ROWS // 2), ROWS // 2), ROWS // 2)

    push_x = {d: remote(xg.at[slot, :], xg.at[slot, :], xsem.at[d], xrsem.at[d], x_mate(d)) for d in (1, 3)}
    push_c = {d: remote(cg.at[slot, :], cg.at[slot, :], csem.at[d], crsem.at[d], x_mate(d)) for d in (1, 3)}

    def relay(ref, sends, receives, d):
        part = half_of(d, d // 2)
        return remote(ref.at[part, :], ref.at[part, :], sends.at[d - 1], receives.at[d - 1], x_mate(d))

    relay_x = {d: relay(xg, xsem, xrsem, d) for d in (1, 3)}
    relay_c = {d: relay(cg, csem, crsem, d) for d in (1, 3)}
    pass_x = [remote(xg.at[block_of(d, c), :], xg.at[block_of(d, c), :], fsem.at[d], frsem.at[d], sib) for d in range(4)]
    half = pl.ds(pl.multiple_of(c * 512, 512), 512)
    rest = pl.ds(pl.multiple_of(512 - c * 512, 512), 512)
    pass_c = [remote(cg.at[block_of(d, c), rest], cg.at[block_of(d, c), rest], gsem.at[d], grsem.at[d], sib) for d in range(4)]
    far_x = remote(hist, xg.at[over, :], xsem.at[0], xrsem.at[0], device(lax.rem(x + 2, 4), 1 - yh, yl, z, 1 - c))

    def first_pushes(when):
        for copy in (push_x[1], push_x[3], pass_x[0]):
            flight.start(copy, when, mirrored=False)

    arrived_x = {}
    for when, name in ((here, "here"), (away, "away")):
        for d in (1, 3):
            arrived_x[name, d] = object()
            flight.expect(arrived_x[name, d], push_x[d].wait_recv, when)
    flight.expect(pass_x[0], pass_x[0].wait_recv)
    first_pushes(here)

    flight.receive(get_w)
    for j in range(4):
        columns = pl.ds(pl.multiple_of(j * 512 + x * HD, HD), HD)
        wht[j * HD : (j + 1) * HD, :] = wp[:, columns].T

    flight.receive(get_c)
    flight.receive(get_o)
    for i in range(2):
        dgs[i * PAIR : (i + 1) * PAIR, :] = dot_nt(wo[i * PAIR : (i + 1) * PAIR, :], cot[...]).astype(BF16)
    hear(0)
    tell(1)
    flight.start(far_x, away)
    at_block = pl.ds(pl.multiple_of((2 * x + yh) * ROWS, ROWS), ROWS)
    for d in range(4):
        head = lax.rem(x + d, 4)
        source = dgs.at[pl.ds(pl.multiple_of(head * HD, HD), HD), :]
        copy = remote(source, dgt.at[:, at_block], dgsem.at[d], dgrsem.at[d * 2 + yh], device(head, c, yl, z, c))
        flight.start(copy, None if d else away, mirrored=False)

    @pl.when(here)
    def _():
        dgt[:, at_block] = dgs[pl.ds(pl.multiple_of(x * HD, HD), HD), :]

    graded = []
    for d in range(4):
        for row in range(2):
            place = dgt.at[:, pl.ds(pl.multiple_of((2 * x_from(d) + row) * ROWS, ROWS), ROWS)]
            copy = remote(place, place, dgsem.at[0], dgrsem.at[d * 2 + row], sib)
            flight.expect(copy, copy.wait_recv, here if d else here & (yh != row))
            graded.append(copy)
    pass_g = remote(dgt, dgt, dgfsem.at[0], dgfsem.at[1], sib)

    def project(d):
        base = x_from(d) * PAIR

        @pl.loop(0, PAIR // 16, unroll=8)
        def _(i):
            rows = pl.ds(pl.multiple_of(base + i * 16, 16), 16)
            values = xg[rows, :].astype(F32)
            centred = values - jnp.mean(values, axis=-1, keepdims=True)
            variance = jnp.mean(centred * centred, axis=-1, keepdims=True)
            xn[rows, :] = (centred * lax.rsqrt(variance + EPSILON)).astype(BF16)

        rows = pl.ds(pl.multiple_of(base, PAIR), PAIR)
        normed = xn[rows, :]
        pres = dot_nt(wht[...], normed)
        for j in range(4):
            pre = pres[j * HD : (j + 1) * HD]
            s = sigmoid(pre)
            value = pre * s
            spt[j * HD : (j + 1) * HD, rows] = s + value * (1.0 - s)
            value = value.astype(BF16)
            projt[j * HD : (j + 1) * HD, rows] = value
            if j == 1:
                vr[rows, :] = value.T
            if j == 3:
                kr[rows, :] = value.T

    flight.receive(swap_x)
    first_pushes(away)
    flight.start(swap_c, away)
    for d in (1, 3):
        flight.receive(arrived_x["here", d])
        flight.start(relay_x[d], here)
        flight.start(pass_x[d], here, mirrored=False)
    flight.receive(pass_x[0])
    project(0)
    for d in (1, 3):
        flight.receive(arrived_x["away", d])
        flight.start(pass_x[d], away, mirrored=False)
        flight.expect(pass_x[d], pass_x[d].wait_recv)
    hear(1)
    tell(2)
    for d in (1, 3):
        flight.receive(pass_x[d])
        project(d)
    flight.receive(far_x)
    for d in (1, 3):
        flight.receive(relay_x[d])
    flight.start(pass_x[2])
    flight.receive(swap_c)

    @pl.when(here)
    def _():
        cg[slot, :] = cot[...]

    for d in (1, 3):
        flight.start(push_c[d])
    flight.start(pass_c[0])
    flight.receive(pass_x[2])
    project(2)

    hear(2)
    flight.receive(send_l)
    ends = jnp.where(here, lown[...], lsib[...])
    first, second = ends[0:1, 0:1], ends[0:1, 1:2]

    for pb in range(4):
        cols = slice(pb * PAIR, (pb + 1) * PAIR)
        q = projt[2 * HD : 3 * HD, cols]
        p_at = lax.broadcasted_iota(jnp.int32, (1, PAIR), 1) + pb * PAIR
        p_end = jnp.where(p_at < first, first, jnp.where(p_at < second, second, EVENTS))
        total = None
        for rb in range(pb, 4):
            rows = slice(rb * PAIR, (rb + 1) * PAIR)
            logits = dot(kr[rows, :], q) * SCALE
            s = sigmoid(logits)
            weight = logits * s
            slope = s + weight * (1.0 - s)
            r_at = lax.broadcasted_iota(jnp.int32, (PAIR, PAIR), 0) + rb * PAIR
            allowed = (r_at >= p_at) & (r_at < p_end)
            weight = jnp.where(allowed, weight, 0.0).astype(BF16)
            wm[rows, cols] = weight
            sm[rows, cols] = jnp.where(allowed, slope, 0.0)
            term = dot(projt[HD : 2 * HD, rows], weight)
            total = term if total is None else total + term
        attnt[:, cols] = total

    for copy in graded:
        flight.receive(copy)
    flight.start(pass_g, here, mirrored=False)
    flight.expect(pass_g, pass_g.wait_recv, away)
    flight.receive(pass_g)
    st[4:8, :] = jnp.zeros((4, EVENTS), F32)
    for pb in range(4):
        cols = slice(pb * PAIR, (pb + 1) * PAIR)
        d_gated = dgt[:, cols].astype(F32)
        attn = attnt[:, cols]
        g = d_gated * projt[0:HD, cols].astype(F32)
        average = jnp.mean(attn, axis=0, keepdims=True)
        centred = attn - average
        st[0:1, cols] = average
        st[1:2, cols] = jnp.sum(centred * centred, axis=0, keepdims=True)
        st[2:3, cols] = jnp.sum(g, axis=0, keepdims=True)
        st[3:4, cols] = jnp.sum(g * centred, axis=0, keepdims=True)

    push_s = [remote(st, stx.at[d], stsem.at[d], strsem.at[d], x_mate(d)) for d in (2, 1, 3)]
    for copy in push_s:
        flight.start(copy)
    for copy in push_s:
        flight.receive(copy)
    for d in (1, 3):
        flight.receive(push_c[d])
        flight.start(relay_c[d])
        flight.start(pass_c[d])
    parts = [st[...]] + [stx[d] for d in range(1, 4)]
    average = (parts[0][0:1] + parts[1][0:1] + parts[2][0:1] + parts[3][0:1]) * 0.25
    spread = sum(p[1:2] + HD * (p[0:1] - average) ** 2 for p in parts) * (1.0 / 512)
    a_scale = lax.rsqrt(spread + EPSILON)
    g_mean = sum(p[2:3] for p in parts) * (1.0 / 512)
    ga_mean = a_scale * (sum(p[3:4] + (p[0:1] - average) * p[2:3] for p in parts) * (1.0 / 512))

    for pb in range(4):
        cols = slice(pb * PAIR, (pb + 1) * PAIR)
        u = projt[0:HD, cols].astype(F32)
        d_gated = dgt[:, cols].astype(F32)
        scale = a_scale[:, cols]
        a_norm = (attnt[:, cols] - average[:, cols]) * scale
        gt[:, cols] = (a_norm * u).astype(BF16)
        dpt[0, :, cols] = (d_gated * a_norm * spt[0:HD, cols]).astype(BF16)
        dat[:, cols] = (scale * (d_gated * u - g_mean[:, cols] - a_norm * ga_mean[:, cols])).astype(BF16)

    for pb in range(4):
        cols = slice(pb * PAIR, (pb + 1) * PAIR)
        q = projt[2 * HD : 3 * HD, cols]
        da = dat[:, cols]
        total = None
        for rb in range(pb, 4):
            rows = slice(rb * PAIR, (rb + 1) * PAIR)
            d_logits = (dot(vr[rows, :], da) * sm[rows, cols]).astype(BF16)
            term = dot(projt[3 * HD : 4 * HD, rows], d_logits)
            total = term if total is None else total + term
            d_key = dot_nt(q, d_logits)
            d_value = dot_nt(da, wm[rows, cols])
            if pb == 0:
                dkt[:, rows] = d_key
                dvt[:, rows] = d_value
            else:
                dkt[:, rows] += d_key
                dvt[:, rows] += d_value
        dpt[2, :, cols] = (total * SCALE * spt[2 * HD : 3 * HD, cols]).astype(BF16)
    dpt[1] = (dvt[...] * spt[HD : 2 * HD, :]).astype(BF16)
    dpt[3] = (dkt[...] * SCALE * spt[3 * HD : 4 * HD, :]).astype(BF16)

    push_y = []
    for d in (2, 1, 3, 0):
        j = lax.rem(y + d, 4)
        pay[j] = dot(dpt[j], xn[:, half]).T.astype(BF16).reshape(8, 64, HD)
        if d:
            push_y.append(remote(pay.at[j], ybuf.at[d], ysem.at[d], yrsem.at[d], y_mate(d)))
            flight.start(push_y[-1])
    for d in (1, 3):
        flight.receive(relay_c[d])
    flight.start(pass_c[2])
    for d in range(4):
        flight.receive(pass_c[d])
    grad_o = dot(gt[...], cg[:, half]).astype(BF16)
    for j in range(4):
        payo[j] = grad_o[:, j * HD : (j + 1) * HD].reshape(8, 16, HD)
    push_o = []
    for d in (2, 1, 3):
        push_o.append(remote(payo.at[lax.rem(y + d, 4)], yobuf.at[d], ysem.at[3 + d], yrsem.at[3 + d], y_mate(d)))
        flight.start(push_o[-1])
    for copy in push_y + push_o:
        flight.receive(copy)
    zsend[:, 0:64, :] = (
        pay[y].astype(F32) + ybuf[1].astype(F32) + ybuf[2].astype(F32) + ybuf[3].astype(F32)
    ).astype(BF16)
    zsend[:, 64:80, :] = (
        payo[y].astype(F32) + yobuf[1].astype(F32) + yobuf[2].astype(F32) + yobuf[3].astype(F32)
    ).astype(BF16)
    push_z = []
    for d in (4, 3, 5, 2, 6, 1, 7):
        copy = remote(zsend.at[lax.rem(z + d, 8)], zbuf.at[d], zsem.at[d], zrsem.at[d], z_mate(d))
        flight.start(copy)
        push_z.append(copy)
    mine = pl.ds(2 * c, 2)
    for dx in range(4):
        for dy in range(2):
            tx, ty = lax.rem(x + dx, 4), lax.rem(yh + dy, 2)
            lanes = pl.ds(pl.multiple_of((tx * 2 + ty) * ROWS, ROWS), ROWS)
            source, place = dpt.at[mine, :, lanes], dpr.at[mine, x]
            copy = remote(source, place, asem.at[dx * 2 + dy], arsem.at[dx * 2 + c], device(tx, ty, yl, z, yh))
            if dx or dy:
                flight.start(copy, mirrored=False)
            else:
                flight.start(copy, away, mirrored=False)
                keep = pltpu.make_async_copy(source, place, asem0)
                flight.start_local(keep, here)
    arrivals = [keep]
    for dx in range(4):
        for core in range(2):
            place = dpr.at[pl.ds(2 * core, 2), x_from(dx)]
            copy = remote(place, place, asem.at[0], arsem.at[dx * 2 + core], sib)
            flight.expect(copy, copy.wait_recv, None if dx else jnp.logical_not(here & (c == core)))
            arrivals.append(copy)

    for copy in push_z:
        flight.receive(copy)
    total = zsend[z].astype(F32)
    for d in range(1, 8):
        total = total + zbuf[d].astype(F32)
    total = total.astype(BF16)
    piece_p[...] = total[0:64].reshape(2, 32, HD)
    piece_o[...] = total[64:80]

    def kind_at(j, head):
        return pl.ds(pl.multiple_of(j * 512 + head * HD, HD), HD)

    own_p = gp.at[c, z, :, :, kind_at(y, x)]
    own_o = go.at[x, z, :, pl.ds(pl.multiple_of(c * 512 + y * HD, HD), HD)]
    keep_p = pltpu.make_async_copy(piece_p, own_p, g0.at[0])
    keep_o = pltpu.make_async_copy(piece_o, own_o, g0.at[1])
    stage1 = [keep_p, keep_o]
    for d in (4, 3, 5, 2, 6, 1, 7):
        stage1.append(remote(piece_p, own_p, g1s.at[d], g1r.at[d], z_mate(d)))
    for d in (2, 1, 3):
        stage1.append(remote(piece_o, own_o, g1s.at[7 + d], g1r.at[7 + d], y_mate(d)))
    flight.start_local(keep_p)
    flight.start_local(keep_o)
    for copy in stage1[2:]:
        flight.start(copy)

    stage4 = []

    def to_sibling(ref):
        i = len(stage4)
        copy = remote(ref, ref, g4s.at[i], g4r.at[i], sib)
        flight.start(copy)
        stage4.append(copy)

    def part_a(kind, head):
        return gp.at[c, :, 0, :, kind_at(kind, head)]

    def part_b(kind, head):
        return gp.at[c, :, 1, :, kind_at(kind, head)]

    def out_row(copies):
        for copy in copies:
            flight.start(copy)
        return copies

    flight.receive(keep_o)
    for copy in stage1[9:]:
        flight.receive(copy)
    ref = go.at[x, z, :, half]
    second_c = out_row([remote(ref, ref, g2s.at[6 + d], g2r.at[6 + d], x_mate(d)) for d in range(1, 4)])

    quarters = {1: pl.ds(0, 4), 3: pl.ds(4, 4)}
    direct, relays = {}, {}

    def third(dj):
        ref = part_a(y_from(dj), x)
        to_sibling(ref)
        direct["a", dj] = {d: remote(ref, ref, g3s.at[dj * 4 + d], g3r.at[dj * 4 + d], x_mate(d)) for d in (1, 3)}
        out_row(direct["a", dj].values())
        ref = part_b(y, x_from(dj))
        to_sibling(ref)
        direct["b", dj] = {d: remote(ref, ref, g3s.at[16 + dj * 4 + d], g3r.at[16 + dj * 4 + d], y_mate(d)) for d in (1, 3)}
        out_row(direct["b", dj].values())

    def pass_on(dj):
        for name in ("a", "b"):
            relays[name, dj] = []
            for d in (1, 3):
                flight.receive(direct[name, dj][d])
                if name == "a":
                    kind, head, row, at, mate = y_from(dj), x_from(d), 0, dj * 4 + d - 1, x_mate(d)
                else:
                    kind, head, row, at, mate = y_from(d), x_from(dj), 1, 16 + dj * 4 + d - 1, y_mate(d)
                ref = gp.at[c, quarters[d], row, :, kind_at(kind, head)]
                relays[name, dj].append(remote(ref, ref, g3s.at[at], g3r.at[at], mate))
                flight.start(relays[name, dj][-1])
            for d in (1, 3):
                to_sibling(part_a(y_from(dj), x_from(d)) if name == "a" else part_b(y_from(d), x_from(dj)))

    def finish(dj):
        for name in ("a", "b"):
            for copy in relays[name, dj]:
                flight.receive(copy)
            to_sibling(part_a(y_from(dj), x_from(2)) if name == "a" else part_b(y_from(2), x_from(dj)))

    flight.receive(keep_p)
    for copy in stage1[2:9]:
        flight.receive(copy)
    ref = part_a(y, x)
    second_a = {d: remote(ref, ref, g2s.at[d], g2r.at[d], y_mate(d)) for d in (2, 1, 3)}
    out_row(second_a.values())
    ref = part_b(y, x)
    second_b = {d: remote(ref, ref, g2s.at[3 + d], g2r.at[3 + d], x_mate(d)) for d in (2, 1, 3)}
    out_row(second_b.values())
    third(0)
    for copy in second_c:
        flight.receive(copy)
    ref = go.at[:, z, :, half]
    last_c = {d: remote(ref, ref, g3s.at[32 + d], g3r.at[32 + d], z_mate(d)) for d in (2, 6, 1, 7)}
    out_row(last_c.values())
    to_sibling(ref)
    for d in (1, 3):
        flight.receive(second_a[d])
        flight.receive(second_b[d])
        third(d)
    pass_on(0)
    flight.receive(second_a[2])
    flight.receive(second_b[2])
    third(2)
    relay_z = []
    for d, near, at in ((2, 1, 4), (6, 7, 0)):
        flight.receive(last_c[d])
        ref = go.at[:, z_from(d), :, half]
        part = go.at[pl.ds(0 if d == 2 else 2, 2), z_from(d), :, half]
        relay_z.append(remote(ref, ref, g3s.at[32 + d + near - (8 if d == 6 else 0)], g3r.at[32 + d + near - (8 if d == 6 else 0)], z_mate(near)))
        relay_z.append(remote(part, part, g3s.at[32 + at], g3r.at[32 + at], z_mate(d)))
        out_row(relay_z[-2:])
        to_sibling(ref)
    pass_on(1)
    pass_on(3)

    for copy in arrivals:
        flight.receive(copy)
    columns = dpr[...].reshape(2048, ROWS)
    for i in range(4):
        part = dot(wp[i * 256 : (i + 1) * 256, :], columns)
        dn[:, i * 256 : (i + 1) * 256] = part.T

    pass_on(2)
    @pl.loop(0, ROWS // 16, unroll=2)
    def _(i):
        rows = pl.ds(pl.multiple_of(i * 16, 16), 16)
        values = hist[rows, :].astype(F32)
        centred = values - jnp.mean(values, axis=-1, keepdims=True)
        variance = jnp.mean(centred * centred, axis=-1, keepdims=True)
        scale = lax.rsqrt(variance + EPSILON)
        normed = centred * scale
        grad = dn[rows, :]
        one = jnp.mean(grad, axis=-1, keepdims=True)
        two = jnp.mean(grad * normed, axis=-1, keepdims=True)
        d_hist[rows, :] = (cot[rows, :].astype(F32) + scale * (grad - one - normed * two)).astype(BF16)

    for d in (1, 7):
        flight.receive(last_c[d])
        to_sibling(go.at[:, z_from(d), :, half])
    finish(0)
    for copy in relay_z:
        flight.receive(copy)
    for d in (3, 5, 4):
        to_sibling(go.at[:, z_from(d), :, half])
    for dj in (1, 3, 2):
        finish(dj)
    for copy in stage4:
        flight.receive(copy)
    flight.land()


def hand_over(rows_in, gp_in, go_in, rows, gp, go, rows_held, gp_held, go_held, get, put):
    steps = []
    for s in range(2):
        steps.append((gp_in.at[s], gp_held.at[s], gp.at[s]))
    steps.append((go_in, go_held, go))
    steps.append((rows_in, rows_held, rows))
    gets = [pltpu.make_async_copy(a, b, get.at[i]) for i, (a, b, _) in enumerate(steps)]
    puts = [pltpu.make_async_copy(b, c, put.at[i]) for i, (_, b, c) in enumerate(steps)]
    for copy in gets:
        copy.start()
    for first, second in zip(gets, puts):
        first.wait()
        second.start()
    for copy in puts:
        copy.wait()


def on_device(history, cotangent, lengths, w_proj, w_out):
    vmem, dma = pltpu.VMEM, pltpu.SemaphoreType.DMA
    whole = pl.BlockSpec(memory_space=vmem)
    anywhere = pl.BlockSpec(memory_space=pl.ANY)
    scratch = [
        vmem((ROWS, D), BF16),
        vmem((ROWS, D), BF16),
        vmem((EVENTS, D), BF16),
        vmem((EVENTS, D), BF16),
        vmem((EVENTS, D), BF16),
        vmem((D, 2048), BF16),
        vmem((512, D), BF16),
        vmem((512, D), BF16),
        vmem((512, ROWS), BF16),
        vmem((8, 128), jnp.int32),
        vmem((8, 128), jnp.int32),
        vmem((512, EVENTS), BF16),
        vmem((512, EVENTS), F32),
        vmem((EVENTS, HD), BF16),
        vmem((EVENTS, HD), BF16),
        vmem((EVENTS, EVENTS), BF16),
        vmem((EVENTS, EVENTS), F32),
        vmem((HD, EVENTS), F32),
        vmem((HD, EVENTS), BF16),
        vmem((8, EVENTS), F32),
        vmem((4, 8, EVENTS), F32),
        vmem((HD, EVENTS), BF16),
        vmem((HD, EVENTS), BF16),
        vmem((HD, EVENTS), F32),
        vmem((HD, EVENTS), F32),
        vmem((4, HD, EVENTS), BF16),
        vmem((4, 4, HD, ROWS), BF16),
        vmem((4, 8, 64, HD), BF16),
        vmem((4, 8, 16, HD), BF16),
        vmem((4, 8, 64, HD), BF16),
        vmem((4, 8, 16, HD), BF16),
        vmem((8, 80, HD), BF16),
        vmem((8, 80, HD), BF16),
        vmem((2, 32, HD), BF16),
        vmem((16, HD), BF16),
        vmem((ROWS, D), F32),
        pltpu.SemaphoreType.REGULAR((3,)), dma((4,)), dma((8,)), dma((2,)), dma((2,)), dma, dma, dma((2,)), dma((4,)),
        dma((4,)), dma((4,)), dma((4,)), dma((4,)), dma((4,)), dma((4,)), dma((4,)), dma((4,)), dma((4,)), dma((4,)),
        dma((8,)), dma((8,)), dma, dma((8,)), dma((8,)), dma((8,)), dma((8,)),
        dma((2,)), dma((11,)), dma((11,)), dma((10,)), dma((10,)), dma((40,)), dma((40,)), dma((40,)), dma((40,)),
    ]
    shapes = (
        jax.ShapeDtypeStruct((ROWS, D), BF16),
        jax.ShapeDtypeStruct((2, 8, 2, 32, 2048), BF16),
        jax.ShapeDtypeStruct((4, 8, 16, 1024), BF16),
    )
    results = pl.pallas_call(
        kernel,
        out_shape=shapes,
        in_specs=[anywhere, anywhere, whole, anywhere, anywhere],
        out_specs=(whole, anywhere, anywhere),
        scratch_shapes=scratch,
        compiler_params=pltpu.CompilerParams(
            collective_id=0, has_side_effects=True, vmem_limit_bytes=58 * 2**20
        ),
        name="layer",
    )(history[0], cotangent[0], lengths, w_proj, w_out)
    d_rows, grad_p, grad_o = pl.pallas_call(
        hand_over,
        out_shape=shapes,
        in_specs=[anywhere] * 3,
        out_specs=(anywhere,) * 3,
        scratch_shapes=[vmem(s.shape, s.dtype) for s in shapes] + [dma((4,)), dma((4,))],
        compiler_params=pltpu.CompilerParams(vmem_limit_bytes=58 * 2**20),
        name="hand_over",
    )(*results)
    return d_rows[None], grad_p.reshape(1024, 2048), grad_o.reshape(512, 1024)


def solution(mesh):
    in_specs = (P("dp", "ctx", None), P("dp", "ctx", None), P("dp", None), P(), P())
    out_specs = (P("dp", "ctx", None), P(), P())
    return jax.shard_map(
        on_device, mesh=mesh, in_specs=in_specs, out_specs=out_specs, check_vma=False
    )
```

```python
import jax
import jax.numpy as jnp
from jax import lax
from jax.experimental import pallas as pl
from jax.experimental.pallas import tpu as pltpu
from jax.sharding import PartitionSpec as P

F32, BF16 = jnp.float32, jnp.bfloat16
MESH = pl.DeviceIdType.MESH
EPSILON = 1e-05
D = 1024
EVENTS = 1024
HD = 128
ROWS = 128
PAIR = 256
SCALE = HD ** (-0.5)
NT = (((1,), (1,)), ((), ()))


def dot(a, b):
    return jnp.dot(a, b, preferred_element_type=F32)


def dot_nt(a, b):
    return lax.dot_general(a, b, NT, preferred_element_type=F32)


def sigmoid(z):
    return 0.5 * jnp.tanh(0.5 * z) + 0.5


def device(x, yh, yl, z, c):
    return ((yl * 8 + z) * 2 + c, x * 2 + yh)


def remote(src, dst, send, recv, target):
    return pltpu.make_async_remote_copy(
        src_ref=src,
        dst_ref=dst,
        send_sem=send,
        recv_sem=recv,
        device_id=target,
        device_id_type=MESH,
    )


class Flight:
    def __init__(self):
        self.unsent, self.unreceived = [], []

    @staticmethod
    def do(action, when):
        if when is None:
            action()
        else:
            pl.when(when)(action)

    def start(self, copy, when=None, mirrored=True):
        self.do(copy.start, when)
        self.unsent.append((copy.wait_send, when))
        if mirrored:
            self.expect(copy, copy.wait_recv, when)

    def start_local(self, copy, when=None):
        self.do(copy.start, when)
        self.expect(copy, copy.wait, when)

    def expect(self, copy, wait, when=None):
        self.unreceived.append((copy, wait, when))

    def receive(self, copy):
        (entry,) = [e for e in self.unreceived if e[0] is copy]
        self.unreceived = [e for e in self.unreceived if e[0] is not copy]
        self.do(entry[1], entry[2])

    def land(self):
        for entry in list(self.unreceived):
            self.receive(entry[0])
        for wait, when in self.unsent:
            self.do(wait, when)


def kernel(
    hist_in, cot_in, lens, w_proj, w_out, d_hist, gp, go,
    hist, cot, xg, cg, xn, wp, wht, wo, dgs, lown, lsib, projt, spt, kr, vr, wm, sm, attnt, dgt, st, stx,
    gt, dat, dkt, dvt, dpt, dpr, pay, payo, ybuf, yobuf, zsend, zbuf, piece_p, piece_o, dn,
    known, dgsem, dgrsem, dgfsem, insem, wsem, osem, lsem, swsem, xsem, xrsem, fsem, frsem, csem, crsem, gsem, grsem, stsem, strsem,
    asem, arsem, asem0, ysem, yrsem, zsem, zrsem, g0, g1s, g1r, g2s, g2r, g3s, g3r, g4s, g4r,
):
    dp, ctx = lax.axis_index("dp"), lax.axis_index("ctx")
    c, z, yl = lax.rem(dp, 2), lax.rem(dp // 2, 8), dp // 16
    x, yh = ctx // 2, lax.rem(ctx, 2)
    y = yh * 2 + yl
    sib = device(x, yh, yl, z, 1 - c)

    def x_mate(d):
        return device(lax.rem(x + d, 4), yh, yl, z, c)

    def y_mate(d):
        other = lax.rem(y + d, 4)
        return device(x, other // 2, lax.rem(other, 2), z, c)

    def z_mate(d):
        return device(x, yh, yl, lax.rem(z + d, 8), c)

    def x_from(d):
        return lax.rem(x + 4 - d, 4)

    def y_from(d):
        return lax.rem(y + 4 - d, 4)

    def z_from(d):
        return lax.rem(z + 8 - d, 8)

    here = c == yh
    away = jnp.logical_not(here)
    flight = Flight()

    get_w = pltpu.make_async_copy(w_proj, wp, wsem)
    get_o = pltpu.make_async_copy(w_out, wo, osem)
    get_x = pltpu.make_async_copy(hist_in, hist, insem.at[0])
    get_c = pltpu.make_async_copy(cot_in, cot, insem.at[1])
    flight.start_local(get_x)
    flight.start_local(get_c)
    flight.start_local(get_o)
    flight.start_local(get_w)

    barrier = pltpu.get_barrier_semaphore()
    swap = device(x, 1 - yh, yl, z, 1 - c)
    near = [sib, swap] + [x_mate(d) for d in range(1, 4)] + [y_mate(d) for d in range(1, 4)] + [z_mate(1), z_mate(7)]
    for mate in near:
        pl.semaphore_signal(barrier, inc=1, device_id=mate, device_id_type=MESH)

    def tell(level):
        for mate in (sib, swap, y_mate(2), z_mate(1), z_mate(7)):
            pl.semaphore_signal(known.at[level], inc=1, device_id=mate, device_id_type=MESH)

    def hear(level):
        pl.semaphore_wait(known.at[level], 5)

    lane = lax.broadcasted_iota(jnp.int32, (8, 128), 1)
    first = jnp.broadcast_to(lens[0:1, 0:1], (8, 128))
    second = first + jnp.broadcast_to(lens[0:1, 1:2], (8, 128))
    lown[...] = jnp.where(lane == 0, first, jnp.where(lane == 1, second, 0))

    pl.semaphore_wait(barrier, len(near))
    tell(0)

    slot = pl.ds(pl.multiple_of((2 * x + c) * ROWS, ROWS), ROWS)
    over = pl.ds(pl.multiple_of((2 * x + 1 - c) * ROWS, ROWS), ROWS)
    swap_x = remote(hist, xg.at[over, :], swsem.at[0], swsem.at[1], swap)
    swap_c = remote(cot, cg.at[over, :], swsem.at[2], swsem.at[3], swap)
    flight.receive(get_x)
    flight.start(swap_x, away)
    send_l = remote(lown, lsib, lsem.at[0], lsem.at[1], sib)
    flight.start(send_l)

    @pl.when(here)
    def _():
        xg[slot, :] = hist[...]

    def block_of(d, core):
        return pl.ds(pl.multiple_of((2 * x_from(d) + core) * ROWS, ROWS), ROWS)

    def half_of(d, part):
        return pl.ds(pl.multiple_of((2 * x_from(d) + c) * ROWS + part * (ROWS // 2), ROWS // 2), ROWS // 2)

    push_x = {d: remote(xg.at[slot, :], xg.at[slot, :], xsem.at[d], xrsem.at[d], x_mate(d)) for d in (1, 3)}
    push_c = {d: remote(cg.at[slot, :], cg.at[slot, :], csem.at[d], crsem.at[d], x_mate(d)) for d in (1, 3)}

    def relay(ref, sends, receives, d):
        part = half_of(d, d // 2)
        return remote(ref.at[part, :], ref.at[part, :], sends.at[d - 1], receives.at[d - 1], x_mate(d))

    relay_x = {d: relay(xg, xsem, xrsem, d) for d in (1, 3)}
    relay_c = {d: relay(cg, csem, crsem, d) for d in (1, 3)}
    pass_x = [remote(xg.at[block_of(d, c), :], xg.at[block_of(d, c), :], fsem.at[d], frsem.at[d], sib) for d in range(4)]
    half = pl.ds(pl.multiple_of(c * 512, 512), 512)
    rest = pl.ds(pl.multiple_of(512 - c * 512, 512), 512)
    pass_c = [remote(cg.at[block_of(d, c), rest], cg.at[block_of(d, c), rest], gsem.at[d], grsem.at[d], sib) for d in range(4)]
    far_x = remote(hist, xg.at[over, :], xsem.at[0], xrsem.at[0], device(lax.rem(x + 2, 4), 1 - yh, yl, z, 1 - c))

    def first_pushes(when):
        for copy in (push_x[1], push_x[3], pass_x[0]):
            flight.start(copy, when, mirrored=False)

    arrived_x = {}
    for when, name in ((here, "here"), (away, "away")):
        for d in (1, 3):
            arrived_x[name, d] = object()
            flight.expect(arrived_x[name, d], push_x[d].wait_recv, when)
    flight.expect(pass_x[0], pass_x[0].wait_recv)
    first_pushes(here)

    flight.receive(get_w)
    for j in range(4):
        columns = pl.ds(pl.multiple_of(j * 512 + x * HD, HD), HD)
        wht[j * HD : (j + 1) * HD, :] = wp[:, columns].T

    flight.receive(get_c)
    flight.receive(get_o)
    for i in range(2):
        dgs[i * PAIR : (i + 1) * PAIR, :] = dot_nt(wo[i * PAIR : (i + 1) * PAIR, :], cot[...]).astype(BF16)
    hear(0)
    tell(1)
    flight.start(far_x, away)
    at_block = pl.ds(pl.multiple_of((2 * x + yh) * ROWS, ROWS), ROWS)
    for d in range(4):
        head = lax.rem(x + d, 4)
        source = dgs.at[pl.ds(pl.multiple_of(head * HD, HD), HD), :]
        copy = remote(source, dgt.at[:, at_block], dgsem.at[d], dgrsem.at[d * 2 + yh], device(head, c, yl, z, c))
        flight.start(copy, None if d else away, mirrored=False)

    @pl.when(here)
    def _():
        dgt[:, at_block] = dgs[pl.ds(pl.multiple_of(x * HD, HD), HD), :]

    graded = []
    for d in range(4):
        for row in range(2):
            place = dgt.at[:, pl.ds(pl.multiple_of((2 * x_from(d) + row) * ROWS, ROWS), ROWS)]
            copy = remote(place, place, dgsem.at[0], dgrsem.at[d * 2 + row], sib)
            flight.expect(copy, copy.wait_recv, here if d else here & (yh != row))
            graded.append(copy)
    pass_g = remote(dgt, dgt, dgfsem.at[0], dgfsem.at[1], sib)

    def project(d):
        base = x_from(d) * PAIR

        @pl.loop(0, PAIR // 16, unroll=8)
        def _(i):
            rows = pl.ds(pl.multiple_of(base + i * 16, 16), 16)
            values = xg[rows, :].astype(F32)
            centred = values - jnp.mean(values, axis=-1, keepdims=True)
            variance = jnp.mean(centred * centred, axis=-1, keepdims=True)
            xn[rows, :] = (centred * lax.rsqrt(variance + EPSILON)).astype(BF16)

        rows = pl.ds(pl.multiple_of(base, PAIR), PAIR)
        normed = xn[rows, :]
        pres = dot_nt(wht[...], normed)
        for j in range(4):
            pre = pres[j * HD : (j + 1) * HD]
            s = sigmoid(pre)
            value = pre * s
            spt[j * HD : (j + 1) * HD, rows] = s + value * (1.0 - s)
            value = value.astype(BF16)
            projt[j * HD : (j + 1) * HD, rows] = value
            if j == 1:
                vr[rows, :] = value.T
            if j == 3:
                kr[rows, :] = value.T

    flight.receive(swap_x)
    first_pushes(away)
    flight.start(swap_c, away)
    for d in (1, 3):
        flight.receive(arrived_x["here", d])
        flight.start(relay_x[d], here)
        flight.start(pass_x[d], here, mirrored=False)
    flight.receive(pass_x[0])
    project(0)
    for d in (1, 3):
        flight.receive(arrived_x["away", d])
        flight.start(pass_x[d], away, mirrored=False)
        flight.expect(pass_x[d], pass_x[d].wait_recv)
    hear(1)
    tell(2)
    for d in (1, 3):
        flight.receive(pass_x[d])
        project(d)
    flight.receive(far_x)
    for d in (1, 3):
        flight.receive(relay_x[d])
    flight.start(pass_x[2])
    flight.receive(swap_c)

    @pl.when(here)
    def _():
        cg[slot, :] = cot[...]

    for d in (1, 3):
        flight.start(push_c[d])
    flight.start(pass_c[0])
    flight.receive(pass_x[2])
    project(2)

    hear(2)
    flight.receive(send_l)
    ends = jnp.where(here, lown[...], lsib[...])
    first, second = ends[0:1, 0:1], ends[0:1, 1:2]

    for pb in range(4):
        cols = slice(pb * PAIR, (pb + 1) * PAIR)
        q = projt[2 * HD : 3 * HD, cols]
        p_at = lax.broadcasted_iota(jnp.int32, (1, PAIR), 1) + pb * PAIR
        p_end = jnp.where(p_at < first, first, jnp.where(p_at < second, second, EVENTS))
        total = None
        for rb in range(pb, 4):
            rows = slice(rb * PAIR, (rb + 1) * PAIR)
            logits = dot(kr[rows, :], q) * SCALE
            s = sigmoid(logits)
            weight = logits * s
            slope = s + weight * (1.0 - s)
            r_at = lax.broadcasted_iota(jnp.int32, (PAIR, PAIR), 0) + rb * PAIR
            allowed = (r_at >= p_at) & (r_at < p_end)
            weight = jnp.where(allowed, weight, 0.0).astype(BF16)
            wm[rows, cols] = weight
            sm[rows, cols] = jnp.where(allowed, slope, 0.0)
            term = dot(projt[HD : 2 * HD, rows], weight)
            total = term if total is None else total + term
        attnt[:, cols] = total

    for copy in graded:
        flight.receive(copy)
    flight.start(pass_g, here, mirrored=False)
    flight.expect(pass_g, pass_g.wait_recv, away)
    flight.receive(pass_g)
    st[4:8, :] = jnp.zeros((4, EVENTS), F32)
    for pb in range(4):
        cols = slice(pb * PAIR, (pb + 1) * PAIR)
        d_gated = dgt[:, cols].astype(F32)
        attn = attnt[:, cols]
        g = d_gated * projt[0:HD, cols].astype(F32)
        average = jnp.mean(attn, axis=0, keepdims=True)
        centred = attn - average
        st[0:1, cols] = average
        st[1:2, cols] = jnp.sum(centred * centred, axis=0, keepdims=True)
        st[2:3, cols] = jnp.sum(g, axis=0, keepdims=True)
        st[3:4, cols] = jnp.sum(g * centred, axis=0, keepdims=True)

    push_s = [remote(st, stx.at[d], stsem.at[d], strsem.at[d], x_mate(d)) for d in (2, 1, 3)]
    for copy in push_s:
        flight.start(copy)
    for copy in push_s:
        flight.receive(copy)
    for d in (1, 3):
        flight.receive(push_c[d])
        flight.start(relay_c[d])
        flight.start(pass_c[d])
    parts = [st[...]] + [stx[d] for d in range(1, 4)]
    average = (parts[0][0:1] + parts[1][0:1] + parts[2][0:1] + parts[3][0:1]) * 0.25
    spread = sum(p[1:2] + HD * (p[0:1] - average) ** 2 for p in parts) * (1.0 / 512)
    a_scale = lax.rsqrt(spread + EPSILON)
    g_mean = sum(p[2:3] for p in parts) * (1.0 / 512)
    ga_mean = a_scale * (sum(p[3:4] + (p[0:1] - average) * p[2:3] for p in parts) * (1.0 / 512))

    for pb in range(4):
        cols = slice(pb * PAIR, (pb + 1) * PAIR)
        u = projt[0:HD, cols].astype(F32)
        d_gated = dgt[:, cols].astype(F32)
        scale = a_scale[:, cols]
        a_norm = (attnt[:, cols] - average[:, cols]) * scale
        gt[:, cols] = (a_norm * u).astype(BF16)
        dpt[0, :, cols] = (d_gated * a_norm * spt[0:HD, cols]).astype(BF16)
        dat[:, cols] = (scale * (d_gated * u - g_mean[:, cols] - a_norm * ga_mean[:, cols])).astype(BF16)

    for pb in range(4):
        cols = slice(pb * PAIR, (pb + 1) * PAIR)
        q = projt[2 * HD : 3 * HD, cols]
        da = dat[:, cols]
        total = None
        for rb in range(pb, 4):
            rows = slice(rb * PAIR, (rb + 1) * PAIR)
            d_logits = (dot(vr[rows, :], da) * sm[rows, cols]).astype(BF16)
            term = dot(projt[3 * HD : 4 * HD, rows], d_logits)
            total = term if total is None else total + term
            d_key = dot_nt(q, d_logits)
            d_value = dot_nt(da, wm[rows, cols])
            if pb == 0:
                dkt[:, rows] = d_key
                dvt[:, rows] = d_value
            else:
                dkt[:, rows] += d_key
                dvt[:, rows] += d_value
        dpt[2, :, cols] = (total * SCALE * spt[2 * HD : 3 * HD, cols]).astype(BF16)
    dpt[1] = (dvt[...] * spt[HD : 2 * HD, :]).astype(BF16)
    dpt[3] = (dkt[...] * SCALE * spt[3 * HD : 4 * HD, :]).astype(BF16)

    push_y = []
    for d in (2, 1, 3, 0):
        j = lax.rem(y + d, 4)
        pay[j] = dot(dpt[j], xn[:, half]).T.astype(BF16).reshape(8, 64, HD)
        if d:
            push_y.append(remote(pay.at[j], ybuf.at[d], ysem.at[d], yrsem.at[d], y_mate(d)))
            flight.start(push_y[-1])
    for d in (1, 3):
        flight.receive(relay_c[d])
    flight.start(pass_c[2])
    for d in range(4):
        flight.receive(pass_c[d])
    grad_o = dot(gt[...], cg[:, half]).astype(BF16)
    for j in range(4):
        payo[j] = grad_o[:, j * HD : (j + 1) * HD].reshape(8, 16, HD)
    push_o = []
    for d in (2, 1, 3):
        push_o.append(remote(payo.at[lax.rem(y + d, 4)], yobuf.at[d], ysem.at[3 + d], yrsem.at[3 + d], y_mate(d)))
        flight.start(push_o[-1])
    for copy in push_y + push_o:
        flight.receive(copy)
    zsend[:, 0:64, :] = (
        pay[y].astype(F32) + ybuf[1].astype(F32) + ybuf[2].astype(F32) + ybuf[3].astype(F32)
    ).astype(BF16)
    zsend[:, 64:80, :] = (
        payo[y].astype(F32) + yobuf[1].astype(F32) + yobuf[2].astype(F32) + yobuf[3].astype(F32)
    ).astype(BF16)
    push_z = []
    for d in (4, 3, 5, 2, 6, 1, 7):
        copy = remote(zsend.at[lax.rem(z + d, 8)], zbuf.at[d], zsem.at[d], zrsem.at[d], z_mate(d))
        flight.start(copy)
        push_z.append(copy)
    mine = pl.ds(2 * c, 2)
    for dx in range(4):
        for dy in range(2):
            tx, ty = lax.rem(x + dx, 4), lax.rem(yh + dy, 2)
            lanes = pl.ds(pl.multiple_of((tx * 2 + ty) * ROWS, ROWS), ROWS)
            source, place = dpt.at[mine, :, lanes], dpr.at[mine, x]
            copy = remote(source, place, asem.at[dx * 2 + dy], arsem.at[dx * 2 + c], device(tx, ty, yl, z, yh))
            if dx or dy:
                flight.start(copy, mirrored=False)
            else:
                flight.start(copy, away, mirrored=False)
                keep = pltpu.make_async_copy(source, place, asem0)
                flight.start_local(keep, here)
    arrivals = [keep]
    for dx in range(4):
        for core in range(2):
            place = dpr.at[pl.ds(2 * core, 2), x_from(dx)]
            copy = remote(place, place, asem.at[0], arsem.at[dx * 2 + core], sib)
            flight.expect(copy, copy.wait_recv, None if dx else jnp.logical_not(here & (c == core)))
            arrivals.append(copy)

    for copy in push_z:
        flight.receive(copy)
    total = zsend[z].astype(F32)
    for d in range(1, 8):
        total = total + zbuf[d].astype(F32)
    total = total.astype(BF16)
    piece_p[...] = total[0:64].reshape(2, 32, HD)
    piece_o[...] = total[64:80]

    def kind_at(j, head):
        return pl.ds(pl.multiple_of(j * 512 + head * HD, HD), HD)

    own_p = gp.at[c, z, :, :, kind_at(y, x)]
    own_o = go.at[x, z, :, pl.ds(pl.multiple_of(c * 512 + y * HD, HD), HD)]
    keep_p = pltpu.make_async_copy(piece_p, own_p, g0.at[0])
    keep_o = pltpu.make_async_copy(piece_o, own_o, g0.at[1])
    stage1 = [keep_p, keep_o]
    for d in (4, 3, 5, 2, 6, 1, 7):
        stage1.append(remote(piece_p, own_p, g1s.at[d], g1r.at[d], z_mate(d)))
    for d in (2, 1, 3):
        stage1.append(remote(piece_o, own_o, g1s.at[7 + d], g1r.at[7 + d], y_mate(d)))
    flight.start_local(keep_p)
    flight.start_local(keep_o)
    for copy in stage1[2:]:
        flight.start(copy)

    stage4 = []

    def to_sibling(ref):
        i = len(stage4)
        copy = remote(ref, ref, g4s.at[i], g4r.at[i], sib)
        flight.start(copy)
        stage4.append(copy)

    def part_a(kind, head):
        return gp.at[c, :, 0, :, kind_at(kind, head)]

    def part_b(kind, head):
        return gp.at[c, :, 1, :, kind_at(kind, head)]

    def out_row(copies):
        for copy in copies:
            flight.start(copy)
        return copies

    flight.receive(keep_o)
    for copy in stage1[9:]:
        flight.receive(copy)
    ref = go.at[x, z, :, half]
    second_c = out_row([remote(ref, ref, g2s.at[6 + d], g2r.at[6 + d], x_mate(d)) for d in range(1, 4)])

    quarters = {1: pl.ds(0, 4), 3: pl.ds(4, 4)}
    direct, relays = {}, {}

    def third(dj):
        ref = part_a(y_from(dj), x)
        to_sibling(ref)
        direct["a", dj] = {d: remote(ref, ref, g3s.at[dj * 4 + d], g3r.at[dj * 4 + d], x_mate(d)) for d in (1, 3)}
        out_row(direct["a", dj].values())
        ref = part_b(y, x_from(dj))
        to_sibling(ref)
        direct["b", dj] = {d: remote(ref, ref, g3s.at[16 + dj * 4 + d], g3r.at[16 + dj * 4 + d], y_mate(d)) for d in (1, 3)}
        out_row(direct["b", dj].values())

    def pass_on(dj):
        for name in ("a", "b"):
            relays[name, dj] = []
            for d in (1, 3):
                flight.receive(direct[name, dj][d])
                if name == "a":
                    kind, head, row, at, mate = y_from(dj), x_from(d), 0, dj * 4 + d - 1, x_mate(d)
                else:
                    kind, head, row, at, mate = y_from(d), x_from(dj), 1, 16 + dj * 4 + d - 1, y_mate(d)
                ref = gp.at[c, quarters[d], row, :, kind_at(kind, head)]
                relays[name, dj].append(remote(ref, ref, g3s.at[at], g3r.at[at], mate))
                flight.start(relays[name, dj][-1])
            for d in (1, 3):
                to_sibling(part_a(y_from(dj), x_from(d)) if name == "a" else part_b(y_from(d), x_from(dj)))

    def finish(dj):
        for name in ("a", "b"):
            for copy in relays[name, dj]:
                flight.receive(copy)
            to_sibling(part_a(y_from(dj), x_from(2)) if name == "a" else part_b(y_from(2), x_from(dj)))

    flight.receive(keep_p)
    for copy in stage1[2:9]:
        flight.receive(copy)
    ref = part_a(y, x)
    second_a = {d: remote(ref, ref, g2s.at[d], g2r.at[d], y_mate(d)) for d in (2, 1, 3)}
    out_row(second_a.values())
    ref = part_b(y, x)
    second_b = {d: remote(ref, ref, g2s.at[3 + d], g2r.at[3 + d], x_mate(d)) for d in (2, 1, 3)}
    out_row(second_b.values())
    third(0)
    for copy in second_c:
        flight.receive(copy)
    ref = go.at[:, z, :, half]
    last_c = {d: remote(ref, ref, g3s.at[32 + d], g3r.at[32 + d], z_mate(d)) for d in (2, 6, 1, 7)}
    out_row(last_c.values())
    to_sibling(ref)
    for d in (1, 3):
        flight.receive(second_a[d])
        flight.receive(second_b[d])
        third(d)
    pass_on(0)
    flight.receive(second_a[2])
    flight.receive(second_b[2])
    third(2)
    relay_z = []
    for d, near, at in ((2, 1, 4), (6, 7, 0)):
        flight.receive(last_c[d])
        ref = go.at[:, z_from(d), :, half]
        part = go.at[pl.ds(0 if d == 2 else 2, 2), z_from(d), :, half]
        relay_z.append(remote(ref, ref, g3s.at[32 + d + near - (8 if d == 6 else 0)], g3r.at[32 + d + near - (8 if d == 6 else 0)], z_mate(near)))
        relay_z.append(remote(part, part, g3s.at[32 + at], g3r.at[32 + at], z_mate(d)))
        out_row(relay_z[-2:])
        to_sibling(ref)
    pass_on(1)
    pass_on(3)

    for copy in arrivals:
        flight.receive(copy)
    columns = dpr[...].reshape(2048, ROWS)
    for i in range(4):
        part = dot(wp[i * 256 : (i + 1) * 256, :], columns)
        dn[:, i * 256 : (i + 1) * 256] = part.T

    pass_on(2)
    @pl.loop(0, ROWS // 16, unroll=2)
    def _(i):
        rows = pl.ds(pl.multiple_of(i * 16, 16), 16)
        values = hist[rows, :].astype(F32)
        centred = values - jnp.mean(values, axis=-1, keepdims=True)
        variance = jnp.mean(centred * centred, axis=-1, keepdims=True)
        scale = lax.rsqrt(variance + EPSILON)
        normed = centred * scale
        grad = dn[rows, :]
        one = jnp.mean(grad, axis=-1, keepdims=True)
        two = jnp.mean(grad * normed, axis=-1, keepdims=True)
        d_hist[rows, :] = (cot[rows, :].astype(F32) + scale * (grad - one - normed * two)).astype(BF16)

    for d in (1, 7):
        flight.receive(last_c[d])
        to_sibling(go.at[:, z_from(d), :, half])
    finish(0)
    for copy in relay_z:
        flight.receive(copy)
    for d in (3, 5, 4):
        to_sibling(go.at[:, z_from(d), :, half])
    for dj in (1, 3, 2):
        finish(dj)
    for copy in stage4:
        flight.receive(copy)
    flight.land()


def hand_over(rows_in, gp_in, go_in, rows, gp, go, sems):
    copies = [pltpu.make_async_copy(gp_in.at[s], gp.at[s], sems.at[s]) for s in range(2)]
    copies += [pltpu.make_async_copy(go_in, go, sems.at[2]), pltpu.make_async_copy(rows_in, rows, sems.at[3])]
    for copy in copies:
        copy.start()
    for copy in copies:
        copy.wait()


def on_device(history, cotangent, lengths, w_proj, w_out):
    vmem, dma = pltpu.VMEM, pltpu.SemaphoreType.DMA
    whole = pl.BlockSpec(memory_space=vmem)
    anywhere = pl.BlockSpec(memory_space=pl.ANY)
    scratch = [
        vmem((ROWS, D), BF16),
        vmem((ROWS, D), BF16),
        vmem((EVENTS, D), BF16),
        vmem((EVENTS, D), BF16),
        vmem((EVENTS, D), BF16),
        vmem((D, 2048), BF16),
        vmem((512, D), BF16),
        vmem((512, D), BF16),
        vmem((512, ROWS), BF16),
        vmem((8, 128), jnp.int32),
        vmem((8, 128), jnp.int32),
        vmem((512, EVENTS), BF16),
        vmem((512, EVENTS), F32),
        vmem((EVENTS, HD), BF16),
        vmem((EVENTS, HD), BF16),
        vmem((EVENTS, EVENTS), BF16),
        vmem((EVENTS, EVENTS), F32),
        vmem((HD, EVENTS), F32),
        vmem((HD, EVENTS), BF16),
        vmem((8, EVENTS), F32),
        vmem((4, 8, EVENTS), F32),
        vmem((HD, EVENTS), BF16),
        vmem((HD, EVENTS), BF16),
        vmem((HD, EVENTS), F32),
        vmem((HD, EVENTS), F32),
        vmem((4, HD, EVENTS), BF16),
        vmem((4, 4, HD, ROWS), BF16),
        vmem((4, 8, 64, HD), BF16),
        vmem((4, 8, 16, HD), BF16),
        vmem((4, 8, 64, HD), BF16),
        vmem((4, 8, 16, HD), BF16),
        vmem((8, 80, HD), BF16),
        vmem((8, 80, HD), BF16),
        vmem((2, 32, HD), BF16),
        vmem((16, HD), BF16),
        vmem((ROWS, D), F32),
        pltpu.SemaphoreType.REGULAR((3,)), dma((4,)), dma((8,)), dma((2,)), dma((2,)), dma, dma, dma((2,)), dma((4,)),
        dma((4,)), dma((4,)), dma((4,)), dma((4,)), dma((4,)), dma((4,)), dma((4,)), dma((4,)), dma((4,)), dma((4,)),
        dma((8,)), dma((8,)), dma, dma((8,)), dma((8,)), dma((8,)), dma((8,)),
        dma((2,)), dma((11,)), dma((11,)), dma((10,)), dma((10,)), dma((40,)), dma((40,)), dma((40,)), dma((40,)),
    ]
    shapes = (
        jax.ShapeDtypeStruct((ROWS, D), BF16),
        jax.ShapeDtypeStruct((2, 8, 2, 32, 2048), BF16),
        jax.ShapeDtypeStruct((4, 8, 16, 1024), BF16),
    )
    results = pl.pallas_call(
        kernel,
        out_shape=shapes,
        in_specs=[anywhere, anywhere, whole, anywhere, anywhere],
        out_specs=(whole, anywhere, anywhere),
        scratch_shapes=scratch,
        compiler_params=pltpu.CompilerParams(
            collective_id=0, has_side_effects=True, vmem_limit_bytes=47 * 2**20
        ),
        name="layer",
    )(history[0], cotangent[0], lengths, w_proj, w_out)
    d_rows, grad_p, grad_o = pl.pallas_call(
        hand_over,
        out_shape=shapes,
        in_specs=[anywhere] * 3,
        out_specs=(anywhere,) * 3,
        scratch_shapes=[dma((4,))],
        compiler_params=pltpu.CompilerParams(vmem_limit_bytes=4 * 2**20),
        name="hand_over",
    )(*results)
    return d_rows[None], grad_p.reshape(1024, 2048), grad_o.reshape(512, 1024)


def solution(mesh):
    in_specs = (P("dp", "ctx", None), P("dp", "ctx", None), P("dp", None), P(), P())
    out_specs = (P("dp", "ctx", None), P(), P())
    return jax.shard_map(
        on_device, mesh=mesh, in_specs=in_specs, out_specs=out_specs, check_vma=False
    )
```

```python
import jax
import jax.numpy as jnp
from jax import lax
from jax.experimental import pallas as pl
from jax.experimental.pallas import tpu as pltpu
from jax.sharding import PartitionSpec as P

F32, BF16 = jnp.float32, jnp.bfloat16
MESH = pl.DeviceIdType.MESH
EPSILON = 1e-05
D = 1024
EVENTS = 1024
HD = 128
ROWS = 128
PAIR = 256
SCALE = HD ** (-0.5)
NT = (((1,), (1,)), ((), ()))


def dot(a, b):
    return jnp.dot(a, b, preferred_element_type=F32)


def dot_nt(a, b):
    return lax.dot_general(a, b, NT, preferred_element_type=F32)


def sigmoid(z):
    return 0.5 * jnp.tanh(0.5 * z) + 0.5


def device(x, yh, yl, z, c):
    return ((yl * 8 + z) * 2 + c, x * 2 + yh)


def remote(src, dst, send, recv, target):
    return pltpu.make_async_remote_copy(
        src_ref=src,
        dst_ref=dst,
        send_sem=send,
        recv_sem=recv,
        device_id=target,
        device_id_type=MESH,
    )


class Flight:
    def __init__(self):
        self.unsent, self.unreceived = [], []

    @staticmethod
    def do(action, when):
        if when is None:
            action()
        else:
            pl.when(when)(action)

    def start(self, copy, when=None, mirrored=True):
        self.do(copy.start, when)
        self.unsent.append((copy.wait_send, when))
        if mirrored:
            self.expect(copy, copy.wait_recv, when)

    def start_local(self, copy, when=None):
        self.do(copy.start, when)
        self.expect(copy, copy.wait, when)

    def expect(self, copy, wait, when=None):
        self.unreceived.append((copy, wait, when))

    def receive(self, copy):
        (entry,) = [e for e in self.unreceived if e[0] is copy]
        self.unreceived = [e for e in self.unreceived if e[0] is not copy]
        self.do(entry[1], entry[2])

    def land(self):
        for entry in list(self.unreceived):
            self.receive(entry[0])
        for wait, when in self.unsent:
            self.do(wait, when)


def kernel(
    hist_in, cot_in, lens, w_proj, w_out, d_hist, gp, go,
    hist, cot, xg, cg, xn, wp, wht, wo, dgs, lown, lsib, projt, spt, kr, vr, wm, sm, attnt, dgt, st, stx,
    gt, dat, dkt, dvt, dpt, dpr, pay, payo, ybuf, yobuf, zsend, zbuf, piece_p, piece_o, dn,
    known, dgsem, dgrsem, dgfsem, insem, wsem, osem, lsem, swsem, xsem, xrsem, fsem, frsem, csem, crsem, gsem, grsem, stsem, strsem,
    asem, arsem, asem0, ysem, yrsem, zsem, zrsem, g0, g1s, g1r, g2s, g2r, g3s, g3r, g4s, g4r,
):
    dp, ctx = lax.axis_index("dp"), lax.axis_index("ctx")
    c, z, yl = lax.rem(dp, 2), lax.rem(dp // 2, 8), dp // 16
    x, yh = ctx // 2, lax.rem(ctx, 2)
    y = yh * 2 + yl
    sib = device(x, yh, yl, z, 1 - c)

    def x_mate(d):
        return device(lax.rem(x + d, 4), yh, yl, z, c)

    def y_mate(d):
        other = lax.rem(y + d, 4)
        return device(x, other // 2, lax.rem(other, 2), z, c)

    def z_mate(d):
        return device(x, yh, yl, lax.rem(z + d, 8), c)

    def x_from(d):
        return lax.rem(x + 4 - d, 4)

    def y_from(d):
        return lax.rem(y + 4 - d, 4)

    def z_from(d):
        return lax.rem(z + 8 - d, 8)

    here = c == yh
    away = jnp.logical_not(here)
    flight = Flight()

    get_w = pltpu.make_async_copy(w_proj, wp, wsem)
    get_o = pltpu.make_async_copy(w_out, wo, osem)
    get_x = pltpu.make_async_copy(hist_in, hist, insem.at[0])
    get_c = pltpu.make_async_copy(cot_in, cot, insem.at[1])
    flight.start_local(get_x)
    flight.start_local(get_c)
    flight.start_local(get_o)
    flight.start_local(get_w)

    barrier = pltpu.get_barrier_semaphore()
    swap = device(x, 1 - yh, yl, z, 1 - c)
    near = [sib, swap] + [x_mate(d) for d in range(1, 4)] + [y_mate(d) for d in range(1, 4)] + [z_mate(1), z_mate(7)]
    for mate in near:
        pl.semaphore_signal(barrier, inc=1, device_id=mate, device_id_type=MESH)

    def tell(level):
        for mate in (sib, swap, y_mate(2), z_mate(1), z_mate(7)):
            pl.semaphore_signal(known.at[level], inc=1, device_id=mate, device_id_type=MESH)

    def hear(level):
        pl.semaphore_wait(known.at[level], 5)

    lane = lax.broadcasted_iota(jnp.int32, (8, 128), 1)
    first = jnp.broadcast_to(lens[0:1, 0:1], (8, 128))
    second = first + jnp.broadcast_to(lens[0:1, 1:2], (8, 128))
    lown[...] = jnp.where(lane == 0, first, jnp.where(lane == 1, second, 0))

    pl.semaphore_wait(barrier, len(near))
    tell(0)

    slot = pl.ds(pl.multiple_of((2 * x + c) * ROWS, ROWS), ROWS)
    over = pl.ds(pl.multiple_of((2 * x + 1 - c) * ROWS, ROWS), ROWS)
    swap_x = remote(hist, xg.at[over, :], swsem.at[0], swsem.at[1], swap)
    swap_c = remote(cot, cg.at[over, :], swsem.at[2], swsem.at[3], swap)
    flight.receive(get_x)
    flight.start(swap_x, away)
    send_l = remote(lown, lsib, lsem.at[0], lsem.at[1], sib)
    flight.start(send_l)

    @pl.when(here)
    def _():
        xg[slot, :] = hist[...]

    def block_of(d, core):
        return pl.ds(pl.multiple_of((2 * x_from(d) + core) * ROWS, ROWS), ROWS)

    def half_of(d, part):
        return pl.ds(pl.multiple_of((2 * x_from(d) + c) * ROWS + part * (ROWS // 2), ROWS // 2), ROWS // 2)

    push_x = {d: remote(xg.at[slot, :], xg.at[slot, :], xsem.at[d], xrsem.at[d], x_mate(d)) for d in (1, 3)}
    push_c = {d: remote(cg.at[slot, :], cg.at[slot, :], csem.at[d], crsem.at[d], x_mate(d)) for d in (1, 3)}

    def relay(ref, sends, receives, d):
        part = half_of(d, d // 2)
        return remote(ref.at[part, :], ref.at[part, :], sends.at[d - 1], receives.at[d - 1], x_mate(d))

    relay_x = {d: relay(xg, xsem, xrsem, d) for d in (1, 3)}
    relay_c = {d: relay(cg, csem, crsem, d) for d in (1, 3)}
    pass_x = [remote(xg.at[block_of(d, c), :], xg.at[block_of(d, c), :], fsem.at[d], frsem.at[d], sib) for d in range(4)]
    half = pl.ds(pl.multiple_of(c * 512, 512), 512)
    rest = pl.ds(pl.multiple_of(512 - c * 512, 512), 512)
    pass_c = [remote(cg.at[block_of(d, c), rest], cg.at[block_of(d, c), rest], gsem.at[d], grsem.at[d], sib) for d in range(4)]
    far_x = remote(hist, xg.at[over, :], xsem.at[0], xrsem.at[0], device(lax.rem(x + 2, 4), 1 - yh, yl, z, 1 - c))

    def first_pushes(when):
        for copy in (push_x[1], push_x[3], pass_x[0]):
            flight.start(copy, when, mirrored=False)

    arrived_x = {}
    for when, name in ((here, "here"), (away, "away")):
        for d in (1, 3):
            arrived_x[name, d] = object()
            flight.expect(arrived_x[name, d], push_x[d].wait_recv, when)
    flight.expect(pass_x[0], pass_x[0].wait_recv)
    first_pushes(here)

    flight.receive(get_w)
    for j in range(4):
        columns = pl.ds(pl.multiple_of(j * 512 + x * HD, HD), HD)
        wht[j * HD : (j + 1) * HD, :] = wp[:, columns].T

    flight.receive(get_c)
    flight.receive(get_o)
    for i in range(2):
        dgs[i * PAIR : (i + 1) * PAIR, :] = dot_nt(wo[i * PAIR : (i + 1) * PAIR, :], cot[...]).astype(BF16)
    hear(0)
    tell(1)
    flight.start(far_x, away)
    at_block = pl.ds(pl.multiple_of((2 * x + yh) * ROWS, ROWS), ROWS)
    for d in range(4):
        head = lax.rem(x + d, 4)
        source = dgs.at[pl.ds(pl.multiple_of(head * HD, HD), HD), :]
        copy = remote(source, dgt.at[:, at_block], dgsem.at[d], dgrsem.at[d * 2 + yh], device(head, c, yl, z, c))
        flight.start(copy, None if d else away, mirrored=False)

    @pl.when(here)
    def _():
        dgt[:, at_block] = dgs[pl.ds(pl.multiple_of(x * HD, HD), HD), :]

    graded = []
    for d in range(4):
        for row in range(2):
            place = dgt.at[:, pl.ds(pl.multiple_of((2 * x_from(d) + row) * ROWS, ROWS), ROWS)]
            copy = remote(place, place, dgsem.at[0], dgrsem.at[d * 2 + row], sib)
            flight.expect(copy, copy.wait_recv, here if d else here & (yh != row))
            graded.append(copy)
    pass_g = remote(dgt, dgt, dgfsem.at[0], dgfsem.at[1], sib)

    def project(d):
        base = x_from(d) * PAIR

        @pl.loop(0, PAIR // 16, unroll=8)
        def _(i):
            rows = pl.ds(pl.multiple_of(base + i * 16, 16), 16)
            values = xg[rows, :].astype(F32)
            centred = values - jnp.mean(values, axis=-1, keepdims=True)
            variance = jnp.mean(centred * centred, axis=-1, keepdims=True)
            xn[rows, :] = (centred * lax.rsqrt(variance + EPSILON)).astype(BF16)

        rows = pl.ds(pl.multiple_of(base, PAIR), PAIR)
        normed = xn[rows, :]
        pres = dot_nt(wht[...], normed)
        for j in range(4):
            pre = pres[j * HD : (j + 1) * HD]
            s = sigmoid(pre)
            value = pre * s
            spt[j * HD : (j + 1) * HD, rows] = s + value * (1.0 - s)
            value = value.astype(BF16)
            projt[j * HD : (j + 1) * HD, rows] = value
            if j == 1:
                vr[rows, :] = value.T
            if j == 3:
                kr[rows, :] = value.T

    flight.receive(swap_x)
    first_pushes(away)
    flight.start(swap_c, away)
    for d in (1, 3):
        flight.receive(arrived_x["here", d])
        flight.start(relay_x[d], here)
        flight.start(pass_x[d], here, mirrored=False)
    flight.receive(pass_x[0])
    project(0)
    for d in (1, 3):
        flight.receive(arrived_x["away", d])
        flight.start(pass_x[d], away, mirrored=False)
        flight.expect(pass_x[d], pass_x[d].wait_recv)
    hear(1)
    tell(2)
    for d in (1, 3):
        flight.receive(pass_x[d])
        project(d)
    flight.receive(far_x)
    for d in (1, 3):
        flight.receive(relay_x[d])
    flight.start(pass_x[2])
    flight.receive(swap_c)

    @pl.when(here)
    def _():
        cg[slot, :] = cot[...]

    for d in (1, 3):
        flight.start(push_c[d])
    flight.start(pass_c[0])
    flight.receive(pass_x[2])
    project(2)

    hear(2)
    flight.receive(send_l)
    ends = jnp.where(here, lown[...], lsib[...])
    first, second = ends[0:1, 0:1], ends[0:1, 1:2]

    for pb in range(4):
        cols = slice(pb * PAIR, (pb + 1) * PAIR)
        q = projt[2 * HD : 3 * HD, cols]
        p_at = lax.broadcasted_iota(jnp.int32, (1, PAIR), 1) + pb * PAIR
        p_end = jnp.where(p_at < first, first, jnp.where(p_at < second, second, EVENTS))
        total = None
        for rb in range(pb, 4):
            rows = slice(rb * PAIR, (rb + 1) * PAIR)
            logits = dot(kr[rows, :], q) * SCALE
            s = sigmoid(logits)
            weight = logits * s
            slope = s + weight * (1.0 - s)
            r_at = lax.broadcasted_iota(jnp.int32, (PAIR, PAIR), 0) + rb * PAIR
            allowed = (r_at >= p_at) & (r_at < p_end)
            weight = jnp.where(allowed, weight, 0.0).astype(BF16)
            wm[rows, cols] = weight
            sm[rows, cols] = jnp.where(allowed, slope, 0.0)
            term = dot(projt[HD : 2 * HD, rows], weight)
            total = term if total is None else total + term
        attnt[:, cols] = total

    for copy in graded:
        flight.receive(copy)
    flight.start(pass_g, here, mirrored=False)
    flight.expect(pass_g, pass_g.wait_recv, away)
    flight.receive(pass_g)
    st[4:8, :] = jnp.zeros((4, EVENTS), F32)
    for pb in range(4):
        cols = slice(pb * PAIR, (pb + 1) * PAIR)
        d_gated = dgt[:, cols].astype(F32)
        attn = attnt[:, cols]
        g = d_gated * projt[0:HD, cols].astype(F32)
        average = jnp.mean(attn, axis=0, keepdims=True)
        centred = attn - average
        st[0:1, cols] = average
        st[1:2, cols] = jnp.sum(centred * centred, axis=0, keepdims=True)
        st[2:3, cols] = jnp.sum(g, axis=0, keepdims=True)
        st[3:4, cols] = jnp.sum(g * centred, axis=0, keepdims=True)

    push_s = [remote(st, stx.at[d], stsem.at[d], strsem.at[d], x_mate(d)) for d in (2, 1, 3)]
    for copy in push_s:
        flight.start(copy)
    for copy in push_s:
        flight.receive(copy)
    for d in (1, 3):
        flight.receive(push_c[d])
        flight.start(relay_c[d])
        flight.start(pass_c[d])
    parts = [st[...]] + [stx[d] for d in range(1, 4)]
    average = (parts[0][0:1] + parts[1][0:1] + parts[2][0:1] + parts[3][0:1]) * 0.25
    spread = sum(p[1:2] + HD * (p[0:1] - average) ** 2 for p in parts) * (1.0 / 512)
    a_scale = lax.rsqrt(spread + EPSILON)
    g_mean = sum(p[2:3] for p in parts) * (1.0 / 512)
    ga_mean = a_scale * (sum(p[3:4] + (p[0:1] - average) * p[2:3] for p in parts) * (1.0 / 512))

    for pb in range(4):
        cols = slice(pb * PAIR, (pb + 1) * PAIR)
        u = projt[0:HD, cols].astype(F32)
        d_gated = dgt[:, cols].astype(F32)
        scale = a_scale[:, cols]
        a_norm = (attnt[:, cols] - average[:, cols]) * scale
        gt[:, cols] = (a_norm * u).astype(BF16)
        dpt[0, :, cols] = (d_gated * a_norm * spt[0:HD, cols]).astype(BF16)
        dat[:, cols] = (scale * (d_gated * u - g_mean[:, cols] - a_norm * ga_mean[:, cols])).astype(BF16)

    for pb in range(4):
        cols = slice(pb * PAIR, (pb + 1) * PAIR)
        q = projt[2 * HD : 3 * HD, cols]
        da = dat[:, cols]
        total = None
        for rb in range(pb, 4):
            rows = slice(rb * PAIR, (rb + 1) * PAIR)
            d_logits = (dot(vr[rows, :], da) * sm[rows, cols]).astype(BF16)
            term = dot(projt[3 * HD : 4 * HD, rows], d_logits)
            total = term if total is None else total + term
            d_key = dot_nt(q, d_logits)
            d_value = dot_nt(da, wm[rows, cols])
            if pb == 0:
                dkt[:, rows] = d_key
                dvt[:, rows] = d_value
            else:
                dkt[:, rows] += d_key
                dvt[:, rows] += d_value
        dpt[2, :, cols] = (total * SCALE * spt[2 * HD : 3 * HD, cols]).astype(BF16)
    dpt[1] = (dvt[...] * spt[HD : 2 * HD, :]).astype(BF16)
    dpt[3] = (dkt[...] * SCALE * spt[3 * HD : 4 * HD, :]).astype(BF16)

    push_y = []
    for d in (2, 1, 3, 0):
        j = lax.rem(y + d, 4)
        pay[j] = dot(dpt[j], xn[:, half]).T.astype(BF16).reshape(8, 64, HD)
        if d:
            push_y.append(remote(pay.at[j], ybuf.at[d], ysem.at[d], yrsem.at[d], y_mate(d)))
            flight.start(push_y[-1])
    for d in (1, 3):
        flight.receive(relay_c[d])
    flight.start(pass_c[2])
    for d in range(4):
        flight.receive(pass_c[d])
    grad_o = dot(gt[...], cg[:, half]).astype(BF16)
    for j in range(4):
        payo[j] = grad_o[:, j * HD : (j + 1) * HD].reshape(8, 16, HD)
    push_o = []
    for d in (2, 1, 3):
        push_o.append(remote(payo.at[lax.rem(y + d, 4)], yobuf.at[d], ysem.at[3 + d], yrsem.at[3 + d], y_mate(d)))
        flight.start(push_o[-1])
    for copy in push_y + push_o:
        flight.receive(copy)
    zsend[:, 0:64, :] = (
        pay[y].astype(F32) + ybuf[1].astype(F32) + ybuf[2].astype(F32) + ybuf[3].astype(F32)
    ).astype(BF16)
    zsend[:, 64:80, :] = (
        payo[y].astype(F32) + yobuf[1].astype(F32) + yobuf[2].astype(F32) + yobuf[3].astype(F32)
    ).astype(BF16)
    push_z = []
    for d in (4, 3, 5, 2, 6, 1, 7):
        copy = remote(zsend.at[lax.rem(z + d, 8)], zbuf.at[d], zsem.at[d], zrsem.at[d], z_mate(d))
        flight.start(copy)
        push_z.append(copy)
    mine = pl.ds(2 * c, 2)
    for dx in range(4):
        for dy in range(2):
            tx, ty = lax.rem(x + dx, 4), lax.rem(yh + dy, 2)
            lanes = pl.ds(pl.multiple_of((tx * 2 + ty) * ROWS, ROWS), ROWS)
            source, place = dpt.at[mine, :, lanes], dpr.at[mine, x]
            copy = remote(source, place, asem.at[dx * 2 + dy], arsem.at[dx * 2 + c], device(tx, ty, yl, z, yh))
            if dx or dy:
                flight.start(copy, mirrored=False)
            else:
                flight.start(copy, away, mirrored=False)
                keep = pltpu.make_async_copy(source, place, asem0)
                flight.start_local(keep, here)
    arrivals = [keep]
    for dx in range(4):
        for core in range(2):
            place = dpr.at[pl.ds(2 * core, 2), x_from(dx)]
            copy = remote(place, place, asem.at[0], arsem.at[dx * 2 + core], sib)
            flight.expect(copy, copy.wait_recv, None if dx else jnp.logical_not(here & (c == core)))
            arrivals.append(copy)

    for copy in push_z:
        flight.receive(copy)
    total = zsend[z].astype(F32)
    for d in range(1, 8):
        total = total + zbuf[d].astype(F32)
    total = total.astype(BF16)
    piece_p[...] = total[0:64].reshape(2, 32, HD)
    piece_o[...] = total[64:80]

    def kind_at(j, head):
        return pl.ds(pl.multiple_of(j * 512 + head * HD, HD), HD)

    own_p = gp.at[c, z, :, :, kind_at(y, x)]
    own_o = go.at[x, z, :, pl.ds(pl.multiple_of(c * 512 + y * HD, HD), HD)]
    keep_p = pltpu.make_async_copy(piece_p, own_p, g0.at[0])
    keep_o = pltpu.make_async_copy(piece_o, own_o, g0.at[1])
    stage1 = [keep_p, keep_o]
    for d in (4, 3, 5, 2, 6, 1, 7):
        stage1.append(remote(piece_p, own_p, g1s.at[d], g1r.at[d], z_mate(d)))
    for d in (2, 1, 3):
        stage1.append(remote(piece_o, own_o, g1s.at[7 + d], g1r.at[7 + d], y_mate(d)))
    flight.start_local(keep_p)
    flight.start_local(keep_o)
    for copy in stage1[2:]:
        flight.start(copy)

    for copy in arrivals:
        flight.receive(copy)
    columns = dpr[...].reshape(2048, ROWS)
    for i in range(4):
        part = dot(wp[i * 256 : (i + 1) * 256, :], columns)
        dn[:, i * 256 : (i + 1) * 256] = part.T

    @pl.loop(0, ROWS // 16, unroll=2)
    def _(i):
        rows = pl.ds(pl.multiple_of(i * 16, 16), 16)
        values = hist[rows, :].astype(F32)
        centred = values - jnp.mean(values, axis=-1, keepdims=True)
        variance = jnp.mean(centred * centred, axis=-1, keepdims=True)
        scale = lax.rsqrt(variance + EPSILON)
        normed = centred * scale
        grad = dn[rows, :]
        one = jnp.mean(grad, axis=-1, keepdims=True)
        two = jnp.mean(grad * normed, axis=-1, keepdims=True)
        d_hist[rows, :] = (cot[rows, :].astype(F32) + scale * (grad - one - normed * two)).astype(BF16)

    stage4 = []

    def to_sibling(ref):
        i = len(stage4)
        copy = remote(ref, ref, g4s.at[i], g4r.at[i], sib)
        flight.start(copy)
        stage4.append(copy)

    def part_a(kind, head):
        return gp.at[c, :, 0, :, kind_at(kind, head)]

    def part_b(kind, head):
        return gp.at[c, :, 1, :, kind_at(kind, head)]

    def out_row(copies):
        for copy in copies:
            flight.start(copy)
        return copies

    flight.receive(keep_o)
    for copy in stage1[9:]:
        flight.receive(copy)
    ref = go.at[x, z, :, half]
    second_c = out_row([remote(ref, ref, g2s.at[6 + d], g2r.at[6 + d], x_mate(d)) for d in range(1, 4)])

    quarters = {1: pl.ds(0, 4), 3: pl.ds(4, 4)}
    direct, relays = {}, {}

    def third(dj):
        ref = part_a(y_from(dj), x)
        to_sibling(ref)
        direct["a", dj] = {d: remote(ref, ref, g3s.at[dj * 4 + d], g3r.at[dj * 4 + d], x_mate(d)) for d in (1, 3)}
        out_row(direct["a", dj].values())
        ref = part_b(y, x_from(dj))
        to_sibling(ref)
        direct["b", dj] = {d: remote(ref, ref, g3s.at[16 + dj * 4 + d], g3r.at[16 + dj * 4 + d], y_mate(d)) for d in (1, 3)}
        out_row(direct["b", dj].values())

    def pass_on(dj):
        for name in ("a", "b"):
            relays[name, dj] = []
            for d in (1, 3):
                flight.receive(direct[name, dj][d])
                if name == "a":
                    kind, head, row, at, mate = y_from(dj), x_from(d), 0, dj * 4 + d - 1, x_mate(d)
                else:
                    kind, head, row, at, mate = y_from(d), x_from(dj), 1, 16 + dj * 4 + d - 1, y_mate(d)
                ref = gp.at[c, quarters[d], row, :, kind_at(kind, head)]
                relays[name, dj].append(remote(ref, ref, g3s.at[at], g3r.at[at], mate))
                flight.start(relays[name, dj][-1])
            for d in (1, 3):
                to_sibling(part_a(y_from(dj), x_from(d)) if name == "a" else part_b(y_from(d), x_from(dj)))

    def finish(dj):
        for name in ("a", "b"):
            for copy in relays[name, dj]:
                flight.receive(copy)
            to_sibling(part_a(y_from(dj), x_from(2)) if name == "a" else part_b(y_from(2), x_from(dj)))

    flight.receive(keep_p)
    for copy in stage1[2:9]:
        flight.receive(copy)
    ref = part_a(y, x)
    second_a = {d: remote(ref, ref, g2s.at[d], g2r.at[d], y_mate(d)) for d in (2, 1, 3)}
    out_row(second_a.values())
    ref = part_b(y, x)
    second_b = {d: remote(ref, ref, g2s.at[3 + d], g2r.at[3 + d], x_mate(d)) for d in (2, 1, 3)}
    out_row(second_b.values())
    third(0)
    for copy in second_c:
        flight.receive(copy)
    ref = go.at[:, z, :, half]
    last_c = {d: remote(ref, ref, g3s.at[32 + d], g3r.at[32 + d], z_mate(d)) for d in (2, 6, 1, 7)}
    out_row(last_c.values())
    to_sibling(ref)
    for d in (1, 3):
        flight.receive(second_a[d])
        flight.receive(second_b[d])
        third(d)
    pass_on(0)
    flight.receive(second_a[2])
    flight.receive(second_b[2])
    third(2)
    relay_z = []
    for d, near, at in ((2, 1, 4), (6, 7, 0)):
        flight.receive(last_c[d])
        ref = go.at[:, z_from(d), :, half]
        part = go.at[pl.ds(0 if d == 2 else 2, 2), z_from(d), :, half]
        relay_z.append(remote(ref, ref, g3s.at[32 + d + near - (8 if d == 6 else 0)], g3r.at[32 + d + near - (8 if d == 6 else 0)], z_mate(near)))
        relay_z.append(remote(part, part, g3s.at[32 + at], g3r.at[32 + at], z_mate(d)))
        out_row(relay_z[-2:])
        to_sibling(ref)
    pass_on(1)
    pass_on(3)

    pass_on(2)
    for d in (1, 7):
        flight.receive(last_c[d])
        to_sibling(go.at[:, z_from(d), :, half])
    finish(0)
    for copy in relay_z:
        flight.receive(copy)
    for d in (3, 5, 4):
        to_sibling(go.at[:, z_from(d), :, half])
    for dj in (1, 3, 2):
        finish(dj)
    for copy in stage4:
        flight.receive(copy)
    flight.land()


def hand_over(rows_in, gp_in, go_in, rows, gp, go, sems):
    copies = [pltpu.make_async_copy(gp_in.at[s], gp.at[s], sems.at[s]) for s in range(2)]
    copies += [pltpu.make_async_copy(go_in, go, sems.at[2]), pltpu.make_async_copy(rows_in, rows, sems.at[3])]
    for copy in copies:
        copy.start()
    for copy in copies:
        copy.wait()


def on_device(history, cotangent, lengths, w_proj, w_out):
    vmem, dma = pltpu.VMEM, pltpu.SemaphoreType.DMA
    whole = pl.BlockSpec(memory_space=vmem)
    anywhere = pl.BlockSpec(memory_space=pl.ANY)
    scratch = [
        vmem((ROWS, D), BF16),
        vmem((ROWS, D), BF16),
        vmem((EVENTS, D), BF16),
        vmem((EVENTS, D), BF16),
        vmem((EVENTS, D), BF16),
        vmem((D, 2048), BF16),
        vmem((512, D), BF16),
        vmem((512, D), BF16),
        vmem((512, ROWS), BF16),
        vmem((8, 128), jnp.int32),
        vmem((8, 128), jnp.int32),
        vmem((512, EVENTS), BF16),
        vmem((512, EVENTS), F32),
        vmem((EVENTS, HD), BF16),
        vmem((EVENTS, HD), BF16),
        vmem((EVENTS, EVENTS), BF16),
        vmem((EVENTS, EVENTS), F32),
        vmem((HD, EVENTS), F32),
        vmem((HD, EVENTS), BF16),
        vmem((8, EVENTS), F32),
        vmem((4, 8, EVENTS), F32),
        vmem((HD, EVENTS), BF16),
        vmem((HD, EVENTS), BF16),
        vmem((HD, EVENTS), F32),
        vmem((HD, EVENTS), F32),
        vmem((4, HD, EVENTS), BF16),
        vmem((4, 4, HD, ROWS), BF16),
        vmem((4, 8, 64, HD), BF16),
        vmem((4, 8, 16, HD), BF16),
        vmem((4, 8, 64, HD), BF16),
        vmem((4, 8, 16, HD), BF16),
        vmem((8, 80, HD), BF16),
        vmem((8, 80, HD), BF16),
        vmem((2, 32, HD), BF16),
        vmem((16, HD), BF16),
        vmem((ROWS, D), F32),
        pltpu.SemaphoreType.REGULAR((3,)), dma((4,)), dma((8,)), dma((2,)), dma((2,)), dma, dma, dma((2,)), dma((4,)),
        dma((4,)), dma((4,)), dma((4,)), dma((4,)), dma((4,)), dma((4,)), dma((4,)), dma((4,)), dma((4,)), dma((4,)),
        dma((8,)), dma((8,)), dma, dma((8,)), dma((8,)), dma((8,)), dma((8,)),
        dma((2,)), dma((11,)), dma((11,)), dma((10,)), dma((10,)), dma((40,)), dma((40,)), dma((40,)), dma((40,)),
    ]
    shapes = (
        jax.ShapeDtypeStruct((ROWS, D), BF16),
        jax.ShapeDtypeStruct((2, 8, 2, 32, 2048), BF16),
        jax.ShapeDtypeStruct((4, 8, 16, 1024), BF16),
    )
    results = pl.pallas_call(
        kernel,
        out_shape=shapes,
        in_specs=[anywhere, anywhere, whole, anywhere, anywhere],
        out_specs=(whole, anywhere, anywhere),
        scratch_shapes=scratch,
        compiler_params=pltpu.CompilerParams(
            collective_id=0, has_side_effects=True, vmem_limit_bytes=47 * 2**20
        ),
        name="layer",
    )(history[0], cotangent[0], lengths, w_proj, w_out)
    d_rows, grad_p, grad_o = pl.pallas_call(
        hand_over,
        out_shape=shapes,
        in_specs=[anywhere] * 3,
        out_specs=(anywhere,) * 3,
        scratch_shapes=[dma((4,))],
        compiler_params=pltpu.CompilerParams(vmem_limit_bytes=4 * 2**20),
        name="hand_over",
    )(*results)
    return d_rows[None], grad_p.reshape(1024, 2048), grad_o.reshape(512, 1024)


def solution(mesh):
    in_specs = (P("dp", "ctx", None), P("dp", "ctx", None), P("dp", None), P(), P())
    out_specs = (P("dp", "ctx", None), P(), P())
    return jax.shard_map(
        on_device, mesh=mesh, in_specs=in_specs, out_specs=out_specs, check_vma=False
    )
```

```python
import jax
import jax.numpy as jnp
from jax import lax
from jax.experimental import pallas as pl
from jax.experimental.pallas import tpu as pltpu
from jax.sharding import PartitionSpec as P

F32, BF16 = jnp.float32, jnp.bfloat16
MESH = pl.DeviceIdType.MESH
EPSILON = 1e-05
D = 1024
EVENTS = 1024
HD = 128
ROWS = 128
PAIR = 256
SCALE = HD ** (-0.5)
NT = (((1,), (1,)), ((), ()))


def dot(a, b):
    return jnp.dot(a, b, preferred_element_type=F32)


def dot_nt(a, b):
    return lax.dot_general(a, b, NT, preferred_element_type=F32)


def sigmoid(z):
    return 0.5 * jnp.tanh(0.5 * z) + 0.5


def device(x, yh, yl, z, c):
    return ((yl * 8 + z) * 2 + c, x * 2 + yh)


def remote(src, dst, send, recv, target):
    return pltpu.make_async_remote_copy(
        src_ref=src,
        dst_ref=dst,
        send_sem=send,
        recv_sem=recv,
        device_id=target,
        device_id_type=MESH,
    )


class Flight:
    def __init__(self):
        self.unsent, self.unreceived = [], []

    @staticmethod
    def do(action, when):
        if when is None:
            action()
        else:
            pl.when(when)(action)

    def start(self, copy, when=None, mirrored=True):
        self.do(copy.start, when)
        self.unsent.append((copy.wait_send, when))
        if mirrored:
            self.expect(copy, copy.wait_recv, when)

    def start_local(self, copy, when=None):
        self.do(copy.start, when)
        self.expect(copy, copy.wait, when)

    def expect(self, copy, wait, when=None):
        self.unreceived.append((copy, wait, when))

    def receive(self, copy):
        (entry,) = [e for e in self.unreceived if e[0] is copy]
        self.unreceived = [e for e in self.unreceived if e[0] is not copy]
        self.do(entry[1], entry[2])

    def land(self):
        for entry in list(self.unreceived):
            self.receive(entry[0])
        for wait, when in self.unsent:
            self.do(wait, when)


def kernel(
    hist_in, cot_in, lens, w_proj, w_out, d_hist, gp, go,
    hist, cot, xg, cg, xn, wp, wht, wo, dgs, lown, lsib, projt, spt, kr, vr, wm, sm, attnt, dgt, st, stx,
    gt, dat, dlm, dpt, dpr, pay, payo, ybuf, yobuf, zsend, zbuf, piece_p, piece_o, dn,
    known, dgsem, dgrsem, dgfsem, insem, wsem, osem, lsem, swsem, xsem, xrsem, fsem, frsem, csem, crsem, gsem, grsem, stsem, strsem,
    asem, arsem, asem0, ysem, yrsem, zsem, zrsem, g0, g1s, g1r, g2s, g2r, g3s, g3r, g4s, g4r,
):
    dp, ctx = lax.axis_index("dp"), lax.axis_index("ctx")
    c, z, yl = lax.rem(dp, 2), lax.rem(dp // 2, 8), dp // 16
    x, yh = ctx // 2, lax.rem(ctx, 2)
    y = yh * 2 + yl
    sib = device(x, yh, yl, z, 1 - c)

    def x_mate(d):
        return device(lax.rem(x + d, 4), yh, yl, z, c)

    def y_mate(d):
        other = lax.rem(y + d, 4)
        return device(x, other // 2, lax.rem(other, 2), z, c)

    def z_mate(d):
        return device(x, yh, yl, lax.rem(z + d, 8), c)

    def x_from(d):
        return lax.rem(x + 4 - d, 4)

    def y_from(d):
        return lax.rem(y + 4 - d, 4)

    def z_from(d):
        return lax.rem(z + 8 - d, 8)

    here = c == yh
    away = jnp.logical_not(here)
    flight = Flight()

    get_w = pltpu.make_async_copy(w_proj, wp, wsem)
    get_o = pltpu.make_async_copy(w_out, wo, osem)
    get_x = pltpu.make_async_copy(hist_in, hist, insem.at[0])
    get_c = pltpu.make_async_copy(cot_in, cot, insem.at[1])
    flight.start_local(get_x)
    flight.start_local(get_c)
    flight.start_local(get_o)
    flight.start_local(get_w)

    barrier = pltpu.get_barrier_semaphore()
    swap = device(x, 1 - yh, yl, z, 1 - c)
    near = [sib, swap] + [x_mate(d) for d in range(1, 4)] + [y_mate(d) for d in range(1, 4)] + [z_mate(1), z_mate(7)]
    for mate in near:
        pl.semaphore_signal(barrier, inc=1, device_id=mate, device_id_type=MESH)

    def tell(level):
        for mate in (sib, swap, y_mate(2), z_mate(1), z_mate(7)):
            pl.semaphore_signal(known.at[level], inc=1, device_id=mate, device_id_type=MESH)

    def hear(level):
        pl.semaphore_wait(known.at[level], 5)

    lane = lax.broadcasted_iota(jnp.int32, (8, 128), 1)
    first = jnp.broadcast_to(lens[0:1, 0:1], (8, 128))
    second = first + jnp.broadcast_to(lens[0:1, 1:2], (8, 128))
    lown[...] = jnp.where(lane == 0, first, jnp.where(lane == 1, second, 0))

    pl.semaphore_wait(barrier, len(near))
    tell(0)

    slot = pl.ds(pl.multiple_of((2 * x + c) * ROWS, ROWS), ROWS)
    over = pl.ds(pl.multiple_of((2 * x + 1 - c) * ROWS, ROWS), ROWS)
    swap_x = remote(hist, xg.at[over, :], swsem.at[0], swsem.at[1], swap)
    swap_c = remote(cot, cg.at[over, :], swsem.at[2], swsem.at[3], swap)
    flight.receive(get_x)
    flight.start(swap_x, away)
    send_l = remote(lown, lsib, lsem.at[0], lsem.at[1], sib)
    flight.start(send_l)

    @pl.when(here)
    def _():
        xg[slot, :] = hist[...]

    def block_of(d, core):
        return pl.ds(pl.multiple_of((2 * x_from(d) + core) * ROWS, ROWS), ROWS)

    def half_of(d, part):
        return pl.ds(pl.multiple_of((2 * x_from(d) + c) * ROWS + part * (ROWS // 2), ROWS // 2), ROWS // 2)

    push_x = {d: remote(xg.at[slot, :], xg.at[slot, :], xsem.at[d], xrsem.at[d], x_mate(d)) for d in (1, 3)}
    push_c = {d: remote(cg.at[slot, :], cg.at[slot, :], csem.at[d], crsem.at[d], x_mate(d)) for d in (1, 3)}

    def relay(ref, sends, receives, d):
        part = half_of(d, d // 2)
        return remote(ref.at[part, :], ref.at[part, :], sends.at[d - 1], receives.at[d - 1], x_mate(d))

    relay_x = {d: relay(xg, xsem, xrsem, d) for d in (1, 3)}
    relay_c = {d: relay(cg, csem, crsem, d) for d in (1, 3)}
    pass_x = [remote(xg.at[block_of(d, c), :], xg.at[block_of(d, c), :], fsem.at[d], frsem.at[d], sib) for d in range(4)]
    half = pl.ds(pl.multiple_of(c * 512, 512), 512)
    rest = pl.ds(pl.multiple_of(512 - c * 512, 512), 512)
    pass_c = [remote(cg.at[block_of(d, c), rest], cg.at[block_of(d, c), rest], gsem.at[d], grsem.at[d], sib) for d in range(4)]
    far_x = remote(hist, xg.at[over, :], xsem.at[0], xrsem.at[0], device(lax.rem(x + 2, 4), 1 - yh, yl, z, 1 - c))

    def first_pushes(when):
        for copy in (push_x[1], push_x[3], pass_x[0]):
            flight.start(copy, when, mirrored=False)

    arrived_x = {}
    for when, name in ((here, "here"), (away, "away")):
        for d in (1, 3):
            arrived_x[name, d] = object()
            flight.expect(arrived_x[name, d], push_x[d].wait_recv, when)
    flight.expect(pass_x[0], pass_x[0].wait_recv)
    first_pushes(here)

    flight.receive(get_w)
    for j in range(4):
        columns = pl.ds(pl.multiple_of(j * 512 + x * HD, HD), HD)
        wht[j * HD : (j + 1) * HD, :] = wp[:, columns].T

    flight.receive(get_c)
    flight.receive(get_o)
    for i in range(2):
        dgs[i * PAIR : (i + 1) * PAIR, :] = dot_nt(wo[i * PAIR : (i + 1) * PAIR, :], cot[...]).astype(BF16)
    hear(0)
    tell(1)
    flight.start(far_x, away)
    at_block = pl.ds(pl.multiple_of((2 * x + yh) * ROWS, ROWS), ROWS)
    for d in range(4):
        head = lax.rem(x + d, 4)
        source = dgs.at[pl.ds(pl.multiple_of(head * HD, HD), HD), :]
        copy = remote(source, dgt.at[:, at_block], dgsem.at[d], dgrsem.at[d * 2 + yh], device(head, c, yl, z, c))
        flight.start(copy, None if d else away, mirrored=False)

    @pl.when(here)
    def _():
        dgt[:, at_block] = dgs[pl.ds(pl.multiple_of(x * HD, HD), HD), :]

    graded = []
    for d in range(4):
        for row in range(2):
            place = dgt.at[:, pl.ds(pl.multiple_of((2 * x_from(d) + row) * ROWS, ROWS), ROWS)]
            copy = remote(place, place, dgsem.at[0], dgrsem.at[d * 2 + row], sib)
            flight.expect(copy, copy.wait_recv, here if d else here & (yh != row))
            graded.append(copy)
    pass_g = remote(dgt, dgt, dgfsem.at[0], dgfsem.at[1], sib)

    def project(d):
        base = x_from(d) * PAIR

        @pl.loop(0, PAIR // 16, unroll=8)
        def _(i):
            rows = pl.ds(pl.multiple_of(base + i * 16, 16), 16)
            values = xg[rows, :].astype(F32)
            centred = values - jnp.mean(values, axis=-1, keepdims=True)
            variance = jnp.mean(centred * centred, axis=-1, keepdims=True)
            xn[rows, :] = (centred * lax.rsqrt(variance + EPSILON)).astype(BF16)

        rows = pl.ds(pl.multiple_of(base, PAIR), PAIR)
        normed = xn[rows, :]
        pres = dot_nt(wht[...], normed)
        for j in range(4):
            pre = pres[j * HD : (j + 1) * HD]
            s = sigmoid(pre)
            value = pre * s
            spt[j * HD : (j + 1) * HD, rows] = s + value * (1.0 - s)
            value = value.astype(BF16)
            projt[j * HD : (j + 1) * HD, rows] = value
            if j == 1:
                vr[rows, :] = value.T
            if j == 3:
                kr[rows, :] = value.T

    flight.receive(swap_x)
    first_pushes(away)
    flight.start(swap_c, away)
    for d in (1, 3):
        flight.receive(arrived_x["here", d])
        flight.start(relay_x[d], here)
        flight.start(pass_x[d], here, mirrored=False)
    flight.receive(pass_x[0])
    project(0)
    for d in (1, 3):
        flight.receive(arrived_x["away", d])
        flight.start(pass_x[d], away, mirrored=False)
        flight.expect(pass_x[d], pass_x[d].wait_recv)
    hear(1)
    tell(2)
    for d in (1, 3):
        flight.receive(pass_x[d])
        project(d)
    flight.receive(far_x)
    for d in (1, 3):
        flight.receive(relay_x[d])
    flight.start(pass_x[2])
    flight.receive(swap_c)

    @pl.when(here)
    def _():
        cg[slot, :] = cot[...]

    for d in (1, 3):
        flight.start(push_c[d])
    flight.start(pass_c[0])
    flight.receive(pass_x[2])
    project(2)

    hear(2)
    flight.receive(send_l)
    ends = jnp.where(here, lown[...], lsib[...])
    first, second = ends[0:1, 0:1], ends[0:1, 1:2]

    for pb in range(4):
        cols = slice(pb * PAIR, (pb + 1) * PAIR)
        q = projt[2 * HD : 3 * HD, cols]
        p_at = lax.broadcasted_iota(jnp.int32, (1, PAIR), 1) + pb * PAIR
        p_end = jnp.where(p_at < first, first, jnp.where(p_at < second, second, EVENTS))
        total = None
        for rb in range(pb, 4):
            rows = slice(rb * PAIR, (rb + 1) * PAIR)
            logits = dot(kr[rows, :], q) * SCALE
            s = sigmoid(logits)
            weight = logits * s
            slope = s + weight * (1.0 - s)
            r_at = lax.broadcasted_iota(jnp.int32, (PAIR, PAIR), 0) + rb * PAIR
            allowed = (r_at >= p_at) & (r_at < p_end)
            weight = jnp.where(allowed, weight, 0.0).astype(BF16)
            wm[rows, cols] = weight
            sm[rows, cols] = jnp.where(allowed, slope, 0.0)
            term = dot(projt[HD : 2 * HD, rows], weight)
            total = term if total is None else total + term
        attnt[:, cols] = total

    for copy in graded:
        flight.receive(copy)
    flight.start(pass_g, here, mirrored=False)
    flight.expect(pass_g, pass_g.wait_recv, away)
    flight.receive(pass_g)
    st[4:8, :] = jnp.zeros((4, EVENTS), F32)
    for pb in range(4):
        cols = slice(pb * PAIR, (pb + 1) * PAIR)
        d_gated = dgt[:, cols].astype(F32)
        attn = attnt[:, cols]
        g = d_gated * projt[0:HD, cols].astype(F32)
        average = jnp.mean(attn, axis=0, keepdims=True)
        centred = attn - average
        st[0:1, cols] = average
        st[1:2, cols] = jnp.sum(centred * centred, axis=0, keepdims=True)
        st[2:3, cols] = jnp.sum(g, axis=0, keepdims=True)
        st[3:4, cols] = jnp.sum(g * centred, axis=0, keepdims=True)

    push_s = [remote(st, stx.at[d], stsem.at[d], strsem.at[d], x_mate(d)) for d in (2, 1, 3)]
    for copy in push_s:
        flight.start(copy)
    for copy in push_s:
        flight.receive(copy)
    for d in (1, 3):
        flight.receive(push_c[d])
        flight.start(relay_c[d])
        flight.start(pass_c[d])
    parts = [st[...]] + [stx[d] for d in range(1, 4)]
    average = (parts[0][0:1] + parts[1][0:1] + parts[2][0:1] + parts[3][0:1]) * 0.25
    spread = sum(p[1:2] + HD * (p[0:1] - average) ** 2 for p in parts) * (1.0 / 512)
    a_scale = lax.rsqrt(spread + EPSILON)
    g_mean = sum(p[2:3] for p in parts) * (1.0 / 512)
    ga_mean = a_scale * (sum(p[3:4] + (p[0:1] - average) * p[2:3] for p in parts) * (1.0 / 512))

    for pb in range(4):
        cols = slice(pb * PAIR, (pb + 1) * PAIR)
        u = projt[0:HD, cols].astype(F32)
        d_gated = dgt[:, cols].astype(F32)
        scale = a_scale[:, cols]
        a_norm = (attnt[:, cols] - average[:, cols]) * scale
        gt[:, cols] = (a_norm * u).astype(BF16)
        dpt[0, :, cols] = (d_gated * a_norm * spt[0:HD, cols]).astype(BF16)
        dat[:, cols] = (scale * (d_gated * u - g_mean[:, cols] - a_norm * ga_mean[:, cols])).astype(BF16)

    for pb in range(4):
        cols = slice(pb * PAIR, (pb + 1) * PAIR)
        da = dat[:, cols]
        for rb in range(pb, 4):
            rows = slice(rb * PAIR, (rb + 1) * PAIR)
            dlm[rows, cols] = (dot(vr[rows, :], da) * sm[rows, cols]).astype(BF16)
        after = slice(pb * PAIR, EVENTS)
        d_query = dot(projt[3 * HD : 4 * HD, after], dlm[after, cols])
        dpt[2, :, cols] = (d_query * SCALE * spt[2 * HD : 3 * HD, cols]).astype(BF16)
    for rb in range(4):
        rows = slice(rb * PAIR, (rb + 1) * PAIR)
        before = slice(0, (rb + 1) * PAIR)
        d_value = dot_nt(dat[:, before], wm[rows, before])
        d_key = dot_nt(projt[2 * HD : 3 * HD, before], dlm[rows, before])
        dpt[1, :, rows] = (d_value * spt[HD : 2 * HD, rows]).astype(BF16)
        dpt[3, :, rows] = (d_key * SCALE * spt[3 * HD : 4 * HD, rows]).astype(BF16)

    push_y = []
    for d in (2, 1, 3, 0):
        j = lax.rem(y + d, 4)
        pay[j] = dot(dpt[j], xn[:, half]).T.astype(BF16).reshape(8, 64, HD)
        if d:
            push_y.append(remote(pay.at[j], ybuf.at[d], ysem.at[d], yrsem.at[d], y_mate(d)))
            flight.start(push_y[-1])
    for d in (1, 3):
        flight.receive(relay_c[d])
    flight.start(pass_c[2])
    for d in range(4):
        flight.receive(pass_c[d])
    grad_o = dot(gt[...], cg[:, half]).astype(BF16)
    for j in range(4):
        payo[j] = grad_o[:, j * HD : (j + 1) * HD].reshape(8, 16, HD)
    push_o = []
    for d in (2, 1, 3):
        push_o.append(remote(payo.at[lax.rem(y + d, 4)], yobuf.at[d], ysem.at[3 + d], yrsem.at[3 + d], y_mate(d)))
        flight.start(push_o[-1])
    for copy in push_y + push_o:
        flight.receive(copy)
    zsend[:, 0:64, :] = (
        pay[y].astype(F32) + ybuf[1].astype(F32) + ybuf[2].astype(F32) + ybuf[3].astype(F32)
    ).astype(BF16)
    zsend[:, 64:80, :] = (
        payo[y].astype(F32) + yobuf[1].astype(F32) + yobuf[2].astype(F32) + yobuf[3].astype(F32)
    ).astype(BF16)
    push_z = []
    for d in (4, 3, 5, 2, 6, 1, 7):
        copy = remote(zsend.at[lax.rem(z + d, 8)], zbuf.at[d], zsem.at[d], zrsem.at[d], z_mate(d))
        flight.start(copy)
        push_z.append(copy)
    mine = pl.ds(2 * c, 2)
    for dx in range(4):
        for dy in range(2):
            tx, ty = lax.rem(x + dx, 4), lax.rem(yh + dy, 2)
            lanes = pl.ds(pl.multiple_of((tx * 2 + ty) * ROWS, ROWS), ROWS)
            source, place = dpt.at[mine, :, lanes], dpr.at[mine, x]
            copy = remote(source, place, asem.at[dx * 2 + dy], arsem.at[dx * 2 + c], device(tx, ty, yl, z, yh))
            if dx or dy:
                flight.start(copy, mirrored=False)
            else:
                flight.start(copy, away, mirrored=False)
                keep = pltpu.make_async_copy(source, place, asem0)
                flight.start_local(keep, here)
    arrivals = [keep]
    for dx in range(4):
        for core in range(2):
            place = dpr.at[pl.ds(2 * core, 2), x_from(dx)]
            copy = remote(place, place, asem.at[0], arsem.at[dx * 2 + core], sib)
            flight.expect(copy, copy.wait_recv, None if dx else jnp.logical_not(here & (c == core)))
            arrivals.append(copy)

    for copy in push_z:
        flight.receive(copy)
    total = zsend[z].astype(F32)
    for d in range(1, 8):
        total = total + zbuf[d].astype(F32)
    total = total.astype(BF16)
    piece_p[...] = total[0:64].reshape(2, 32, HD)
    piece_o[...] = total[64:80]

    def kind_at(j, head):
        return pl.ds(pl.multiple_of(j * 512 + head * HD, HD), HD)

    own_p = gp.at[c, z, :, :, kind_at(y, x)]
    own_o = go.at[x, z, :, pl.ds(pl.multiple_of(c * 512 + y * HD, HD), HD)]
    keep_p = pltpu.make_async_copy(piece_p, own_p, g0.at[0])
    keep_o = pltpu.make_async_copy(piece_o, own_o, g0.at[1])
    stage1 = [keep_p, keep_o]
    for d in (4, 3, 5, 2, 6, 1, 7):
        stage1.append(remote(piece_p, own_p, g1s.at[d], g1r.at[d], z_mate(d)))
    for d in (2, 1, 3):
        stage1.append(remote(piece_o, own_o, g1s.at[7 + d], g1r.at[7 + d], y_mate(d)))
    flight.start_local(keep_p)
    flight.start_local(keep_o)
    for copy in stage1[2:]:
        flight.start(copy)

    stage4 = []

    def to_sibling(ref):
        i = len(stage4)
        copy = remote(ref, ref, g4s.at[i], g4r.at[i], sib)
        flight.start(copy)
        stage4.append(copy)

    def part_a(kind, head):
        return gp.at[c, :, 0, :, kind_at(kind, head)]

    def part_b(kind, head):
        return gp.at[c, :, 1, :, kind_at(kind, head)]

    def out_row(copies):
        for copy in copies:
            flight.start(copy)
        return copies

    flight.receive(keep_o)
    for copy in stage1[9:]:
        flight.receive(copy)
    ref = go.at[x, z, :, half]
    second_c = out_row([remote(ref, ref, g2s.at[6 + d], g2r.at[6 + d], x_mate(d)) for d in range(1, 4)])

    quarters = {1: pl.ds(0, 4), 3: pl.ds(4, 4)}
    direct, relays = {}, {}

    def third(dj):
        ref = part_a(y_from(dj), x)
        to_sibling(ref)
        direct["a", dj] = {d: remote(ref, ref, g3s.at[dj * 4 + d], g3r.at[dj * 4 + d], x_mate(d)) for d in (1, 3)}
        out_row(direct["a", dj].values())
        ref = part_b(y, x_from(dj))
        to_sibling(ref)
        direct["b", dj] = {d: remote(ref, ref, g3s.at[16 + dj * 4 + d], g3r.at[16 + dj * 4 + d], y_mate(d)) for d in (1, 3)}
        out_row(direct["b", dj].values())

    def pass_on(dj):
        for name in ("a", "b"):
            relays[name, dj] = []
            for d in (1, 3):
                flight.receive(direct[name, dj][d])
                if name == "a":
                    kind, head, row, at, mate = y_from(dj), x_from(d), 0, dj * 4 + d - 1, x_mate(d)
                else:
                    kind, head, row, at, mate = y_from(d), x_from(dj), 1, 16 + dj * 4 + d - 1, y_mate(d)
                ref = gp.at[c, quarters[d], row, :, kind_at(kind, head)]
                relays[name, dj].append(remote(ref, ref, g3s.at[at], g3r.at[at], mate))
                flight.start(relays[name, dj][-1])
            for d in (1, 3):
                to_sibling(part_a(y_from(dj), x_from(d)) if name == "a" else part_b(y_from(d), x_from(dj)))

    def finish(dj):
        for name in ("a", "b"):
            for copy in relays[name, dj]:
                flight.receive(copy)
            to_sibling(part_a(y_from(dj), x_from(2)) if name == "a" else part_b(y_from(2), x_from(dj)))

    flight.receive(keep_p)
    for copy in stage1[2:9]:
        flight.receive(copy)
    ref = part_a(y, x)
    second_a = {d: remote(ref, ref, g2s.at[d], g2r.at[d], y_mate(d)) for d in (2, 1, 3)}
    out_row(second_a.values())
    ref = part_b(y, x)
    second_b = {d: remote(ref, ref, g2s.at[3 + d], g2r.at[3 + d], x_mate(d)) for d in (2, 1, 3)}
    out_row(second_b.values())
    third(0)
    for copy in second_c:
        flight.receive(copy)
    ref = go.at[:, z, :, half]
    last_c = {d: remote(ref, ref, g3s.at[32 + d], g3r.at[32 + d], z_mate(d)) for d in (2, 6, 1, 7)}
    out_row(last_c.values())
    to_sibling(ref)
    for d in (1, 3):
        flight.receive(second_a[d])
        flight.receive(second_b[d])
        third(d)
    pass_on(0)
    flight.receive(second_a[2])
    flight.receive(second_b[2])
    third(2)
    relay_z = []
    for d, near, at in ((2, 1, 4), (6, 7, 0)):
        flight.receive(last_c[d])
        ref = go.at[:, z_from(d), :, half]
        part = go.at[pl.ds(0 if d == 2 else 2, 2), z_from(d), :, half]
        relay_z.append(remote(ref, ref, g3s.at[32 + d + near - (8 if d == 6 else 0)], g3r.at[32 + d + near - (8 if d == 6 else 0)], z_mate(near)))
        relay_z.append(remote(part, part, g3s.at[32 + at], g3r.at[32 + at], z_mate(d)))
        out_row(relay_z[-2:])
        to_sibling(ref)
    pass_on(1)
    pass_on(3)

    for copy in arrivals:
        flight.receive(copy)
    columns = dpr[...].reshape(2048, ROWS)
    for i in range(4):
        part = dot(wp[i * 256 : (i + 1) * 256, :], columns)
        dn[:, i * 256 : (i + 1) * 256] = part.T

    pass_on(2)
    @pl.loop(0, ROWS // 16, unroll=2)
    def _(i):
        rows = pl.ds(pl.multiple_of(i * 16, 16), 16)
        values = hist[rows, :].astype(F32)
        centred = values - jnp.mean(values, axis=-1, keepdims=True)
        variance = jnp.mean(centred * centred, axis=-1, keepdims=True)
        scale = lax.rsqrt(variance + EPSILON)
        normed = centred * scale
        grad = dn[rows, :]
        one = jnp.mean(grad, axis=-1, keepdims=True)
        two = jnp.mean(grad * normed, axis=-1, keepdims=True)
        d_hist[rows, :] = (cot[rows, :].astype(F32) + scale * (grad - one - normed * two)).astype(BF16)

    for d in (1, 7):
        flight.receive(last_c[d])
        to_sibling(go.at[:, z_from(d), :, half])
    finish(0)
    for copy in relay_z:
        flight.receive(copy)
    for d in (3, 5, 4):
        to_sibling(go.at[:, z_from(d), :, half])
    for dj in (1, 3, 2):
        finish(dj)
    for copy in stage4:
        flight.receive(copy)
    flight.land()


def hand_over(rows_in, gp_in, go_in, rows, gp, go, sems):
    copies = [pltpu.make_async_copy(gp_in.at[s], gp.at[s], sems.at[s]) for s in range(2)]
    copies += [pltpu.make_async_copy(go_in, go, sems.at[2]), pltpu.make_async_copy(rows_in, rows, sems.at[3])]
    for copy in copies:
        copy.start()
    for copy in copies:
        copy.wait()


def on_device(history, cotangent, lengths, w_proj, w_out):
    vmem, dma = pltpu.VMEM, pltpu.SemaphoreType.DMA
    whole = pl.BlockSpec(memory_space=vmem)
    anywhere = pl.BlockSpec(memory_space=pl.ANY)
    scratch = [
        vmem((ROWS, D), BF16),
        vmem((ROWS, D), BF16),
        vmem((EVENTS, D), BF16),
        vmem((EVENTS, D), BF16),
        vmem((EVENTS, D), BF16),
        vmem((D, 2048), BF16),
        vmem((512, D), BF16),
        vmem((512, D), BF16),
        vmem((512, ROWS), BF16),
        vmem((8, 128), jnp.int32),
        vmem((8, 128), jnp.int32),
        vmem((512, EVENTS), BF16),
        vmem((512, EVENTS), F32),
        vmem((EVENTS, HD), BF16),
        vmem((EVENTS, HD), BF16),
        vmem((EVENTS, EVENTS), BF16),
        vmem((EVENTS, EVENTS), F32),
        vmem((HD, EVENTS), F32),
        vmem((HD, EVENTS), BF16),
        vmem((8, EVENTS), F32),
        vmem((4, 8, EVENTS), F32),
        vmem((HD, EVENTS), BF16),
        vmem((HD, EVENTS), BF16),
        vmem((EVENTS, EVENTS), BF16),
        vmem((4, HD, EVENTS), BF16),
        vmem((4, 4, HD, ROWS), BF16),
        vmem((4, 8, 64, HD), BF16),
        vmem((4, 8, 16, HD), BF16),
        vmem((4, 8, 64, HD), BF16),
        vmem((4, 8, 16, HD), BF16),
        vmem((8, 80, HD), BF16),
        vmem((8, 80, HD), BF16),
        vmem((2, 32, HD), BF16),
        vmem((16, HD), BF16),
        vmem((ROWS, D), F32),
        pltpu.SemaphoreType.REGULAR((3,)), dma((4,)), dma((8,)), dma((2,)), dma((2,)), dma, dma, dma((2,)), dma((4,)),
        dma((4,)), dma((4,)), dma((4,)), dma((4,)), dma((4,)), dma((4,)), dma((4,)), dma((4,)), dma((4,)), dma((4,)),
        dma((8,)), dma((8,)), dma, dma((8,)), dma((8,)), dma((8,)), dma((8,)),
        dma((2,)), dma((11,)), dma((11,)), dma((10,)), dma((10,)), dma((40,)), dma((40,)), dma((40,)), dma((40,)),
    ]
    shapes = (
        jax.ShapeDtypeStruct((ROWS, D), BF16),
        jax.ShapeDtypeStruct((2, 8, 2, 32, 2048), BF16),
        jax.ShapeDtypeStruct((4, 8, 16, 1024), BF16),
    )
    results = pl.pallas_call(
        kernel,
        out_shape=shapes,
        in_specs=[anywhere, anywhere, whole, anywhere, anywhere],
        out_specs=(whole, anywhere, anywhere),
        scratch_shapes=scratch,
        compiler_params=pltpu.CompilerParams(
            collective_id=0, has_side_effects=True, vmem_limit_bytes=47 * 2**20
        ),
        name="layer",
    )(history[0], cotangent[0], lengths, w_proj, w_out)
    d_rows, grad_p, grad_o = pl.pallas_call(
        hand_over,
        out_shape=shapes,
        in_specs=[anywhere] * 3,
        out_specs=(anywhere,) * 3,
        scratch_shapes=[dma((4,))],
        compiler_params=pltpu.CompilerParams(vmem_limit_bytes=4 * 2**20),
        name="hand_over",
    )(*results)
    return d_rows[None], grad_p.reshape(1024, 2048), grad_o.reshape(512, 1024)


def solution(mesh):
    in_specs = (P("dp", "ctx", None), P("dp", "ctx", None), P("dp", None), P(), P())
    out_specs = (P("dp", "ctx", None), P(), P())
    return jax.shard_map(
        on_device, mesh=mesh, in_specs=in_specs, out_specs=out_specs, check_vma=False
    )
```

```python
import jax
import jax.numpy as jnp
from jax import lax
from jax.experimental import pallas as pl
from jax.experimental.pallas import tpu as pltpu
from jax.sharding import PartitionSpec as P

F32, BF16 = jnp.float32, jnp.bfloat16
MESH = pl.DeviceIdType.MESH
EPSILON = 1e-05
D = 1024
EVENTS = 1024
HD = 128
ROWS = 128
PAIR = 256
SCALE = HD ** (-0.5)
NT = (((1,), (1,)), ((), ()))


def dot(a, b):
    return jnp.dot(a, b, preferred_element_type=F32)


def dot_nt(a, b):
    return lax.dot_general(a, b, NT, preferred_element_type=F32)


def sigmoid(z):
    return 0.5 * jnp.tanh(0.5 * z) + 0.5


def device(x, yh, yl, z, c):
    return ((yl * 8 + z) * 2 + c, x * 2 + yh)


def remote(src, dst, send, recv, target):
    return pltpu.make_async_remote_copy(
        src_ref=src,
        dst_ref=dst,
        send_sem=send,
        recv_sem=recv,
        device_id=target,
        device_id_type=MESH,
    )


class Flight:
    def __init__(self):
        self.unsent, self.unreceived = [], []

    @staticmethod
    def do(action, when):
        if when is None:
            action()
        else:
            pl.when(when)(action)

    def start(self, copy, when=None, mirrored=True):
        self.do(copy.start, when)
        self.unsent.append((copy.wait_send, when))
        if mirrored:
            self.expect(copy, copy.wait_recv, when)

    def start_local(self, copy, when=None):
        self.do(copy.start, when)
        self.expect(copy, copy.wait, when)

    def expect(self, copy, wait, when=None):
        self.unreceived.append((copy, wait, when))

    def receive(self, copy):
        (entry,) = [e for e in self.unreceived if e[0] is copy]
        self.unreceived = [e for e in self.unreceived if e[0] is not copy]
        self.do(entry[1], entry[2])

    def land(self):
        for entry in list(self.unreceived):
            self.receive(entry[0])
        for wait, when in self.unsent:
            self.do(wait, when)


def kernel(
    hist_in, cot_in, lens, w_proj, w_out, d_hist, gp, go,
    hist, cot, xg, cg, xn, wp, wht, wo, dgs, lown, lsib, projt, spt, kr, vr, wm, sm, attnt, dgt, st, stx,
    gt, dat, dlm, dpt, dpr, pay, payo, ybuf, yobuf, zsend, zbuf, piece_p, piece_o, dn,
    known, dgsem, dgrsem, dgfsem, insem, wsem, osem, lsem, swsem, xsem, xrsem, fsem, frsem, csem, crsem, gsem, grsem, stsem, strsem,
    asem, arsem, asem0, ysem, yrsem, zsem, zrsem, g0, g1s, g1r, g2s, g2r, g3s, g3r, g4s, g4r,
):
    dp, ctx = lax.axis_index("dp"), lax.axis_index("ctx")
    c, z, yl = lax.rem(dp, 2), lax.rem(dp // 2, 8), dp // 16
    x, yh = ctx // 2, lax.rem(ctx, 2)
    y = yh * 2 + yl
    sib = device(x, yh, yl, z, 1 - c)

    def x_mate(d):
        return device(lax.rem(x + d, 4), yh, yl, z, c)

    def y_mate(d):
        other = lax.rem(y + d, 4)
        return device(x, other // 2, lax.rem(other, 2), z, c)

    def z_mate(d):
        return device(x, yh, yl, lax.rem(z + d, 8), c)

    def x_from(d):
        return lax.rem(x + 4 - d, 4)

    def y_from(d):
        return lax.rem(y + 4 - d, 4)

    def z_from(d):
        return lax.rem(z + 8 - d, 8)

    here = c == yh
    away = jnp.logical_not(here)
    flight = Flight()

    get_w = pltpu.make_async_copy(w_proj, wp, wsem)
    get_o = pltpu.make_async_copy(w_out, wo, osem)
    get_x = pltpu.make_async_copy(hist_in, hist, insem.at[0])
    get_c = pltpu.make_async_copy(cot_in, cot, insem.at[1])
    flight.start_local(get_x)
    flight.start_local(get_c)
    flight.start_local(get_o)
    flight.start_local(get_w)

    barrier = pltpu.get_barrier_semaphore()
    swap = device(x, 1 - yh, yl, z, 1 - c)
    near = [sib, swap] + [x_mate(d) for d in range(1, 4)] + [y_mate(d) for d in range(1, 4)] + [z_mate(1), z_mate(7)]
    for mate in near:
        pl.semaphore_signal(barrier, inc=1, device_id=mate, device_id_type=MESH)

    def tell(level):
        for mate in (sib, swap, y_mate(2), z_mate(1), z_mate(7)):
            pl.semaphore_signal(known.at[level], inc=1, device_id=mate, device_id_type=MESH)

    def hear(level):
        pl.semaphore_wait(known.at[level], 5)

    lane = lax.broadcasted_iota(jnp.int32, (8, 128), 1)
    first = jnp.broadcast_to(lens[0:1, 0:1], (8, 128))
    second = first + jnp.broadcast_to(lens[0:1, 1:2], (8, 128))
    lown[...] = jnp.where(lane == 0, first, jnp.where(lane == 1, second, 0))

    pl.semaphore_wait(barrier, len(near))
    tell(0)

    slot = pl.ds(pl.multiple_of((2 * x + c) * ROWS, ROWS), ROWS)
    over = pl.ds(pl.multiple_of((2 * x + 1 - c) * ROWS, ROWS), ROWS)
    swap_x = remote(hist, xg.at[over, :], swsem.at[0], swsem.at[1], swap)
    swap_c = remote(cot, cg.at[over, :], swsem.at[2], swsem.at[3], swap)
    flight.receive(get_x)
    flight.start(swap_x, away)
    send_l = remote(lown, lsib, lsem.at[0], lsem.at[1], sib)
    flight.start(send_l)

    @pl.when(here)
    def _():
        xg[slot, :] = hist[...]

    def block_of(d, core):
        return pl.ds(pl.multiple_of((2 * x_from(d) + core) * ROWS, ROWS), ROWS)

    def half_of(d, part):
        return pl.ds(pl.multiple_of((2 * x_from(d) + c) * ROWS + part * (ROWS // 2), ROWS // 2), ROWS // 2)

    push_x = {d: remote(xg.at[slot, :], xg.at[slot, :], xsem.at[d], xrsem.at[d], x_mate(d)) for d in (1, 3)}
    push_c = {d: remote(cg.at[slot, :], cg.at[slot, :], csem.at[d], crsem.at[d], x_mate(d)) for d in (1, 3)}

    def relay(ref, sends, receives, d):
        part = half_of(d, d // 2)
        return remote(ref.at[part, :], ref.at[part, :], sends.at[d - 1], receives.at[d - 1], x_mate(d))

    relay_x = {d: relay(xg, xsem, xrsem, d) for d in (1, 3)}
    relay_c = {d: relay(cg, csem, crsem, d) for d in (1, 3)}
    pass_x = [remote(xg.at[block_of(d, c), :], xg.at[block_of(d, c), :], fsem.at[d], frsem.at[d], sib) for d in range(4)]
    half = pl.ds(pl.multiple_of(c * 512, 512), 512)
    rest = pl.ds(pl.multiple_of(512 - c * 512, 512), 512)
    pass_c = [remote(cg.at[block_of(d, c), rest], cg.at[block_of(d, c), rest], gsem.at[d], grsem.at[d], sib) for d in range(4)]
    far_x = remote(hist, xg.at[over, :], xsem.at[0], xrsem.at[0], device(lax.rem(x + 2, 4), 1 - yh, yl, z, 1 - c))

    def first_pushes(when):
        for copy in (push_x[1], push_x[3], pass_x[0]):
            flight.start(copy, when, mirrored=False)

    arrived_x = {}
    for when, name in ((here, "here"), (away, "away")):
        for d in (1, 3):
            arrived_x[name, d] = object()
            flight.expect(arrived_x[name, d], push_x[d].wait_recv, when)
    flight.expect(pass_x[0], pass_x[0].wait_recv)
    first_pushes(here)

    flight.receive(get_w)
    for j in range(4):
        columns = pl.ds(pl.multiple_of(j * 512 + x * HD, HD), HD)
        wht[j * HD : (j + 1) * HD, :] = wp[:, columns].T

    flight.receive(get_c)
    flight.receive(get_o)
    for i in range(2):
        dgs[i * PAIR : (i + 1) * PAIR, :] = dot_nt(wo[i * PAIR : (i + 1) * PAIR, :], cot[...]).astype(BF16)
    hear(0)
    tell(1)
    flight.start(far_x, away)
    at_block = pl.ds(pl.multiple_of((2 * x + yh) * ROWS, ROWS), ROWS)
    for d in range(4):
        head = lax.rem(x + d, 4)
        source = dgs.at[pl.ds(pl.multiple_of(head * HD, HD), HD), :]
        copy = remote(source, dgt.at[:, at_block], dgsem.at[d], dgrsem.at[d * 2 + yh], device(head, c, yl, z, c))
        flight.start(copy, None if d else away, mirrored=False)

    @pl.when(here)
    def _():
        dgt[:, at_block] = dgs[pl.ds(pl.multiple_of(x * HD, HD), HD), :]

    graded = []
    for d in range(4):
        for row in range(2):
            place = dgt.at[:, pl.ds(pl.multiple_of((2 * x_from(d) + row) * ROWS, ROWS), ROWS)]
            copy = remote(place, place, dgsem.at[0], dgrsem.at[d * 2 + row], sib)
            flight.expect(copy, copy.wait_recv, here if d else here & (yh != row))
            graded.append(copy)
    pass_g = remote(dgt, dgt, dgfsem.at[0], dgfsem.at[1], sib)

    def project(d):
        base = x_from(d) * PAIR

        @pl.loop(0, PAIR // 16, unroll=8)
        def _(i):
            rows = pl.ds(pl.multiple_of(base + i * 16, 16), 16)
            values = xg[rows, :].astype(F32)
            centred = values - jnp.mean(values, axis=-1, keepdims=True)
            variance = jnp.mean(centred * centred, axis=-1, keepdims=True)
            xn[rows, :] = (centred * lax.rsqrt(variance + EPSILON)).astype(BF16)

        rows = pl.ds(pl.multiple_of(base, PAIR), PAIR)
        normed = xn[rows, :]
        pres = dot_nt(wht[...], normed)
        for j in range(4):
            pre = pres[j * HD : (j + 1) * HD]
            s = sigmoid(pre)
            value = pre * s
            spt[j * HD : (j + 1) * HD, rows] = s + value * (1.0 - s)
            value = value.astype(BF16)
            projt[j * HD : (j + 1) * HD, rows] = value
            if j == 1:
                vr[rows, :] = value.T
            if j == 3:
                kr[rows, :] = value.T

    flight.receive(swap_x)
    first_pushes(away)
    flight.start(swap_c, away)
    for d in (1, 3):
        flight.receive(arrived_x["here", d])
        flight.start(relay_x[d], here)
        flight.start(pass_x[d], here, mirrored=False)
    flight.receive(pass_x[0])
    project(0)
    for d in (1, 3):
        flight.receive(arrived_x["away", d])
        flight.start(pass_x[d], away, mirrored=False)
        flight.expect(pass_x[d], pass_x[d].wait_recv)
    hear(1)
    tell(2)
    for d in (1, 3):
        flight.receive(pass_x[d])
        project(d)
    flight.receive(far_x)
    for d in (1, 3):
        flight.receive(relay_x[d])
    flight.start(pass_x[2])
    flight.receive(swap_c)

    @pl.when(here)
    def _():
        cg[slot, :] = cot[...]

    for d in (1, 3):
        flight.start(push_c[d])
    flight.start(pass_c[0])
    flight.receive(pass_x[2])
    project(2)

    hear(2)
    flight.receive(send_l)
    ends = jnp.where(here, lown[...], lsib[...])
    first, second = ends[0:1, 0:1], ends[0:1, 1:2]

    for pb in range(4):
        cols = slice(pb * PAIR, (pb + 1) * PAIR)
        q = projt[2 * HD : 3 * HD, cols]
        p_at = lax.broadcasted_iota(jnp.int32, (1, PAIR), 1) + pb * PAIR
        p_end = jnp.where(p_at < first, first, jnp.where(p_at < second, second, EVENTS))
        for rb in range(pb, 4):
            rows = slice(rb * PAIR, (rb + 1) * PAIR)
            logits = dot(kr[rows, :], q) * SCALE
            s = sigmoid(logits)
            weight = logits * s
            slope = s + weight * (1.0 - s)
            r_at = lax.broadcasted_iota(jnp.int32, (PAIR, PAIR), 0) + rb * PAIR
            allowed = (r_at >= p_at) & (r_at < p_end)
            weight = jnp.where(allowed, weight, 0.0).astype(BF16)
            wm[rows, cols] = weight
            sm[rows, cols] = jnp.where(allowed, slope, 0.0)
        after = slice(pb * PAIR, EVENTS)
        attnt[:, cols] = dot(projt[HD : 2 * HD, after], wm[after, cols])

    for copy in graded:
        flight.receive(copy)
    flight.start(pass_g, here, mirrored=False)
    flight.expect(pass_g, pass_g.wait_recv, away)
    flight.receive(pass_g)
    st[4:8, :] = jnp.zeros((4, EVENTS), F32)
    for pb in range(4):
        cols = slice(pb * PAIR, (pb + 1) * PAIR)
        d_gated = dgt[:, cols].astype(F32)
        attn = attnt[:, cols]
        g = d_gated * projt[0:HD, cols].astype(F32)
        average = jnp.mean(attn, axis=0, keepdims=True)
        centred = attn - average
        st[0:1, cols] = average
        st[1:2, cols] = jnp.sum(centred * centred, axis=0, keepdims=True)
        st[2:3, cols] = jnp.sum(g, axis=0, keepdims=True)
        st[3:4, cols] = jnp.sum(g * centred, axis=0, keepdims=True)

    push_s = [remote(st, stx.at[d], stsem.at[d], strsem.at[d], x_mate(d)) for d in (2, 1, 3)]
    for copy in push_s:
        flight.start(copy)
    for copy in push_s:
        flight.receive(copy)
    for d in (1, 3):
        flight.receive(push_c[d])
        flight.start(relay_c[d])
        flight.start(pass_c[d])
    parts = [st[...]] + [stx[d] for d in range(1, 4)]
    average = (parts[0][0:1] + parts[1][0:1] + parts[2][0:1] + parts[3][0:1]) * 0.25
    spread = sum(p[1:2] + HD * (p[0:1] - average) ** 2 for p in parts) * (1.0 / 512)
    a_scale = lax.rsqrt(spread + EPSILON)
    g_mean = sum(p[2:3] for p in parts) * (1.0 / 512)
    ga_mean = a_scale * (sum(p[3:4] + (p[0:1] - average) * p[2:3] for p in parts) * (1.0 / 512))

    for pb in range(4):
        cols = slice(pb * PAIR, (pb + 1) * PAIR)
        u = projt[0:HD, cols].astype(F32)
        d_gated = dgt[:, cols].astype(F32)
        scale = a_scale[:, cols]
        a_norm = (attnt[:, cols] - average[:, cols]) * scale
        gt[:, cols] = (a_norm * u).astype(BF16)
        dpt[0, :, cols] = (d_gated * a_norm * spt[0:HD, cols]).astype(BF16)
        dat[:, cols] = (scale * (d_gated * u - g_mean[:, cols] - a_norm * ga_mean[:, cols])).astype(BF16)

    for pb in range(4):
        cols = slice(pb * PAIR, (pb + 1) * PAIR)
        da = dat[:, cols]
        for rb in range(pb, 4):
            rows = slice(rb * PAIR, (rb + 1) * PAIR)
            dlm[rows, cols] = (dot(vr[rows, :], da) * sm[rows, cols]).astype(BF16)
        after = slice(pb * PAIR, EVENTS)
        d_query = dot(projt[3 * HD : 4 * HD, after], dlm[after, cols])
        dpt[2, :, cols] = (d_query * SCALE * spt[2 * HD : 3 * HD, cols]).astype(BF16)
    for rb in range(4):
        rows = slice(rb * PAIR, (rb + 1) * PAIR)
        before = slice(0, (rb + 1) * PAIR)
        d_value = dot_nt(dat[:, before], wm[rows, before])
        d_key = dot_nt(projt[2 * HD : 3 * HD, before], dlm[rows, before])
        dpt[1, :, rows] = (d_value * spt[HD : 2 * HD, rows]).astype(BF16)
        dpt[3, :, rows] = (d_key * SCALE * spt[3 * HD : 4 * HD, rows]).astype(BF16)

    push_y = []
    for d in (2, 1, 3, 0):
        j = lax.rem(y + d, 4)
        pay[j] = dot(dpt[j], xn[:, half]).T.astype(BF16).reshape(8, 64, HD)
        if d:
            push_y.append(remote(pay.at[j], ybuf.at[d], ysem.at[d], yrsem.at[d], y_mate(d)))
            flight.start(push_y[-1])
    for d in (1, 3):
        flight.receive(relay_c[d])
    flight.start(pass_c[2])
    for d in range(4):
        flight.receive(pass_c[d])
    grad_o = dot(gt[...], cg[:, half]).astype(BF16)
    for j in range(4):
        payo[j] = grad_o[:, j * HD : (j + 1) * HD].reshape(8, 16, HD)
    push_o = []
    for d in (2, 1, 3):
        push_o.append(remote(payo.at[lax.rem(y + d, 4)], yobuf.at[d], ysem.at[3 + d], yrsem.at[3 + d], y_mate(d)))
        flight.start(push_o[-1])
    for copy in push_y + push_o:
        flight.receive(copy)
    zsend[:, 0:64, :] = (
        pay[y].astype(F32) + ybuf[1].astype(F32) + ybuf[2].astype(F32) + ybuf[3].astype(F32)
    ).astype(BF16)
    zsend[:, 64:80, :] = (
        payo[y].astype(F32) + yobuf[1].astype(F32) + yobuf[2].astype(F32) + yobuf[3].astype(F32)
    ).astype(BF16)
    push_z = []
    for d in (4, 3, 5, 2, 6, 1, 7):
        copy = remote(zsend.at[lax.rem(z + d, 8)], zbuf.at[d], zsem.at[d], zrsem.at[d], z_mate(d))
        flight.start(copy)
        push_z.append(copy)
    mine = pl.ds(2 * c, 2)
    for dx in range(4):
        for dy in range(2):
            tx, ty = lax.rem(x + dx, 4), lax.rem(yh + dy, 2)
            lanes = pl.ds(pl.multiple_of((tx * 2 + ty) * ROWS, ROWS), ROWS)
            source, place = dpt.at[mine, :, lanes], dpr.at[mine, x]
            copy = remote(source, place, asem.at[dx * 2 + dy], arsem.at[dx * 2 + c], device(tx, ty, yl, z, yh))
            if dx or dy:
                flight.start(copy, mirrored=False)
            else:
                flight.start(copy, away, mirrored=False)
                keep = pltpu.make_async_copy(source, place, asem0)
                flight.start_local(keep, here)
    arrivals = [keep]
    for dx in range(4):
        for core in range(2):
            place = dpr.at[pl.ds(2 * core, 2), x_from(dx)]
            copy = remote(place, place, asem.at[0], arsem.at[dx * 2 + core], sib)
            flight.expect(copy, copy.wait_recv, None if dx else jnp.logical_not(here & (c == core)))
            arrivals.append(copy)

    for copy in push_z:
        flight.receive(copy)
    total = zsend[z].astype(F32)
    for d in range(1, 8):
        total = total + zbuf[d].astype(F32)
    total = total.astype(BF16)
    piece_p[...] = total[0:64].reshape(2, 32, HD)
    piece_o[...] = total[64:80]

    def kind_at(j, head):
        return pl.ds(pl.multiple_of(j * 512 + head * HD, HD), HD)

    own_p = gp.at[c, z, :, :, kind_at(y, x)]
    own_o = go.at[x, z, :, pl.ds(pl.multiple_of(c * 512 + y * HD, HD), HD)]
    keep_p = pltpu.make_async_copy(piece_p, own_p, g0.at[0])
    keep_o = pltpu.make_async_copy(piece_o, own_o, g0.at[1])
    stage1 = [keep_p, keep_o]
    for d in (4, 3, 5, 2, 6, 1, 7):
        stage1.append(remote(piece_p, own_p, g1s.at[d], g1r.at[d], z_mate(d)))
    for d in (2, 1, 3):
        stage1.append(remote(piece_o, own_o, g1s.at[7 + d], g1r.at[7 + d], y_mate(d)))
    flight.start_local(keep_p)
    flight.start_local(keep_o)
    for copy in stage1[2:]:
        flight.start(copy)

    stage4 = []

    def to_sibling(ref):
        i = len(stage4)
        copy = remote(ref, ref, g4s.at[i], g4r.at[i], sib)
        flight.start(copy)
        stage4.append(copy)

    def part_a(kind, head):
        return gp.at[c, :, 0, :, kind_at(kind, head)]

    def part_b(kind, head):
        return gp.at[c, :, 1, :, kind_at(kind, head)]

    def out_row(copies):
        for copy in copies:
            flight.start(copy)
        return copies

    flight.receive(keep_o)
    for copy in stage1[9:]:
        flight.receive(copy)
    ref = go.at[x, z, :, half]
    second_c = out_row([remote(ref, ref, g2s.at[6 + d], g2r.at[6 + d], x_mate(d)) for d in range(1, 4)])

    quarters = {1: pl.ds(0, 4), 3: pl.ds(4, 4)}
    direct, relays = {}, {}

    def third(dj):
        ref = part_a(y_from(dj), x)
        to_sibling(ref)
        direct["a", dj] = {d: remote(ref, ref, g3s.at[dj * 4 + d], g3r.at[dj * 4 + d], x_mate(d)) for d in (1, 3)}
        out_row(direct["a", dj].values())
        ref = part_b(y, x_from(dj))
        to_sibling(ref)
        direct["b", dj] = {d: remote(ref, ref, g3s.at[16 + dj * 4 + d], g3r.at[16 + dj * 4 + d], y_mate(d)) for d in (1, 3)}
        out_row(direct["b", dj].values())

    def pass_on(dj):
        for name in ("a", "b"):
            relays[name, dj] = []
            for d in (1, 3):
                flight.receive(direct[name, dj][d])
                if name == "a":
                    kind, head, row, at, mate = y_from(dj), x_from(d), 0, dj * 4 + d - 1, x_mate(d)
                else:
                    kind, head, row, at, mate = y_from(d), x_from(dj), 1, 16 + dj * 4 + d - 1, y_mate(d)
                ref = gp.at[c, quarters[d], row, :, kind_at(kind, head)]
                relays[name, dj].append(remote(ref, ref, g3s.at[at], g3r.at[at], mate))
                flight.start(relays[name, dj][-1])
            for d in (1, 3):
                to_sibling(part_a(y_from(dj), x_from(d)) if name == "a" else part_b(y_from(d), x_from(dj)))

    def finish(dj):
        for name in ("a", "b"):
            for copy in relays[name, dj]:
                flight.receive(copy)
            to_sibling(part_a(y_from(dj), x_from(2)) if name == "a" else part_b(y_from(2), x_from(dj)))

    flight.receive(keep_p)
    for copy in stage1[2:9]:
        flight.receive(copy)
    ref = part_a(y, x)
    second_a = {d: remote(ref, ref, g2s.at[d], g2r.at[d], y_mate(d)) for d in (2, 1, 3)}
    out_row(second_a.values())
    ref = part_b(y, x)
    second_b = {d: remote(ref, ref, g2s.at[3 + d], g2r.at[3 + d], x_mate(d)) for d in (2, 1, 3)}
    out_row(second_b.values())
    third(0)
    for copy in second_c:
        flight.receive(copy)
    ref = go.at[:, z, :, half]
    last_c = {d: remote(ref, ref, g3s.at[32 + d], g3r.at[32 + d], z_mate(d)) for d in (2, 6, 1, 7)}
    out_row(last_c.values())
    to_sibling(ref)
    for d in (1, 3):
        flight.receive(second_a[d])
        flight.receive(second_b[d])
        third(d)
    pass_on(0)
    flight.receive(second_a[2])
    flight.receive(second_b[2])
    third(2)
    relay_z = []
    for d, near, at in ((2, 1, 4), (6, 7, 0)):
        flight.receive(last_c[d])
        ref = go.at[:, z_from(d), :, half]
        part = go.at[pl.ds(0 if d == 2 else 2, 2), z_from(d), :, half]
        relay_z.append(remote(ref, ref, g3s.at[32 + d + near - (8 if d == 6 else 0)], g3r.at[32 + d + near - (8 if d == 6 else 0)], z_mate(near)))
        relay_z.append(remote(part, part, g3s.at[32 + at], g3r.at[32 + at], z_mate(d)))
        out_row(relay_z[-2:])
        to_sibling(ref)
    pass_on(1)
    pass_on(3)

    for copy in arrivals:
        flight.receive(copy)
    columns = dpr[...].reshape(2048, ROWS)
    for i in range(4):
        part = dot(wp[i * 256 : (i + 1) * 256, :], columns)
        dn[:, i * 256 : (i + 1) * 256] = part.T

    pass_on(2)
    @pl.loop(0, ROWS // 16, unroll=2)
    def _(i):
        rows = pl.ds(pl.multiple_of(i * 16, 16), 16)
        values = hist[rows, :].astype(F32)
        centred = values - jnp.mean(values, axis=-1, keepdims=True)
        variance = jnp.mean(centred * centred, axis=-1, keepdims=True)
        scale = lax.rsqrt(variance + EPSILON)
        normed = centred * scale
        grad = dn[rows, :]
        one = jnp.mean(grad, axis=-1, keepdims=True)
        two = jnp.mean(grad * normed, axis=-1, keepdims=True)
        d_hist[rows, :] = (cot[rows, :].astype(F32) + scale * (grad - one - normed * two)).astype(BF16)

    for d in (1, 7):
        flight.receive(last_c[d])
        to_sibling(go.at[:, z_from(d), :, half])
    finish(0)
    for copy in relay_z:
        flight.receive(copy)
    for d in (3, 5, 4):
        to_sibling(go.at[:, z_from(d), :, half])
    for dj in (1, 3, 2):
        finish(dj)
    for copy in stage4:
        flight.receive(copy)
    flight.land()


def hand_over(rows_in, gp_in, go_in, rows, gp, go, sems):
    copies = [pltpu.make_async_copy(gp_in.at[s], gp.at[s], sems.at[s]) for s in range(2)]
    copies += [pltpu.make_async_copy(go_in, go, sems.at[2]), pltpu.make_async_copy(rows_in, rows, sems.at[3])]
    for copy in copies:
        copy.start()
    for copy in copies:
        copy.wait()


def on_device(history, cotangent, lengths, w_proj, w_out):
    vmem, dma = pltpu.VMEM, pltpu.SemaphoreType.DMA
    whole = pl.BlockSpec(memory_space=vmem)
    anywhere = pl.BlockSpec(memory_space=pl.ANY)
    scratch = [
        vmem((ROWS, D), BF16),
        vmem((ROWS, D), BF16),
        vmem((EVENTS, D), BF16),
        vmem((EVENTS, D), BF16),
        vmem((EVENTS, D), BF16),
        vmem((D, 2048), BF16),
        vmem((512, D), BF16),
        vmem((512, D), BF16),
        vmem((512, ROWS), BF16),
        vmem((8, 128), jnp.int32),
        vmem((8, 128), jnp.int32),
        vmem((512, EVENTS), BF16),
        vmem((512, EVENTS), F32),
        vmem((EVENTS, HD), BF16),
        vmem((EVENTS, HD), BF16),
        vmem((EVENTS, EVENTS), BF16),
        vmem((EVENTS, EVENTS), F32),
        vmem((HD, EVENTS), F32),
        vmem((HD, EVENTS), BF16),
        vmem((8, EVENTS), F32),
        vmem((4, 8, EVENTS), F32),
        vmem((HD, EVENTS), BF16),
        vmem((HD, EVENTS), BF16),
        vmem((EVENTS, EVENTS), BF16),
        vmem((4, HD, EVENTS), BF16),
        vmem((4, 4, HD, ROWS), BF16),
        vmem((4, 8, 64, HD), BF16),
        vmem((4, 8, 16, HD), BF16),
        vmem((4, 8, 64, HD), BF16),
        vmem((4, 8, 16, HD), BF16),
        vmem((8, 80, HD), BF16),
        vmem((8, 80, HD), BF16),
        vmem((2, 32, HD), BF16),
        vmem((16, HD), BF16),
        vmem((ROWS, D), F32),
        pltpu.SemaphoreType.REGULAR((3,)), dma((4,)), dma((8,)), dma((2,)), dma((2,)), dma, dma, dma((2,)), dma((4,)),
        dma((4,)), dma((4,)), dma((4,)), dma((4,)), dma((4,)), dma((4,)), dma((4,)), dma((4,)), dma((4,)), dma((4,)),
        dma((8,)), dma((8,)), dma, dma((8,)), dma((8,)), dma((8,)), dma((8,)),
        dma((2,)), dma((11,)), dma((11,)), dma((10,)), dma((10,)), dma((40,)), dma((40,)), dma((40,)), dma((40,)),
    ]
    shapes = (
        jax.ShapeDtypeStruct((ROWS, D), BF16),
        jax.ShapeDtypeStruct((2, 8, 2, 32, 2048), BF16),
        jax.ShapeDtypeStruct((4, 8, 16, 1024), BF16),
    )
    results = pl.pallas_call(
        kernel,
        out_shape=shapes,
        in_specs=[anywhere, anywhere, whole, anywhere, anywhere],
        out_specs=(whole, anywhere, anywhere),
        scratch_shapes=scratch,
        compiler_params=pltpu.CompilerParams(
            collective_id=0, has_side_effects=True, vmem_limit_bytes=47 * 2**20
        ),
        name="layer",
    )(history[0], cotangent[0], lengths, w_proj, w_out)
    d_rows, grad_p, grad_o = pl.pallas_call(
        hand_over,
        out_shape=shapes,
        in_specs=[anywhere] * 3,
        out_specs=(anywhere,) * 3,
        scratch_shapes=[dma((4,))],
        compiler_params=pltpu.CompilerParams(vmem_limit_bytes=4 * 2**20),
        name="hand_over",
    )(*results)
    return d_rows[None], grad_p.reshape(1024, 2048), grad_o.reshape(512, 1024)


def solution(mesh):
    in_specs = (P("dp", "ctx", None), P("dp", "ctx", None), P("dp", None), P(), P())
    out_specs = (P("dp", "ctx", None), P(), P())
    return jax.shard_map(
        on_device, mesh=mesh, in_specs=in_specs, out_specs=out_specs, check_vma=False
    )
```
